32 devices in a mesh: row: 4 (over y, x), col: 8 (over z, core).
Axes of the slice: x: 2, y: 2, z: 4, core: 2. Of those that a mesh axis runs over, the one named last changes fastest.
Arguments:
- embeddings: bfloat16 [8192, 1152], P(('col', 'row')), may hold values from -6 to 6
- seed_labels: bfloat16 [8192, 256], P(('col', 'row')), may hold values from 0 to 1
- pattern: int32 [64, 16], replicated, may hold values from 0 to 63, as said below
Outputs:
- propagated: float32 [8192, 256], P(('col', 'row'))
The draws below stay inside these ranges and needn't reach their ends.
Inputs may be any that keep to these rules, and one draw needn't show every extreme that they name: `pattern`: each row names 16 different blocks, never its own block.
All inputs are finite; a program needn't handle non-finite values.
Results may differ from the reference program's by a relative error of at most 0.0012.
Values may be sent and summed in bfloat16 or wider, within the bound.
No kernel may reach another device: no remote copies, remote signals or barrier semaphores. Data moves between devices by JAX's collectives and lax.ppermute only.
A program may use at most 64 MiB of HBM per device.

```python
import jax
import jax.numpy as jnp
from jax import lax

D = 1152
C = 256
BLOCK = 128
ITERS = 2
BLK_COL = 8
NB = 64
CLIPS = 8192
K = 16


def cluster_members(key):
    group_total = max(CLIPS // 128, 8)
    members = jax.random.randint(jax.random.fold_in(key, 5), (CLIPS,), 0, group_total)
    return (members, group_total)


def draw_embeddings(key, part):
    members, group_total = cluster_members(key)
    key = jax.random.fold_in(key, 21)
    key_centre, key_noise = jax.random.split(key, 2)
    centres = jax.random.normal(key_centre, (group_total, D), jnp.float32)
    noise = jax.random.normal(key_noise, (CLIPS, D), jnp.float32)
    values = 0.5 * centres[members] + noise
    return jnp.clip(values, -6.0, 6.0).astype(jnp.bfloat16)


def draw_seed_labels(key, part):
    members, group_total = cluster_members(key)
    key = jax.random.fold_in(key, 22)
    key_profile, key_noise = jax.random.split(key)
    profile = jax.random.uniform(key_profile, (group_total, C), jnp.float32)
    noise = jax.random.uniform(key_noise, (CLIPS, C), jnp.float32)
    values = 0.6 * profile[members] + 0.4 * noise
    return values.astype(jnp.bfloat16)


def draw_pattern(key, part):
    key = jax.random.fold_in(key, 11)
    key_warm, key_rank = jax.random.split(key)
    group_count = NB // BLK_COL
    warmth = jax.random.randint(key_warm, (group_count,), 0, 4)
    jitter = jax.random.randint(key_rank, (NB, NB), 0, 2 ** 20)
    source = jnp.arange(NB, dtype=jnp.int32)[None, :]
    target = jnp.arange(NB, dtype=jnp.int32)[:, None]
    ranking = (warmth[source // BLK_COL] * 2 ** 18 + jitter) * NB + source
    pinned = (target == 0) & (source == NB - 1) | (target == NB - 1) & (source == 0)
    ranking = jnp.where(pinned, 2 ** 30 + 2 ** 29, ranking)
    ranking = jnp.where(source == target, -1, ranking)
    return lax.top_k(ranking, K)[1].astype(jnp.int32)


def setup_inputs(seed: int = 0) -> dict:
    splits = jax.random.split(jax.random.key(seed), 4)
    embeddings = draw_embeddings(jax.random.fold_in(splits[3], 71), 0)
    seed_labels = draw_seed_labels(jax.random.fold_in(splits[3], 71), 0)
    pattern = draw_pattern(jax.random.fold_in(splits[3], 71), 0)
    return dict(embeddings=embeddings, seed_labels=seed_labels, pattern=pattern)


sharpness = 30.0
mixing = 0.8
epsilon = 1e-06

def normalize_rows(embeddings):
    values = embeddings.astype(jnp.float32)
    mean_square = lax.optimization_barrier(jnp.mean(values * values, axis=1, keepdims=True))
    scaled = values * lax.rsqrt(mean_square + epsilon) * values.shape[1] ** (-0.5)
    return scaled.astype(jnp.bfloat16)

def reference(embeddings, seed_labels, pattern):
    unit_rows = normalize_rows(embeddings)
    blocks = unit_rows.reshape(NB, BLOCK, D)
    order = jnp.arange(NB, dtype=jnp.int32)

    def block_kernel(target_block):
        gathered = blocks[pattern[target_block]].reshape(K * BLOCK, D)
        scores = jnp.dot(blocks[target_block], gathered.T, preferred_element_type=jnp.float32)
        return jnp.exp(sharpness * scores).astype(jnp.bfloat16)
    kernel = lax.map(block_kernel, order)
    totals = lax.optimization_barrier(jnp.sum(kernel.astype(jnp.float32), axis=2))
    own_seed = seed_labels.astype(jnp.float32).reshape(NB, BLOCK, C)
    panel_rows = seed_labels
    labels = own_seed
    for sweep_index in range(ITERS):
        panel_blocks = panel_rows.reshape(NB, BLOCK, C)

        def propagate(target_block):
            gathered = panel_blocks[pattern[target_block]].reshape(K * BLOCK, C)
            return jnp.dot(kernel[target_block], gathered, preferred_element_type=jnp.float32)
        numerators = lax.map(propagate, order)
        labels = mixing * numerators / totals[:, :, None] + (1.0 - mixing) * own_seed
        panel_rows = labels.reshape(CLIPS, C).astype(jnp.bfloat16)
    return labels.reshape(CLIPS, C)
```

```python
import functools
import math

import jax
import jax.numpy as jnp
from jax import lax
from jax.experimental import pallas as pl
from jax.experimental.pallas import tpu as pltpu
from jax.sharding import PartitionSpec as P

BLOCK = 128
ITERS = 2
AXES = ("row", "col")

sharpness = 30.0
mixing = 0.8
epsilon = 1e-06


def split_two(n):
    low = max(d for d in range(1, math.isqrt(n) + 1) if n % d == 0)
    return n // low, low


class Layout:
    def __init__(self, rows, cols):
        core = 2 if cols % 2 == 0 else 1
        ny, nx = split_two(rows)
        nzh, nzl = split_two(cols // core)
        self.sizes = dict(y=ny, x=nx, zh=nzh, zl=nzl, core=core)
        self.rows, self.cols = rows, cols

    def coords(self, row, col):
        s = self.sizes
        return dict(
            y=row // s["x"],
            x=row % s["x"],
            zh=col // (s["zl"] * s["core"]),
            zl=col // s["core"] % s["zl"],
            core=col % s["core"],
        )

    def moved(self, at, offset):
        return {k: (at[k] + offset.get(k, 0)) % self.sizes[k] for k in at}

    def row_col(self, at):
        s = self.sizes
        return at["y"] * s["x"] + at["x"], (at["zh"] * s["zl"] + at["zl"]) * s["core"] + at["core"]

    def fetch(self, value, **offset):
        if all(v % self.sizes[k] == 0 for k, v in offset.items()):
            return value
        pairs = []
        for row in range(self.rows):
            for col in range(self.cols):
                r, c = self.row_col(self.moved(self.coords(row, col), offset))
                pairs.append((r * self.cols + c, row * self.cols + col))
        return lax.ppermute(value, AXES, pairs)

    def device(self, offset):
        at = self.coords(lax.axis_index("row"), lax.axis_index("col"))
        row, col = self.row_col(self.moved(at, offset))
        return col * self.rows + row


def unit_kernel(emb_ref, out_ref):
    values = emb_ref[...].astype(jnp.float32)
    mean_square = jnp.mean(values * values, axis=1, keepdims=True)
    scaled = values * lax.rsqrt(mean_square + epsilon) * values.shape[1] ** (-0.5)
    out_ref[...] = scaled.astype(jnp.bfloat16)


def unit_rows(embeddings):
    return pl.pallas_call(
        unit_kernel,
        out_shape=jax.ShapeDtypeStruct(embeddings.shape, jnp.bfloat16),
    )(embeddings)


def store_numerators(kern, pcat, own_ref, other_refs, m, tile):
    rows = kern.shape[0]
    for t in range(rows // tile):
        part = jnp.dot(
            kern[pl.ds(t * tile, tile), :], pcat[...], preferred_element_type=jnp.float32
        )
        for q in range(tile // m):
            piece = t * (tile // m) + q
            value = part[q * m : (q + 1) * m]
            if piece == 0:
                own_ref[...] = value
            else:
                other_refs[piece - 1][...] = value.astype(jnp.bfloat16)


def gram_kernel(nt, ns, m, tile, flags, *refs):
    t_in, s_in, p_in = refs[:nt], refs[nt : nt + ns], refs[nt + ns : nt + 2 * ns]
    rest = refs[nt + 2 * ns :]
    kern_out, tot_out, own_ref = rest[:3]
    other_refs = rest[3 : 2 + nt]
    tcat, scat, pcat, kern, acc, sem_t, sem_s, sem_p, sem_k = rest[2 + nt :]
    copies_t = [
        pltpu.make_async_copy(t_in[i], tcat.at[pl.ds(i * m, m)], sem_t.at[i]) for i in range(nt)
    ]
    copies_s = [
        pltpu.make_async_copy(s_in[j], scat.at[pl.ds(j * m, m)], sem_s.at[j]) for j in range(ns)
    ]
    copies_p = [
        pltpu.make_async_copy(p_in[j], pcat.at[pl.ds(j * m, m)], sem_p.at[j]) for j in range(ns)
    ]
    for copy in copies_t + copies_s + copies_p:
        copy.start()
    rows = nt * m
    acc[...] = jnp.zeros_like(acc)
    for copy in copies_t:
        copy.wait()
    sub = min(m, BLOCK)
    for j in range(ns * m // tile):
        for i in range(tile // m):
            copies_s[j * (tile // m) + i].wait()

        def step(t, carry):
            at = pl.multiple_of(t * tile, tile)
            scores = lax.dot_general(
                tcat[pl.ds(at, tile), :],
                scat[pl.ds(j * tile, tile), :],
                (((1,), (1,)), ((), ())),
                preferred_element_type=jnp.float32,
            )
            value = jnp.exp(sharpness * scores).astype(jnp.bfloat16).astype(jnp.float32)
            for a in range(tile // sub):
                flag = flags[pl.ds(t * (tile // sub) + a, 1), pl.ds(j * tile, tile)]
                part = jnp.where(flag > 0, value[a * sub : (a + 1) * sub], 0.0)
                where = pl.ds(at + a * sub, sub)
                kern[where, pl.ds(j * tile, tile)] = part.astype(jnp.bfloat16)
                for b in range(tile // BLOCK):
                    acc[where, :] += part[:, b * BLOCK : (b + 1) * BLOCK]
            return carry

        lax.fori_loop(0, rows // tile, step, 0, unroll=rows // tile <= 4)
    copy_k = pltpu.make_async_copy(kern, kern_out, sem_k)
    copy_k.start()
    for k in range(rows // BLOCK):
        block = acc[pl.ds(k * BLOCK, BLOCK), :]
        tot_out[pl.ds(k, 1), :] = jnp.sum(block.T, axis=0, keepdims=True)
    for copy in copies_p:
        copy.wait()
    store_numerators(kern, pcat, own_ref, other_refs, m, tile)
    copy_k.wait()


def gram_call(flags, t_pieces, s_pieces, p_pieces):
    nt, ns = len(t_pieces), len(s_pieces)
    m, d = t_pieces[0].shape
    c = p_pieces[0].shape[1]
    rows, cols = nt * m, ns * m
    tile = max(m, 2 * BLOCK)
    any_spec = pl.BlockSpec(memory_space=pl.ANY)
    vmem = pl.BlockSpec(memory_space=pltpu.VMEM)
    return pl.pallas_call(
        functools.partial(gram_kernel, nt, ns, m, tile),
        out_shape=[
            jax.ShapeDtypeStruct((rows, cols), jnp.bfloat16),
            jax.ShapeDtypeStruct((rows // BLOCK, BLOCK), jnp.float32),
            jax.ShapeDtypeStruct((m, c), jnp.float32),
        ]
        + [jax.ShapeDtypeStruct((m, c), jnp.bfloat16)] * (nt - 1),
        in_specs=[vmem] + [any_spec] * (nt + 2 * ns),
        out_specs=[any_spec, vmem, vmem] + [vmem] * (nt - 1),
        scratch_shapes=[
            pltpu.VMEM((rows, d), jnp.bfloat16),
            pltpu.VMEM((cols, d), jnp.bfloat16),
            pltpu.VMEM((cols, c), jnp.bfloat16),
            pltpu.VMEM((rows, cols), jnp.bfloat16),
            pltpu.VMEM((rows, BLOCK), jnp.float32),
            pltpu.SemaphoreType.DMA((nt,)),
            pltpu.SemaphoreType.DMA((ns,)),
            pltpu.SemaphoreType.DMA((ns,)),
            pltpu.SemaphoreType.DMA,
        ],
        compiler_params=pltpu.CompilerParams(vmem_limit_bytes=56 * 2**20),
        cost_estimate=pl.CostEstimate(
            flops=2 * rows * cols * (d + c),
            bytes_accessed=2 * (rows + cols) * (d + c),
            transcendentals=rows * cols,
        ),
    )(flags, *t_pieces, *s_pieces, *p_pieces)


def spread_kernel(nt, ns, m, tile, kern_in, *refs):
    p_in, own_ref, other_refs = refs[:ns], refs[ns], refs[ns + 1 : ns + nt]
    pcat, kern, sem_p, sem_k = refs[ns + nt :]
    rows = nt * m
    copies_p = [
        pltpu.make_async_copy(p_in[j], pcat.at[pl.ds(j * m, m)], sem_p.at[j]) for j in range(ns)
    ]
    copy_k = pltpu.make_async_copy(kern_in, kern, sem_k)
    for copy in copies_p + [copy_k]:
        copy.start()
    for copy in copies_p + [copy_k]:
        copy.wait()
    store_numerators(kern, pcat, own_ref, other_refs, m, tile)


def spread_call(kern, p_pieces):
    ns = len(p_pieces)
    m, c = p_pieces[0].shape
    rows, cols = kern.shape
    nt = rows // m
    any_spec = pl.BlockSpec(memory_space=pl.ANY)
    vmem = pl.BlockSpec(memory_space=pltpu.VMEM)
    return pl.pallas_call(
        functools.partial(spread_kernel, nt, ns, m, max(m, 2 * BLOCK)),
        out_shape=[jax.ShapeDtypeStruct((m, c), jnp.float32)]
        + [jax.ShapeDtypeStruct((m, c), jnp.bfloat16)] * (nt - 1),
        in_specs=[any_spec] * (1 + ns),
        out_specs=[vmem] * nt,
        scratch_shapes=[
            pltpu.VMEM((cols, c), jnp.bfloat16),
            pltpu.VMEM((rows, cols), jnp.bfloat16),
            pltpu.SemaphoreType.DMA((ns,)),
            pltpu.SemaphoreType.DMA,
        ],
        compiler_params=pltpu.CompilerParams(vmem_limit_bytes=40 * 2**20),
        cost_estimate=pl.CostEstimate(
            flops=2 * rows * cols * c,
            bytes_accessed=2 * (rows * cols + cols * c),
            transcendentals=0,
        ),
    )(kern, *p_pieces)


def on_device(embeddings, seed_labels, pattern):
    layout = Layout(lax.axis_size("row"), lax.axis_size("col"))
    size = layout.sizes
    m = embeddings.shape[0]
    t_offsets = [dict(x=a, zl=b) for b in range(size["zl"]) for a in range(size["x"])]
    half_offsets = [dict(y=a, zh=b) for b in range(size["zh"]) for a in range(size["y"])]
    s_offsets = [dict(o, core=c) for o in half_offsets for c in range(size["core"])]

    sub = min(m, BLOCK)

    def blocks_of(offsets):
        starts = jnp.stack([layout.device(o) * m for o in offsets])
        rows = starts[:, None] + sub * jnp.arange(m // sub, dtype=starts.dtype)
        return rows.reshape(-1) // BLOCK

    t_blocks, s_blocks = blocks_of(t_offsets), blocks_of(s_offsets)
    flags = jnp.any(pattern[t_blocks][:, None, :] == s_blocks[None, :, None], axis=2)
    flags = jnp.repeat(flags.astype(jnp.int32), sub, axis=1)

    def gather(value, far, near):
        by_far = [layout.fetch(value, **{far: b}) for b in range(size[far])]
        return [layout.fetch(v, **{near: a}) for v in by_far for a in range(size[near])]

    def sources(value):
        return [
            layout.fetch(v, core=c) for v in gather(value, "zh", "y") for c in range(size["core"])
        ]

    units = unit_rows(embeddings)
    t_pieces = gather(units, "zl", "x")
    s_pieces = sources(units)
    own_seed = seed_labels.astype(jnp.float32)

    def collect(own, others):
        for value, o in zip(others, t_offsets[1:]):
            own = own + layout.fetch(value, **{k: -v for k, v in o.items()}).astype(jnp.float32)
        return own

    kern, tots, own, *others = gram_call(flags, t_pieces, s_pieces, sources(seed_labels))
    tots = tots.reshape(len(t_offsets), m)
    totals = collect(tots[0], [tots[i] for i in range(1, len(t_offsets))])[:, None]
    for sweep_index in range(ITERS):
        if sweep_index > 0:
            own, *others = spread_call(kern, sources(labels.astype(jnp.bfloat16)))
        labels = mixing * collect(own, others) / totals + (1.0 - mixing) * own_seed
    return labels


def solution(mesh):
    return jax.shard_map(
        on_device,
        mesh=mesh,
        in_specs=(P(("col", "row"), None), P(("col", "row"), None), P()),
        out_specs=P(("col", "row"), None),
        check_vma=False,
    )
```

```python
import functools
import math

import jax
import jax.numpy as jnp
from jax import lax
from jax.experimental import pallas as pl
from jax.experimental.pallas import tpu as pltpu
from jax.sharding import PartitionSpec as P

BLOCK = 128
ITERS = 2
AXES = ("row", "col")

sharpness = 30.0
mixing = 0.8
epsilon = 1e-06


def split_two(n):
    low = max(d for d in range(1, math.isqrt(n) + 1) if n % d == 0)
    return n // low, low


class Layout:
    def __init__(self, rows, cols):
        core = 2 if cols % 2 == 0 else 1
        ny, nx = split_two(rows)
        nzh, nzl = split_two(cols // core)
        self.sizes = dict(y=ny, x=nx, zh=nzh, zl=nzl, core=core)
        self.rows, self.cols = rows, cols

    def coords(self, row, col):
        s = self.sizes
        return dict(
            y=row // s["x"],
            x=row % s["x"],
            zh=col // (s["zl"] * s["core"]),
            zl=col // s["core"] % s["zl"],
            core=col % s["core"],
        )

    def moved(self, at, offset):
        return {k: (at[k] + offset.get(k, 0)) % self.sizes[k] for k in at}

    def row_col(self, at):
        s = self.sizes
        return at["y"] * s["x"] + at["x"], (at["zh"] * s["zl"] + at["zl"]) * s["core"] + at["core"]

    def fetch(self, value, **offset):
        if all(v % self.sizes[k] == 0 for k, v in offset.items()):
            return value
        pairs = []
        for row in range(self.rows):
            for col in range(self.cols):
                r, c = self.row_col(self.moved(self.coords(row, col), offset))
                pairs.append((r * self.cols + c, row * self.cols + col))
        return lax.ppermute(value, AXES, pairs)

    def device(self, offset):
        at = self.coords(lax.axis_index("row"), lax.axis_index("col"))
        row, col = self.row_col(self.moved(at, offset))
        return col * self.rows + row


def unit_kernel(emb_ref, out_ref):
    values = emb_ref[...].astype(jnp.float32)
    mean_square = jnp.mean(values * values, axis=1, keepdims=True)
    scaled = values * lax.rsqrt(mean_square + epsilon) * values.shape[1] ** (-0.5)
    out_ref[...] = scaled.astype(jnp.bfloat16)


VMEM = pl.BlockSpec(memory_space=pltpu.VMEM)


def unit_rows(embeddings):
    return pl.pallas_call(
        unit_kernel,
        out_shape=jax.ShapeDtypeStruct(embeddings.shape, jnp.bfloat16),
        in_specs=[VMEM],
        out_specs=VMEM,
    )(embeddings)


def gram_kernel(nt, ns, sub, flags, *refs):
    t_in, s_in, (kern, acc) = refs[:nt], refs[nt : nt + ns], refs[nt + ns :]
    col = 0
    for j in range(ns):
        width = s_in[j].shape[0]
        row = 0
        for i in range(nt):
            height = t_in[i].shape[0]
            scores = lax.dot_general(
                t_in[i][...],
                s_in[j][...],
                (((1,), (1,)), ((), ())),
                preferred_element_type=jnp.float32,
            )
            value = jnp.exp(sharpness * scores).astype(jnp.bfloat16).astype(jnp.float32)
            for a in range(height // sub):
                at = row + a * sub
                flag = flags[at // sub : at // sub + 1, col : col + width]
                part = jnp.where(flag > 0, value[a * sub : (a + 1) * sub], 0.0)
                kern[at : at + sub, col : col + width] = part.astype(jnp.bfloat16)
                total = part[:, :BLOCK]
                for b in range(1, width // BLOCK):
                    total = total + part[:, b * BLOCK : (b + 1) * BLOCK]
                if j > 0:
                    total = total + acc[at : at + sub, :]
                acc[at : at + sub, :] = total
            row += height
        col += width


def gram_call(flags, t_pieces, s_pieces, sub):
    rows, cols = (sum(p.shape[0] for p in pieces) for pieces in (t_pieces, s_pieces))
    d = t_pieces[0].shape[1]
    return pl.pallas_call(
        functools.partial(gram_kernel, len(t_pieces), len(s_pieces), sub),
        out_shape=[
            jax.ShapeDtypeStruct((rows, cols), jnp.bfloat16),
            jax.ShapeDtypeStruct((rows, BLOCK), jnp.float32),
        ],
        in_specs=[VMEM] * (1 + len(t_pieces) + len(s_pieces)),
        out_specs=[VMEM] * 2,
        compiler_params=pltpu.CompilerParams(vmem_limit_bytes=32 * 2**20),
        cost_estimate=pl.CostEstimate(
            flops=2 * rows * cols * d,
            bytes_accessed=2 * (rows + cols) * d,
            transcendentals=rows * cols,
        ),
    )(flags, *t_pieces, *s_pieces)


def spread_kernel(nk, na, ns, nt, m, rects, *refs):
    kerns, refs = refs[:nk], refs[nk:]
    accs, refs = refs[:na], refs[na:]
    p_in, refs = refs[:ns], refs[ns:]
    outs, pcat = refs[:-1], refs[-1]
    own_ref, other_refs = outs[0], outs[-(nt - 1) :] if nt > 1 else ()
    c = pcat.shape[1]
    at = 0
    for ref in p_in:
        pcat[at : at + ref.shape[0], :] = ref[...]
        at += ref.shape[0]
    tile = max(m, 2 * BLOCK)
    for r0 in range(0, nt * m, tile):
        part = None
        for kern, (t0, t1, c0, c1) in zip(kerns, rects):
            if t0 <= r0 < t1:
                term = jnp.dot(
                    kern[r0 - t0 : r0 - t0 + tile, :],
                    pcat[c0:c1, :],
                    preferred_element_type=jnp.float32,
                )
                part = term if part is None else part + term
        for piece in range(r0 // m, (r0 + tile) // m):
            value = part[piece * m - r0 : (piece + 1) * m - r0]
            if piece == 0:
                own_ref[...] = value
            else:
                other_refs[piece - 1][:m, :] = value.astype(jnp.bfloat16)
            if not na:
                continue
            step = min(m, BLOCK)
            for lane in range(0, m, step):
                total = None
                for acc, (t0, t1, c0, c1) in zip(accs, rects):
                    if t0 <= piece * m < t1:
                        start = piece * m - t0 + lane
                        term = acc[start : start + step, :]
                        total = term if total is None else total + term
                total = jnp.sum(total.T, axis=0, keepdims=True)
                if piece == 0:
                    outs[1][:, lane : lane + step] = total
                else:
                    high = total.astype(jnp.bfloat16).astype(jnp.float32)
                    mid = (total - high).astype(jnp.bfloat16).astype(jnp.float32)
                    low = total - high - mid
                    index = lax.broadcasted_iota(jnp.int32, (16, step), 0)
                    terms = jnp.where(index == 0, high, jnp.where(index == 1, mid, low))
                    terms = jnp.where(index < 3, terms, 0.0)
                    other_refs[piece - 1][m:, lane : lane + step] = terms.astype(jnp.bfloat16)


def spread_call(kerns, accs, p_pieces, m, nt, rects):
    c = p_pieces[0].shape[1]
    cols = sum(p.shape[0] for p in p_pieces)
    rows = nt * m
    extra = 16 if accs else 0
    outs = [jax.ShapeDtypeStruct((m, c), jnp.float32)]
    if accs:
        outs.append(jax.ShapeDtypeStruct((1, m), jnp.float32))
    outs += [jax.ShapeDtypeStruct((m + extra, c), jnp.bfloat16)] * (nt - 1)
    got = pl.pallas_call(
        functools.partial(spread_kernel, len(kerns), len(accs), len(p_pieces), nt, m, rects),
        out_shape=outs,
        in_specs=[VMEM] * (len(kerns) + len(accs) + len(p_pieces)),
        out_specs=[VMEM] * len(outs),
        scratch_shapes=[pltpu.VMEM((cols, c), jnp.bfloat16)],
        compiler_params=pltpu.CompilerParams(vmem_limit_bytes=32 * 2**20),
        cost_estimate=pl.CostEstimate(
            flops=2 * rows * cols * c,
            bytes_accessed=2 * (rows * cols + cols * c),
            transcendentals=0,
        ),
    )(*kerns, *accs, *p_pieces)
    return got if accs else [got[0], None] + list(got[1:])


def after(value, *earlier):
    return lax.optimization_barrier((value, *earlier))[0]


def on_device(embeddings, seed_labels, pattern):
    layout = Layout(lax.axis_size("row"), lax.axis_size("col"))
    size = layout.sizes
    m = embeddings.shape[0]
    sub = min(m, BLOCK)
    halves = 2 if m % (2 * BLOCK) == 0 else 1
    fetch = layout.fetch
    cores = range(size["core"])
    t_offsets = [dict(x=a, zl=b) for b in range(size["zl"]) for a in range(size["x"])]
    nt = len(t_offsets)
    half = m // halves
    near = [(dict(y=a, zh=0, core=c), 0, m) for a in range(size["y"]) for c in cores]
    far = [
        [
            (dict(y=a, zh=b, core=c), h * half, half)
            for b in range(1, size["zh"])
            for a in range(size["y"])
            for c in cores
        ]
        for h in range(halves)
    ]
    s_groups = [near] + far if size["zh"] > 1 else [near]
    s_all = [p for group in s_groups for p in group]

    t_blocks = jnp.concatenate(
        [layout.device(o) * m // BLOCK + jnp.arange(0, m, sub) // BLOCK for o in t_offsets]
    ) if m >= BLOCK else jnp.stack([layout.device(o) * m // BLOCK for o in t_offsets])
    s_blocks = jnp.concatenate(
        [
            (layout.device(o) * m + start + jnp.arange(0, rows, sub)) // BLOCK
            for o, start, rows in s_all
        ]
    )
    flags = jnp.any(pattern[t_blocks][:, None, :] == s_blocks[None, :, None], axis=2)
    flags = jnp.repeat(flags.astype(jnp.int32), sub, axis=1)

    own_seed = seed_labels.astype(jnp.float32)
    units = unit_rows(embeddings)

    def cored(value):
        return [fetch(value, core=c) for c in cores]

    t_zl = [fetch(units, zl=b) for b in range(size["zl"])]
    t_pieces = [fetch(v, x=a) for v in t_zl for a in range(size["x"])]
    s_near = [p for a in range(size["y"]) for p in cored(fetch(units, y=a))]
    s_far, sent = [], None
    for h in range(halves):
        rows = units[h * half : (h + 1) * half]
        if sent is not None:
            rows = after(rows, *sent)
        sent = [fetch(rows, zh=b) for b in range(1, size["zh"])]
        s_far.append([p for v in sent for a in range(size["y"]) for p in cored(fetch(v, y=a))])
    s_pieces = [s_near] + s_far if size["zh"] > 1 else [s_near]

    def panel_pieces(panel):
        whole = {}
        for b in range(size["zh"]):
            value = fetch(panel, zh=b)
            for a in range(size["y"]):
                for c, piece in zip(cores, cored(fetch(value, y=a))):
                    whole[a, b, c] = piece
        return [
            whole[o["y"], o["zh"], o["core"]][start : start + rows] for o, start, rows in s_all
        ]

    seeds = panel_pieces(after(seed_labels, *sent))

    def merged(pieces):
        return pieces if m >= BLOCK else [jnp.concatenate(pieces)]

    early = [i for i, o in enumerate(t_offsets) if o["x"] == 0 or o["zl"] == 0]
    if m < BLOCK or early != list(range(len(early))):
        early = list(range(nt))
    late = [i for i in range(nt) if i not in early]
    kerns, accs, rects = [], [], []
    col = 0
    for g, group in enumerate(s_pieces):
        width = sum(p.shape[0] for p in group)
        for rows in [early, late] if g == 0 and late else [list(range(nt))]:
            t0, t1 = rows[0] * m, (rows[-1] + 1) * m
            kern, acc = gram_call(
                flags[t0 // sub : t1 // sub, col : col + width],
                merged([t_pieces[i] for i in rows]),
                merged(group),
                sub,
            )
            kerns.append(kern)
            accs.append(acc)
            rects.append((t0, t1, col, col + width))
        col += width

    def home(values):
        return [fetch(v, **{k: -d for k, d in o.items()}) for v, o in zip(values, t_offsets[1:])]

    own, totals, *others = spread_call(kerns, accs, seeds, m, nt, rects)
    for sweep_index in range(ITERS):
        if sweep_index > 0:
            pieces = panel_pieces(labels.astype(jnp.bfloat16))
            own, _, *others = spread_call(kerns, [], pieces, m, nt, rects)
        numerators = own
        got = home(others)
        for value in got:
            numerators = numerators + value[:m].astype(jnp.float32)
        if sweep_index == 0:
            for value in got:
                totals = totals + jnp.sum(value[m : m + 3, :m].astype(jnp.float32), axis=0)
            totals = totals.reshape(m, 1)
        labels = mixing * numerators / totals + (1.0 - mixing) * own_seed
    return labels


def solution(mesh):
    return jax.shard_map(
        on_device,
        mesh=mesh,
        in_specs=(P(("col", "row"), None), P(("col", "row"), None), P()),
        out_specs=P(("col", "row"), None),
        check_vma=False,
    )
```

```python
import functools
import math

import jax
import jax.numpy as jnp
from jax import lax
from jax.experimental import pallas as pl
from jax.experimental.pallas import tpu as pltpu
from jax.sharding import PartitionSpec as P

BLOCK = 128
AXES = ("row", "col")

sharpness = 30.0
mixing = 0.8
epsilon = 1e-06


def split_two(n):
    low = max(d for d in range(1, math.isqrt(n) + 1) if n % d == 0)
    return n // low, low


class Layout:
    def __init__(self, rows, cols):
        core = 2 if cols % 2 == 0 else 1
        ny, nx = split_two(rows)
        nzh, nzl = split_two(cols // core)
        self.sizes = dict(y=ny, x=nx, zh=nzh, zl=nzl, core=core)
        self.rows, self.cols = rows, cols

    def coords(self, row, col):
        s = self.sizes
        return dict(
            y=row // s["x"],
            x=row % s["x"],
            zh=col // (s["zl"] * s["core"]),
            zl=col // s["core"] % s["zl"],
            core=col % s["core"],
        )

    def moved(self, at, offset):
        return {k: (at[k] + offset.get(k, 0)) % self.sizes[k] for k in at}

    def row_col(self, at):
        s = self.sizes
        return at["y"] * s["x"] + at["x"], (at["zh"] * s["zl"] + at["zl"]) * s["core"] + at["core"]

    def fetch(self, value, **offset):
        if all(v % self.sizes[k] == 0 for k, v in offset.items()):
            return value
        pairs = []
        for row in range(self.rows):
            for col in range(self.cols):
                r, c = self.row_col(self.moved(self.coords(row, col), offset))
                pairs.append((r * self.cols + c, row * self.cols + col))
        return lax.ppermute(value, AXES, pairs)

    def device(self, offset):
        at = self.coords(lax.axis_index("row"), lax.axis_index("col"))
        row, col = self.row_col(self.moved(at, offset))
        return col * self.rows + row


VMEM = pl.BlockSpec(memory_space=pltpu.VMEM)


def limits(mib=32):
    return pltpu.CompilerParams(vmem_limit_bytes=mib * 2**20)


def unit_kernel(t_chunks, s_chunks, emb_ref, seed_ref, *outs):
    values = emb_ref[...].astype(jnp.float32)
    d = values.shape[1]
    mean_square = jnp.mean(values * values, axis=1, keepdims=True)
    scaled = values * lax.rsqrt(mean_square + epsilon) * d ** (-0.5)
    unit = scaled.astype(jnp.bfloat16)
    outs[0][...] = unit
    outs[1][:, :d] = unit
    outs[1][:, d:] = seed_ref[...]
    for out, (start, rows) in zip(outs[2:], t_chunks + s_chunks):
        out[...] = unit[start : start + rows]


def unit_rows(embeddings, seeds, t_chunks, s_chunks):
    m, d = embeddings.shape
    shapes = [(m, d), (m, d + seeds.shape[1])] + [(rows, d) for _, rows in t_chunks + s_chunks]
    got = pl.pallas_call(
        functools.partial(unit_kernel, t_chunks, s_chunks),
        out_shape=[jax.ShapeDtypeStruct(s, jnp.bfloat16) for s in shapes],
        in_specs=[VMEM] * 2,
        out_specs=[VMEM] * len(shapes),
        compiler_params=limits(),
    )(embeddings, seeds)
    return got[0], got[1], got[2 : 2 + len(t_chunks)], got[2 + len(t_chunks) :]


def gram_kernel(nt, ns, sub, d, flags, *refs):
    t_in, s_in, (kern, acc), scratch = refs[:nt], refs[nt : nt + ns], refs[nt + ns : nt + ns + 2], refs[nt + ns + 2 :]
    if scratch:
        at = 0
        for ref in s_in:
            scratch[0][at : at + ref.shape[0], :] = ref[:, :d]
            at += ref.shape[0]
        width = 2 * BLOCK if at % (2 * BLOCK) == 0 else BLOCK if at % BLOCK == 0 else at
        tiles = [(scratch[0], k, width) for k in range(0, at, width)]
    else:
        tiles = [(ref, 0, ref.shape[0]) for ref in s_in]
    col = 0
    for s_ref, s_at, width in tiles:
        row = 0
        for i in range(nt):
            height = t_in[i].shape[0]
            scores = lax.dot_general(
                t_in[i][...],
                s_ref[s_at : s_at + width, :d],
                (((1,), (1,)), ((), ())),
                preferred_element_type=jnp.float32,
            )
            value = jnp.exp(sharpness * scores).astype(jnp.bfloat16).astype(jnp.float32)
            for a in range(height // sub):
                at = row + a * sub
                flag = flags[at // sub : at // sub + 1, col : col + width]
                part = jnp.where(flag > 0, value[a * sub : (a + 1) * sub], 0.0)
                kern[at : at + sub, col : col + width] = part.astype(jnp.bfloat16)
                total = part[:, :BLOCK]
                for b in range(1, width // BLOCK):
                    total = total + part[:, b * BLOCK : (b + 1) * BLOCK]
                if col > 0:
                    total = total + acc[at : at + sub, :]
                acc[at : at + sub, :] = total
            row += height
        col += width


def gram_call(flags, t_pieces, s_pieces, sub):
    rows, cols = (sum(p.shape[0] for p in pieces) for pieces in (t_pieces, s_pieces))
    d = t_pieces[0].shape[1]
    direct = all(p.shape[0] == 2 * BLOCK for p in s_pieces)
    return pl.pallas_call(
        functools.partial(gram_kernel, len(t_pieces), len(s_pieces), sub, d),
        out_shape=[
            jax.ShapeDtypeStruct((rows, cols), jnp.bfloat16),
            jax.ShapeDtypeStruct((rows, BLOCK), jnp.float32),
        ],
        in_specs=[VMEM] * (1 + len(t_pieces) + len(s_pieces)),
        out_specs=[VMEM] * 2,
        scratch_shapes=[] if direct else [pltpu.VMEM((cols, d), jnp.bfloat16)],
        compiler_params=limits(),
        cost_estimate=pl.CostEstimate(
            flops=2 * rows * cols * d,
            bytes_accessed=2 * (rows + cols) * d,
            transcendentals=rows * cols,
        ),
    )(flags, *t_pieces, *s_pieces)


def spread_kernel(plan, nk, na, ns, *refs):
    m, t_layout, rects, p_map = plan
    kerns, refs = refs[:nk], refs[nk:]
    accs, refs = refs[:na], refs[na:]
    p_in, refs = refs[:ns], refs[ns:]
    outs, pcat = refs[:-1], refs[-1]
    own_ref, other_refs = outs[0], outs[2:] if na else outs[1:]
    c = pcat.shape[1]
    at = 0
    for index, start, rows in p_map:
        ref = p_in[index]
        pcat[at : at + rows, :] = ref[start : start + rows, ref.shape[1] - c :]
        at += rows
    row = 0
    for piece, start, rows in t_layout:
        part = None
        for kern, (t0, t1, c0, c1) in zip(kerns, rects):
            if t0 <= row < t1:
                term = jnp.dot(
                    kern[row - t0 : row - t0 + rows, :],
                    pcat[c0:c1, :],
                    preferred_element_type=jnp.float32,
                )
                part = term if part is None else part + term
        if piece == 0:
            own_ref[start : start + rows, :] = part
        else:
            other_refs[piece - 1][start : start + rows, :] = part.astype(jnp.bfloat16)
        step = min(rows, BLOCK)
        for lane in range(0, rows if na else 0, step):
            total = None
            for acc, (t0, t1, c0, c1) in zip(accs, rects):
                if t0 <= row < t1:
                    first = row - t0 + lane
                    term = acc[first : first + step, :]
                    total = term if total is None else total + term
            total = jnp.sum(total.T, axis=0, keepdims=True)
            lanes = slice(start + lane, start + lane + step)
            if piece == 0:
                outs[1][:, lanes] = total
            else:
                high = total.astype(jnp.bfloat16).astype(jnp.float32)
                mid = (total - high).astype(jnp.bfloat16).astype(jnp.float32)
                low = total - high - mid
                index = lax.broadcasted_iota(jnp.int32, (16, step), 0)
                terms = jnp.where(index == 0, high, jnp.where(index == 1, mid, low))
                terms = jnp.where(index < 3, terms, 0.0)
                other_refs[piece - 1][m:, lanes] = terms.astype(jnp.bfloat16)
        row += rows


def spread_call(kerns, accs, p_pieces, c, plan):
    m, t_layout, rects, p_map = plan
    nt = 1 + max(piece for piece, _, _ in t_layout)
    cols = sum(rows for _, _, rows in p_map)
    extra = 16 if accs else 0
    outs = [jax.ShapeDtypeStruct((m, c), jnp.float32)]
    if accs:
        outs.append(jax.ShapeDtypeStruct((1, m), jnp.float32))
    outs += [jax.ShapeDtypeStruct((m + extra, c), jnp.bfloat16)] * (nt - 1)
    return pl.pallas_call(
        functools.partial(spread_kernel, plan, len(kerns), len(accs), len(p_pieces)),
        out_shape=outs,
        in_specs=[VMEM] * (len(kerns) + len(accs) + len(p_pieces)),
        out_specs=[VMEM] * len(outs),
        scratch_shapes=[pltpu.VMEM((cols, c), jnp.bfloat16)],
        compiler_params=limits(),
        cost_estimate=pl.CostEstimate(
            flops=2 * nt * m * cols * c,
            bytes_accessed=2 * (nt * m * cols + cols * c),
            transcendentals=0,
        ),
    )(*kerns, *accs, *p_pieces)


def first_update_kernel(seed_ref, own_ref, own_total_ref, *refs):
    got, (panel_ref, total_ref) = refs[:-2], refs[-2:]
    m = seed_ref.shape[0]
    numerators = own_ref[...]
    for ref in got:
        numerators = numerators + ref[:m, :].astype(jnp.float32)
    totals = own_total_ref[...]
    for ref in got:
        terms = ref[m:, :m].astype(jnp.float32)
        totals = totals + jnp.sum(terms, axis=0, keepdims=True)
    step = min(m, BLOCK)
    for k in range(0, m, step):
        total_ref[k : k + step, :] = jnp.broadcast_to(totals[:, k : k + step], (BLOCK, step)).T
    for k in range(0, seed_ref.shape[1], BLOCK):
        labels = mixing * numerators[:, k : k + BLOCK] / total_ref[...] + (
            1.0 - mixing
        ) * seed_ref[:, k : k + BLOCK].astype(jnp.float32)
        panel_ref[:, k : k + BLOCK] = labels.astype(jnp.bfloat16)


def last_update_kernel(seed_ref, own_ref, total_ref, *refs):
    got, out_ref = refs[:-1], refs[-1]
    numerators = own_ref[...]
    for ref in got:
        numerators = numerators + ref[...].astype(jnp.float32)
    for k in range(0, seed_ref.shape[1], BLOCK):
        out_ref[:, k : k + BLOCK] = mixing * numerators[:, k : k + BLOCK] / total_ref[...] + (
            1.0 - mixing
        ) * seed_ref[:, k : k + BLOCK].astype(jnp.float32)


def update(kernel, seeds, own, totals, got, out_shape):
    return pl.pallas_call(
        kernel,
        out_shape=out_shape,
        in_specs=[VMEM] * (3 + len(got)),
        out_specs=jax.tree.map(lambda _: VMEM, out_shape),
        compiler_params=limits(),
    )(seeds, own, totals, *got)


def after(value, *earlier):
    return lax.optimization_barrier((value, *earlier))[0]


def on_device(embeddings, seed_labels, pattern):
    layout = Layout(lax.axis_size("row"), lax.axis_size("col"))
    size = layout.sizes
    m, c = embeddings.shape[0], seed_labels.shape[1]
    sub = min(m, BLOCK)
    fetch = layout.fetch
    cores, ys = range(size["core"]), range(size["y"])
    chunked = m % (2 * BLOCK) == 0
    t_chunks = [(0, m // 2), (m // 2, m // 2)] if chunked else [(0, m)]
    s_chunks = [(0, 3 * m // 4), (3 * m // 4, m // 4)] if chunked else [(0, m)]

    t_index = {(b, a): b * size["x"] + a for b in range(size["zl"]) for a in range(size["x"])}
    t_layout = [(t_index[0, a], 0, m) for a in range(size["x"])]
    ends = [size["x"] * m]
    for start, rows in t_chunks:
        for a in range(size["x"]):
            t_layout += [(t_index[b, a], start, rows) for b in range(1, size["zl"])]
            ends.append(ends[-1] + (size["zl"] - 1) * rows)
    near = [dict(y=a, core=k) for a in ys for k in cores]
    far = [dict(zh=b, y=a, core=k) for b in range(1, size["zh"]) for a in ys for k in cores]
    s_layout = [(i, o, 0, m) for i, o in enumerate(near)]
    columns = [len(near) * m]
    for start, rows in s_chunks:
        s_layout += [(len(near) + i, o, start, rows) for i, o in enumerate(far)]
        columns.append(columns[-1] + len(far) * rows)
    p_map = [(i, start, rows) for i, _, start, rows in s_layout]

    t_offsets = [dict(zl=b, x=a) for b, a in t_index]
    t_blocks = jnp.concatenate(
        [
            (layout.device(t_offsets[i]) * m + start + jnp.arange(0, rows, sub)) // BLOCK
            for i, start, rows in t_layout
        ]
    )
    s_blocks = jnp.concatenate(
        [(layout.device(o) * m + start + jnp.arange(rows)) // BLOCK for _, o, start, rows in s_layout]
    )
    flags = jnp.any(pattern[t_blocks][:, :, None] == s_blocks[None, None, :], axis=1)
    flags = flags.astype(jnp.int32)

    units, packed, t_parts, s_parts = unit_rows(embeddings, seed_labels, t_chunks, s_chunks)

    def cored(value):
        return [fetch(value, core=k) for k in cores]

    by_x = [fetch(units, x=a) for a in range(size["x"])]
    by_y = [fetch(packed, y=a) for a in ys]
    t_pieces, held = list(by_x), ()
    for part in t_parts:
        by_zl = [fetch(after(part, *held), zl=b) for b in range(1, size["zl"])]
        held = by_zl
        t_pieces += [fetch(v, x=a) for a in range(size["x"]) for v in by_zl]
    s_near = cored(after(packed, *by_y[1:])) + [p for v in by_y[1:] for p in cored(v)]
    by_zh, held = [], ()
    for part in s_parts:
        by_zh.append([fetch(after(part, *held), zh=b) for b in range(1, size["zh"])])
        held = by_zh[-1] + by_x[1:] + by_y[1:]
    s_far = []

    def near_panels(panel):
        return [p for a in ys for p in cored(fetch(panel, y=a))]

    def far_panels(panel):
        by_zh = [fetch(panel, zh=b) for b in range(1, size["zh"])]
        return [p for v in by_zh for a in ys for p in cored(fetch(v, y=a))]

    t_ends = [ends[1], ends[2], ends[-1]] if chunked and size["x"] == 2 else [ends[-1]]
    kerns, accs, rects = [], [], []

    def rectangle(t0, t1, g):
        row, pieces = 0, []
        for piece, (_, _, rows) in zip(t_pieces, t_layout):
            if t0 <= row < t1:
                pieces.append(piece)
            row += rows
        c0, c1 = ([0] + columns)[g : g + 2]
        kern, acc = gram_call(
            flags[t0 // sub : t1 // sub, c0:c1], pieces, ([s_near] + s_far)[g], sub
        )
        kerns.append(kern)
        accs.append(acc)
        rects.append((t0, t1, c0, c1))

    def onward(g, *earlier):
        values = [after(v, *earlier) for v in by_zh[g]]
        s_far.append([p for v in values for a in ys for p in cored(fetch(v, y=a))])

    if len(t_ends) == 3 and far:
        onward(0)
        rectangle(0, t_ends[0], 0)
        onward(1, accs[0])
        rectangle(t_ends[0], t_ends[1], 0)
        rectangle(0, t_ends[1], 1)
        rectangle(t_ends[1], t_ends[2], 0)
        rectangle(t_ends[1], t_ends[2], 1)
        rectangle(0, t_ends[2], 2)
    else:
        for g in range(len(s_chunks) if far else 0):
            onward(g)
        for g in range(1 + len(s_far)):
            rectangle(0, ends[-1], g)
    plan = (m, t_layout, rects, p_map)

    def home(values):
        return [fetch(v, **{k: -d for k, d in o.items()}) for v, o in zip(values, t_offsets[1:])]

    seeds = s_near + far_panels(after(seed_labels, *held))
    own, totals, *others = spread_call(kerns, accs, seeds, c, plan)
    panel, totals = update(
        first_update_kernel,
        seed_labels,
        own,
        totals,
        home(others),
        [
            jax.ShapeDtypeStruct((m, c), jnp.bfloat16),
            jax.ShapeDtypeStruct((m, BLOCK), jnp.float32),
        ],
    )
    own, *others = spread_call(kerns, [], near_panels(panel) + far_panels(panel), c, plan)
    return update(
        last_update_kernel,
        seed_labels,
        own,
        totals,
        home(others),
        jax.ShapeDtypeStruct((m, c), jnp.float32),
    )


def solution(mesh):
    return jax.shard_map(
        on_device,
        mesh=mesh,
        in_specs=(P(("col", "row"), None), P(("col", "row"), None), P()),
        out_specs=P(("col", "row"), None),
        check_vma=False,
    )
```

```python
import functools
import math

import jax
import jax.numpy as jnp
from jax import lax
from jax.experimental import pallas as pl
from jax.experimental.pallas import tpu as pltpu
from jax.sharding import PartitionSpec as P

BLOCK = 128
AXES = ("row", "col")

sharpness = 30.0
mixing = 0.8
epsilon = 1e-06


def split_two(n):
    low = max(d for d in range(1, math.isqrt(n) + 1) if n % d == 0)
    return n // low, low


class Layout:
    def __init__(self, rows, cols):
        core = 2 if cols % 2 == 0 else 1
        ny, nx = split_two(rows)
        nzh, nzl = split_two(cols // core)
        self.sizes = dict(y=ny, x=nx, zh=nzh, zl=nzl, core=core)
        self.rows, self.cols = rows, cols

    def coords(self, row, col):
        s = self.sizes
        return dict(
            y=row // s["x"],
            x=row % s["x"],
            zh=col // (s["zl"] * s["core"]),
            zl=col // s["core"] % s["zl"],
            core=col % s["core"],
        )

    def moved(self, at, offset):
        return {k: (at[k] + offset.get(k, 0)) % self.sizes[k] for k in at}

    def row_col(self, at):
        s = self.sizes
        return at["y"] * s["x"] + at["x"], (at["zh"] * s["zl"] + at["zl"]) * s["core"] + at["core"]

    def fetch(self, value, **offset):
        if all(v % self.sizes[k] == 0 for k, v in offset.items()):
            return value
        pairs = []
        for row in range(self.rows):
            for col in range(self.cols):
                r, c = self.row_col(self.moved(self.coords(row, col), offset))
                pairs.append((r * self.cols + c, row * self.cols + col))
        return lax.ppermute(value, AXES, pairs)

    def device(self, offset):
        at = self.coords(lax.axis_index("row"), lax.axis_index("col"))
        row, col = self.row_col(self.moved(at, offset))
        return col * self.rows + row


VMEM = pl.BlockSpec(memory_space=pltpu.VMEM)


def limits(mib=32):
    return pltpu.CompilerParams(vmem_limit_bytes=mib * 2**20)


def unit_of(values):
    values = values.astype(jnp.float32)
    mean_square = jnp.mean(values * values, axis=1, keepdims=True)
    scaled = values * lax.rsqrt(mean_square + epsilon) * values.shape[1] ** (-0.5)
    return scaled.astype(jnp.bfloat16)


def first_unit_kernel(emb_ref, out_ref):
    out_ref[...] = unit_of(emb_ref[: out_ref.shape[0], :])


def unit_kernel(emb_ref, seed_ref, first_ref, unit_ref, packed_ref, *second):
    d, head = emb_ref.shape[1], first_ref.shape[0]
    packed_ref[:, d:] = seed_ref[...]
    unit_ref[:head, :] = first_ref[...]
    packed_ref[:head, :d] = first_ref[...]
    if second:
        rest = unit_of(emb_ref[head:, :])
        unit_ref[head:, :] = rest
        packed_ref[head:, :d] = rest
        second[0][...] = rest


def unit_rows(embeddings, seeds, chunks):
    (m, d), c = embeddings.shape, seeds.shape[1]
    head = chunks[0][1]
    first = pl.pallas_call(
        first_unit_kernel,
        out_shape=jax.ShapeDtypeStruct((head, d), jnp.bfloat16),
        in_specs=[VMEM],
        out_specs=VMEM,
        compiler_params=limits(),
    )(embeddings)
    shapes = [(m, d), (m, d + c)] + [(rows, d) for _, rows in chunks[1:]]
    units, packed, *second = pl.pallas_call(
        unit_kernel,
        out_shape=[jax.ShapeDtypeStruct(s, jnp.bfloat16) for s in shapes],
        in_specs=[VMEM] * 3,
        out_specs=[VMEM] * len(shapes),
        compiler_params=limits(),
    )(embeddings, seeds, first)
    return units, packed, [first] + second


def joined(refs, scratch, d):
    if scratch is None:
        return refs[0]
    at = 0
    for ref in refs:
        scratch[at : at + ref.shape[0], :] = ref[:, :d]
        at += ref.shape[0]
    return scratch


def gram_kernel(nt, ns, sub, d, join_t, join_s, flags, *refs):
    t_in, s_in, refs = refs[:nt], refs[nt : nt + ns], refs[nt + ns :]
    (kern, acc), scratch = refs[:2], list(refs[2:])
    t_ref = joined(t_in, scratch.pop(0) if join_t else None, d)
    if join_s:
        s_ref = joined(s_in, scratch.pop(0), d)
        total = s_ref.shape[0]
        width = next(w for w in (2 * BLOCK, BLOCK, total) if total % w == 0)
        tiles = [(s_ref, k, width) for k in range(0, total, width)]
    else:
        tiles = [(ref, 0, ref.shape[0]) for ref in s_in]
    rows = kern.shape[0]
    tall = next(h for h in (512, 384, 256, 128, rows) if rows % h == 0)
    col = 0
    for s_ref, s_at, width in tiles:
        for row in range(0, rows, tall):
            scores = lax.dot_general(
                t_ref[row : row + tall, :],
                s_ref[s_at : s_at + width, :d],
                (((1,), (1,)), ((), ())),
                preferred_element_type=jnp.float32,
            )
            value = jnp.exp(sharpness * scores).astype(jnp.bfloat16).astype(jnp.float32)
            for a in range(tall // sub):
                at = row + a * sub
                flag = flags[at // sub : at // sub + 1, col : col + width]
                part = jnp.where(flag > 0, value[a * sub : (a + 1) * sub], 0.0)
                kern[at : at + sub, col : col + width] = part.astype(jnp.bfloat16)
                total = part[:, :BLOCK]
                for b in range(1, width // BLOCK):
                    total = total + part[:, b * BLOCK : (b + 1) * BLOCK]
                if col > 0:
                    total = total + acc[at : at + sub, :]
                acc[at : at + sub, :] = total
        col += width


def gram_call(flags, t_pieces, s_pieces, sub):
    rows, cols = (sum(p.shape[0] for p in pieces) for pieces in (t_pieces, s_pieces))
    d = t_pieces[0].shape[1]
    join_t = len(t_pieces) > 1
    join_s = any(p.shape[0] != 2 * BLOCK for p in s_pieces)
    return pl.pallas_call(
        functools.partial(gram_kernel, len(t_pieces), len(s_pieces), sub, d, join_t, join_s),
        out_shape=[
            jax.ShapeDtypeStruct((rows, cols), jnp.bfloat16),
            jax.ShapeDtypeStruct((rows, BLOCK), jnp.float32),
        ],
        in_specs=[VMEM] * (1 + len(t_pieces) + len(s_pieces)),
        out_specs=[VMEM] * 2,
        scratch_shapes=[pltpu.VMEM((rows, d), jnp.bfloat16)] * join_t
        + [pltpu.VMEM((cols, d), jnp.bfloat16)] * join_s,
        compiler_params=limits(),
        cost_estimate=pl.CostEstimate(
            flops=2 * rows * cols * d,
            bytes_accessed=2 * (rows + cols) * d,
            transcendentals=rows * cols,
        ),
    )(flags, *t_pieces, *s_pieces)


def spread_kernel(plan, nk, na, ns, *refs):
    m, t_layout, rects, p_map = plan
    kerns, refs = refs[:nk], refs[nk:]
    accs, refs = refs[:na], refs[na:]
    p_in, refs = refs[:ns], refs[ns:]
    outs, pcat = refs[:-1], refs[-1]
    own_ref, other_refs = outs[0], outs[2:] if na else outs[1:]
    c = pcat.shape[1]
    at = 0
    for index, start, rows in p_map:
        ref = p_in[index]
        pcat[at : at + rows, :] = ref[start : start + rows, ref.shape[1] - c :]
        at += rows
    row = 0
    for piece, start, rows in t_layout:
        part = None
        for kern, (t0, t1, c0, c1) in zip(kerns, rects):
            if t0 <= row < t1:
                term = jnp.dot(
                    kern[row - t0 : row - t0 + rows, :],
                    pcat[c0:c1, :],
                    preferred_element_type=jnp.float32,
                )
                part = term if part is None else part + term
        if piece == 0:
            own_ref[start : start + rows, :] = part
        else:
            other_refs[piece - 1][start : start + rows, :] = part.astype(jnp.bfloat16)
        step = min(rows, BLOCK)
        for lane in range(0, rows if na else 0, step):
            total = None
            for acc, (t0, t1, c0, c1) in zip(accs, rects):
                if t0 <= row < t1:
                    first = row - t0 + lane
                    term = acc[first : first + step, :]
                    total = term if total is None else total + term
            total = jnp.sum(total.T, axis=0, keepdims=True)
            lanes = slice(start + lane, start + lane + step)
            if piece == 0:
                outs[1][:, lanes] = total
            else:
                high = total.astype(jnp.bfloat16).astype(jnp.float32)
                mid = (total - high).astype(jnp.bfloat16).astype(jnp.float32)
                low = total - high - mid
                index = lax.broadcasted_iota(jnp.int32, (16, step), 0)
                terms = jnp.where(index == 0, high, jnp.where(index == 1, mid, low))
                terms = jnp.where(index < 3, terms, 0.0)
                other_refs[piece - 1][m:, lanes] = terms.astype(jnp.bfloat16)
        row += rows


def spread_call(kerns, accs, p_pieces, c, plan):
    m, t_layout, rects, p_map = plan
    nt = 1 + max(piece for piece, _, _ in t_layout)
    cols = sum(rows for _, _, rows in p_map)
    extra = 16 if accs else 0
    outs = [jax.ShapeDtypeStruct((m, c), jnp.float32)]
    if accs:
        outs.append(jax.ShapeDtypeStruct((1, m), jnp.float32))
    outs += [jax.ShapeDtypeStruct((m + extra, c), jnp.bfloat16)] * (nt - 1)
    return pl.pallas_call(
        functools.partial(spread_kernel, plan, len(kerns), len(accs), len(p_pieces)),
        out_shape=outs,
        in_specs=[VMEM] * (len(kerns) + len(accs) + len(p_pieces)),
        out_specs=[VMEM] * len(outs),
        scratch_shapes=[pltpu.VMEM((cols, c), jnp.bfloat16)],
        compiler_params=limits(),
        cost_estimate=pl.CostEstimate(
            flops=2 * nt * m * cols * c,
            bytes_accessed=2 * (nt * m * cols + cols * c),
            transcendentals=0,
        ),
    )(*kerns, *accs, *p_pieces)


def first_update_kernel(seed_ref, own_ref, own_total_ref, *refs):
    got, (panel_ref, total_ref) = refs[:-2], refs[-2:]
    m = seed_ref.shape[0]
    numerators = own_ref[...]
    for ref in got:
        numerators = numerators + ref[:m, :].astype(jnp.float32)
    totals = own_total_ref[...]
    for ref in got:
        terms = ref[m:, :m].astype(jnp.float32)
        totals = totals + jnp.sum(terms, axis=0, keepdims=True)
    step = min(m, BLOCK)
    for k in range(0, m, step):
        total_ref[k : k + step, :] = jnp.broadcast_to(totals[:, k : k + step], (BLOCK, step)).T
    for k in range(0, seed_ref.shape[1], BLOCK):
        labels = mixing * numerators[:, k : k + BLOCK] / total_ref[...] + (
            1.0 - mixing
        ) * seed_ref[:, k : k + BLOCK].astype(jnp.float32)
        panel_ref[:, k : k + BLOCK] = labels.astype(jnp.bfloat16)


def last_update_kernel(seed_ref, own_ref, total_ref, *refs):
    got, out_ref = refs[:-1], refs[-1]
    numerators = own_ref[...]
    for ref in got:
        numerators = numerators + ref[...].astype(jnp.float32)
    for k in range(0, seed_ref.shape[1], BLOCK):
        out_ref[:, k : k + BLOCK] = mixing * numerators[:, k : k + BLOCK] / total_ref[...] + (
            1.0 - mixing
        ) * seed_ref[:, k : k + BLOCK].astype(jnp.float32)


def update(kernel, seeds, own, totals, got, out_shape):
    return pl.pallas_call(
        kernel,
        out_shape=out_shape,
        in_specs=[VMEM] * (3 + len(got)),
        out_specs=jax.tree.map(lambda _: VMEM, out_shape),
        compiler_params=limits(),
    )(seeds, own, totals, *got)


def after(value, *earlier):
    return lax.optimization_barrier((value, *earlier))[0]


def on_device(embeddings, seed_labels, pattern):
    layout = Layout(lax.axis_size("row"), lax.axis_size("col"))
    size = layout.sizes
    m, c = embeddings.shape[0], seed_labels.shape[1]
    sub = min(m, BLOCK)
    other = {k: range(1, size[k]) for k in size}
    chunks = [(0, m // 2), (m // 2, m // 2)] if m % (2 * BLOCK) == 0 else [(0, m)]

    def fetch(values, axis, *earlier):
        return [
            layout.fetch(after(v, *earlier), **{axis: k}) for k in other[axis] for v in values
        ]

    units, packed, parts = unit_rows(embeddings, seed_labels, chunks)

    t_index = {(b, a): b * size["x"] + a for b in range(size["zl"]) for a in range(size["x"])}
    t_layout = [(t_index[0, a], 0, m) for a in range(size["x"])]
    t_groups = [len(t_layout)]
    for start, rows in chunks:
        t_layout += [(t_index[b, 0], start, rows) for b in other["zl"]]
        t_groups.append(len(t_layout))
        t_layout += [(t_index[b, a], start, rows) for a in other["x"] for b in other["zl"]]
        t_groups.append(len(t_layout))
    both = [0] + list(other["core"])
    groups = [[(0, a, k, 0, m) for a in range(size["y"]) for k in both]]
    for start, rows in chunks:
        groups.append([(b, 0, k, start, rows) for k in both for b in other["zh"]])
        groups.append(
            [(b, a, k, start, rows) for k in both for a in other["y"] for b in other["zh"]]
        )
    s_layout = [piece for group in groups for piece in group]
    whole = [(0, a, k) for a in range(size["y"]) for k in both]
    whole += [(b, 0, k) for k in both for b in other["zh"]]
    whole += [(b, a, k) for k in both for a in other["y"] for b in other["zh"]]
    p_map = [(whole.index(piece[:3]), *piece[3:]) for piece in s_layout]

    t_offsets = [dict(zl=b, x=a) for b, a in t_index]
    t_blocks = jnp.concatenate(
        [
            (layout.device(t_offsets[i]) * m + start + jnp.arange(0, rows, sub)) // BLOCK
            for i, start, rows in t_layout
        ]
    )
    s_blocks = jnp.concatenate(
        [
            (layout.device(dict(zh=b, y=a, core=k)) * m + start + jnp.arange(rows)) // BLOCK
            for b, a, k, start, rows in s_layout
        ]
    )
    flags = jnp.any(pattern[t_blocks][:, :, None] == s_blocks[None, None, :], axis=1)
    flags = flags.astype(jnp.int32)

    t_pieces, kerns, accs, rects = [], [], [], []
    s_pieces = [None] * len(groups)

    def rectangle(first, last, g0, g1):
        t0, t1 = (sum(rows for _, _, rows in t_layout[:i]) for i in (first, last))
        c0, c1 = (sum(p[4] for group in groups[:g] for p in group) for g in (g0, g1))
        if t0 == t1 or c0 == c1:
            return []
        kern, acc = gram_call(
            flags[t0 // sub : t1 // sub, c0:c1],
            t_pieces[first:last],
            [p for g in range(g0, g1) for p in s_pieces[g]],
            sub,
        )
        kerns.append(kern)
        accs.append(acc)
        rects.append((t0, t1, c0, c1))
        return [acc]

    zh, zl = fetch(parts[:1], "zh"), fetch(parts[:1], "zl")
    x, y = fetch([units], "x"), fetch([packed], "y")
    own_core = fetch([packed], "core")
    done = zh + zl + x + y + own_core
    t_pieces += [units] + x + zl
    zh_next, zl_next = fetch(parts[1:], "zh", *done), fetch(parts[1:], "zl", *done)
    zh_y, zl_x = fetch(zh, "y", *done), fetch(zl, "x", *done)
    y_core = [fetch([v], "core", *done) for v in y]
    t_pieces += zl_x
    s_pieces[0] = [packed] + own_core + [p for v, w in zip(y, y_core) for p in [v] + w]
    first = rectangle(0, t_groups[1], 0, 1)
    zh_core = fetch(zh, "core", *done, *[p for w in y_core for p in w])
    s_pieces[1] = zh + zh_core
    done = zh_next + zl_next + zh_y + zl_x + zh_core + first
    seeds_zh = fetch([seed_labels], "zh", *done)
    zh_y_core = fetch(zh_y, "core", *done)
    s_pieces[2] = zh_y + zh_y_core
    if parts[1:]:
        zh_next_y, zl_next_x = fetch(zh_next, "y", *done), fetch(zl_next, "x", *done)
        zh_next_core = fetch(zh_next, "core", *done)
        t_pieces += zl_next + zl_next_x
        second = rectangle(t_groups[1], t_groups[2], 0, 1) + rectangle(0, t_groups[2], 1, 3)
        done = zh_next_y + zl_next_x + zh_next_core + zh_y_core + seeds_zh + second
        zh_next_y_core = fetch(zh_next_y, "core", *done)
        s_pieces[3] = zh_next + zh_next_core
        s_pieces[4] = zh_next_y + zh_next_y_core
    else:
        done = zh_y_core + seeds_zh
    seeds_y, seeds_core = fetch(seeds_zh, "y", *done), fetch(seeds_zh, "core", *done)
    seeds_y_core = fetch(seeds_y, "core")
    last = len(t_pieces)
    if parts[1:]:
        rectangle(t_groups[2], last, 0, 1)
        rectangle(t_groups[2], last, 1, 3)
        rectangle(0, last, 3, 4)
        rectangle(0, last, 4, 5)
    else:
        rectangle(t_groups[1], last, 0, 1)
        rectangle(0, last, 1, 2)
        rectangle(0, last, 2, 3)
    plan = (m, t_layout, rects, p_map)

    def home(values):
        return [
            layout.fetch(v, **{k: -d for k, d in o.items()})
            for v, o in zip(values, t_offsets[1:])
        ]

    def panels(panel):
        far, near = fetch([panel], "zh"), fetch([panel], "y")
        far_y = fetch(far, "y")
        near = [p for v in [panel] + near for p in [v] + fetch([v], "core")]
        return near + far + fetch(far, "core") + far_y + fetch(far_y, "core")

    seeds = s_pieces[0] + seeds_zh + seeds_core + seeds_y + seeds_y_core
    own, totals, *others = spread_call(kerns, accs, seeds, c, plan)
    panel, totals = update(
        first_update_kernel,
        seed_labels,
        own,
        totals,
        home(others),
        [
            jax.ShapeDtypeStruct((m, c), jnp.bfloat16),
            jax.ShapeDtypeStruct((m, BLOCK), jnp.float32),
        ],
    )
    own, *others = spread_call(kerns, [], panels(panel), c, plan)
    return update(
        last_update_kernel,
        seed_labels,
        own,
        totals,
        home(others),
        jax.ShapeDtypeStruct((m, c), jnp.float32),
    )


def solution(mesh):
    return jax.shard_map(
        on_device,
        mesh=mesh,
        in_specs=(P(("col", "row"), None), P(("col", "row"), None), P()),
        out_specs=P(("col", "row"), None),
        check_vma=False,
    )
```

```python
import functools
import math

import jax
import jax.numpy as jnp
from jax import lax
from jax.experimental import pallas as pl
from jax.experimental.pallas import tpu as pltpu
from jax.sharding import PartitionSpec as P

BLOCK = 128
AXES = ("row", "col")

sharpness = 30.0
mixing = 0.8
epsilon = 1e-06


def split_two(n):
    low = max(d for d in range(1, math.isqrt(n) + 1) if n % d == 0)
    return n // low, low


class Layout:
    def __init__(self, rows, cols):
        core = 2 if cols % 2 == 0 else 1
        ny, nx = split_two(rows)
        nzh, nzl = split_two(cols // core)
        self.sizes = dict(y=ny, x=nx, zh=nzh, zl=nzl, core=core)
        self.rows, self.cols = rows, cols

    def coords(self, row, col):
        s = self.sizes
        return dict(
            y=row // s["x"],
            x=row % s["x"],
            zh=col // (s["zl"] * s["core"]),
            zl=col // s["core"] % s["zl"],
            core=col % s["core"],
        )

    def moved(self, at, offset):
        return {k: (at[k] + offset.get(k, 0)) % self.sizes[k] for k in at}

    def row_col(self, at):
        s = self.sizes
        return at["y"] * s["x"] + at["x"], (at["zh"] * s["zl"] + at["zl"]) * s["core"] + at["core"]

    def fetch(self, value, **offset):
        if all(v % self.sizes[k] == 0 for k, v in offset.items()):
            return value
        pairs = []
        for row in range(self.rows):
            for col in range(self.cols):
                r, c = self.row_col(self.moved(self.coords(row, col), offset))
                pairs.append((r * self.cols + c, row * self.cols + col))
        return lax.ppermute(value, AXES, pairs)

    def device(self, offset):
        at = self.coords(lax.axis_index("row"), lax.axis_index("col"))
        row, col = self.row_col(self.moved(at, offset))
        return col * self.rows + row


VMEM = pl.BlockSpec(memory_space=pltpu.VMEM)


def limits(*arrays, mib=3):
    total = sum(max(math.prod(a.shape), 8 * BLOCK) * a.dtype.itemsize for a in arrays)
    return pltpu.CompilerParams(vmem_limit_bytes=total * 5 // 4 + mib * 2**20)


def shape(dims, dtype=jnp.bfloat16):
    return jax.ShapeDtypeStruct(dims, dtype)


def unit_of(values):
    values = values.astype(jnp.float32)
    mean_square = jnp.mean(values * values, axis=1, keepdims=True)
    scaled = values * lax.rsqrt(mean_square + epsilon) * values.shape[1] ** (-0.5)
    return scaled.astype(jnp.bfloat16)


def first_unit_kernel(emb_ref, out_ref):
    out_ref[...] = unit_of(emb_ref[: out_ref.shape[0], :])


def unit_kernel(emb_ref, seed_ref, first_ref, unit_ref, packed_ref, *second):
    d, head = emb_ref.shape[1], first_ref.shape[0]
    unit_ref[:head, :] = first_ref[...]
    packed_ref[:head, :d] = first_ref[...]
    packed_ref[:, d:] = seed_ref[...]
    if second:
        unit = unit_of(emb_ref[head:, :])
        unit_ref[head:, :] = unit
        packed_ref[head:, :d] = unit
        second[0][...] = unit


def unit_rows(embeddings, seeds, chunks):
    (m, d), c = embeddings.shape, seeds.shape[1]
    first = pl.pallas_call(
        first_unit_kernel,
        out_shape=shape((chunks[0][1], d)),
        in_specs=[VMEM],
        out_specs=VMEM,
        compiler_params=limits(embeddings, mib=16),
    )(embeddings)
    outs = [shape((m, d)), shape((m, d + c))] + [shape((rows, d)) for _, rows in chunks[1:]]
    units, packed, *second = pl.pallas_call(
        unit_kernel,
        out_shape=outs,
        in_specs=[VMEM] * 3,
        out_specs=[VMEM] * len(outs),
        compiler_params=limits(embeddings, seeds, *outs, *outs, mib=16),
    )(embeddings, seeds, first)
    return units, packed, [[first], second]


def flags_kernel(layout, m, t_parts, s_parts, unit, place_ref, pattern_ref, out_ref, block_ref):
    at = layout.coords(place_ref[0], place_ref[1])

    def block(offset, start):
        row, col = layout.row_col(layout.moved(at, offset))
        return ((col * layout.rows + row) * m + start) // BLOCK

    for k, (offset, start) in enumerate(s_parts):
        block_ref[:, k * unit : (k + 1) * unit] = jnp.full((1, unit), block(offset, start), jnp.int32)
    blocks = block_ref[...]
    for r, (offset, start) in enumerate(t_parts):
        target = block(offset, start)
        hits = blocks == pattern_ref[0, target]
        for k in range(1, pattern_ref.shape[0]):
            hits = hits | (blocks == pattern_ref[k, target])
        out_ref[r : r + 1, :] = jnp.where(hits, 1, 0)


def flags_call(layout, m, t_parts, s_parts, unit, pattern):
    place = jnp.stack([lax.axis_index("row"), lax.axis_index("col")]).astype(jnp.int32)
    out = shape((len(t_parts), len(s_parts) * unit), jnp.int32)
    smem = pl.BlockSpec(memory_space=pltpu.SMEM)
    return pl.pallas_call(
        functools.partial(flags_kernel, layout, m, t_parts, s_parts, unit),
        out_shape=out,
        in_specs=[smem] * 2,
        out_specs=VMEM,
        scratch_shapes=[pltpu.VMEM((1, out.shape[1]), jnp.int32)],
        compiler_params=limits(out, out),
        cost_estimate=pl.CostEstimate(flops=0, bytes_accessed=32 * 2**20, transcendentals=0),
    )(place, pattern.T)


def tiles_of(refs, scratch, d):
    tiles, held = [], 0
    for ref in refs:
        rows = ref.shape[0]
        if rows % (2 * BLOCK) == 0:
            tiles += [(ref, k, 2 * BLOCK) for k in range(0, rows, 2 * BLOCK)]
        else:
            scratch[held : held + rows, :] = ref[:, :d]
            held += rows
    k = 0
    while k < held:
        rows = min(2 * BLOCK, held - k)
        tiles.append((scratch, k, rows))
        k += rows
    return tiles


def gram_kernel(nt, ns, sub, d, t_first, s_first, flags, *refs):
    t_in, s_in, refs = refs[:nt], refs[nt : nt + ns], refs[nt + ns :]
    kern, acc, t_join, s_join = refs
    t_tiles, s_tiles = tiles_of(t_in, t_join, d), tiles_of(s_in, s_join, d)
    rows, cols = kern.shape
    col = 0
    for s_ref, s_at, width in s_tiles:
        row = 0
        for t_ref, t_at, tall in t_tiles:
            scores = lax.dot_general(
                t_ref[t_at : t_at + tall, :],
                s_ref[s_at : s_at + width, :d],
                (((1,), (1,)), ((), ())),
                preferred_element_type=jnp.float32,
            )
            value = jnp.exp(sharpness * scores).astype(jnp.bfloat16).astype(jnp.float32)
            for a in range(tall // sub):
                at = row + a * sub
                flag = flags[
                    (t_first + at) // sub : (t_first + at) // sub + 1,
                    s_first + col : s_first + col + width,
                ]
                part = jnp.where(flag > 0, value[a * sub : (a + 1) * sub], 0.0)
                kern[at : at + sub, col : col + width] = part.astype(jnp.bfloat16)
                total = part[:, :BLOCK]
                for b in range(1, width // BLOCK):
                    total = total + part[:, b * BLOCK : (b + 1) * BLOCK]
                if col > 0:
                    total = total + acc[at : at + sub, :]
                acc[at : at + sub, :] = total
            row += tall
        col += width


def gram_call(flags, t_pieces, s_pieces, sub, t_first, s_first):
    rows, cols = (sum(p.shape[0] for p in pieces) for pieces in (t_pieces, s_pieces))
    d = t_pieces[0].shape[1]
    join = [
        shape((max(16, sum(p.shape[0] for p in pieces if p.shape[0] % (2 * BLOCK))), d))
        for pieces in (t_pieces, s_pieces)
    ]
    outs = [shape((rows, cols)), shape((rows, BLOCK), jnp.float32)]
    return pl.pallas_call(
        functools.partial(
            gram_kernel, len(t_pieces), len(s_pieces), sub, d, t_first, s_first
        ),
        out_shape=outs,
        in_specs=[VMEM] * (1 + len(t_pieces) + len(s_pieces)),
        out_specs=[VMEM] * 2,
        scratch_shapes=[pltpu.VMEM(j.shape, j.dtype) for j in join],
        compiler_params=limits(flags, *t_pieces, *s_pieces, *outs, *join),
        cost_estimate=pl.CostEstimate(
            flops=2 * rows * cols * d,
            bytes_accessed=2 * (rows + cols) * d,
            transcendentals=rows * cols,
        ),
    )(flags, *t_pieces, *s_pieces)


def spread_kernel(plan, nk, na, ns, *refs):
    m, t_layout, rects, p_map = plan
    kerns, refs = refs[:nk], refs[nk:]
    accs, refs = refs[:na], refs[na:]
    p_in, refs = refs[:ns], refs[ns:]
    outs, pcat = refs[:-1], refs[-1]
    own_ref, other_refs = outs[0], outs[2:] if na else outs[1:]
    c = pcat.shape[1]
    at = 0
    for index, start, rows in p_map:
        ref = p_in[index]
        pcat[at : at + rows, :] = ref[start : start + rows, ref.shape[1] - c :]
        at += rows
    row = 0
    for piece, start, rows in t_layout:
        part = None
        for kern, (t0, t1, c0, c1) in zip(kerns, rects):
            if t0 <= row < t1:
                term = jnp.dot(
                    kern[row - t0 : row - t0 + rows, :],
                    pcat[c0:c1, :],
                    preferred_element_type=jnp.float32,
                )
                part = term if part is None else part + term
        if piece == 0:
            own_ref[start : start + rows, :] = part
        else:
            other_refs[piece - 1][start : start + rows, :] = part.astype(jnp.bfloat16)
        step = math.gcd(rows, BLOCK)
        for lane in range(0, rows if na else 0, step):
            total = None
            for acc, (t0, t1, c0, c1) in zip(accs, rects):
                if t0 <= row < t1:
                    first = row - t0 + lane
                    term = acc[first : first + step, :]
                    total = term if total is None else total + term
            total = jnp.sum(total.T, axis=0, keepdims=True)
            lanes = slice(start + lane, start + lane + step)
            if piece == 0:
                outs[1][:, lanes] = total
            else:
                high = total.astype(jnp.bfloat16).astype(jnp.float32)
                mid = (total - high).astype(jnp.bfloat16).astype(jnp.float32)
                low = total - high - mid
                index = lax.broadcasted_iota(jnp.int32, (16, step), 0)
                terms = jnp.where(index == 0, high, jnp.where(index == 1, mid, low))
                terms = jnp.where(index < 3, terms, 0.0)
                other_refs[piece - 1][m:, lanes] = terms.astype(jnp.bfloat16)
        row += rows


def spread_call(kerns, accs, p_pieces, c, plan):
    m, t_layout, rects, p_map = plan
    nt = 1 + max(piece for piece, _, _ in t_layout)
    cols = sum(rows for _, _, rows in p_map)
    extra = 16 if accs else 0
    outs = [jax.ShapeDtypeStruct((m, c), jnp.float32)]
    if accs:
        outs.append(jax.ShapeDtypeStruct((1, m), jnp.float32))
    outs += [jax.ShapeDtypeStruct((m + extra, c), jnp.bfloat16)] * (nt - 1)
    return pl.pallas_call(
        functools.partial(spread_kernel, plan, len(kerns), len(accs), len(p_pieces)),
        out_shape=outs,
        in_specs=[VMEM] * (len(kerns) + len(accs) + len(p_pieces)),
        out_specs=[VMEM] * len(outs),
        scratch_shapes=[pltpu.VMEM((cols, c), jnp.bfloat16)],
        compiler_params=limits(*kerns, *accs, *p_pieces, *outs, shape((cols, c))),
        cost_estimate=pl.CostEstimate(
            flops=2 * nt * m * cols * c,
            bytes_accessed=2 * (nt * m * cols + cols * c),
            transcendentals=0,
        ),
    )(*kerns, *accs, *p_pieces)


def first_update_kernel(seed_ref, own_ref, own_total_ref, *refs):
    got, (panel_ref, total_ref) = refs[:-2], refs[-2:]
    m = seed_ref.shape[0]
    numerators = own_ref[...]
    for ref in got:
        numerators = numerators + ref[:m, :].astype(jnp.float32)
    totals = own_total_ref[...]
    for ref in got:
        terms = ref[m:, :m].astype(jnp.float32)
        totals = totals + jnp.sum(terms, axis=0, keepdims=True)
    step = min(m, BLOCK)
    for k in range(0, m, step):
        total_ref[k : k + step, :] = jnp.broadcast_to(totals[:, k : k + step], (BLOCK, step)).T
    for k in range(0, seed_ref.shape[1], BLOCK):
        labels = mixing * numerators[:, k : k + BLOCK] / total_ref[...] + (
            1.0 - mixing
        ) * seed_ref[:, k : k + BLOCK].astype(jnp.float32)
        panel_ref[:, k : k + BLOCK] = labels.astype(jnp.bfloat16)


def last_update_kernel(seed_ref, own_ref, total_ref, *refs):
    got, out_ref = refs[:-1], refs[-1]
    numerators = own_ref[...]
    for ref in got:
        numerators = numerators + ref[...].astype(jnp.float32)
    for k in range(0, seed_ref.shape[1], BLOCK):
        out_ref[:, k : k + BLOCK] = mixing * numerators[:, k : k + BLOCK] / total_ref[...] + (
            1.0 - mixing
        ) * seed_ref[:, k : k + BLOCK].astype(jnp.float32)


def update(kernel, seeds, own, totals, got, out_shape):
    return pl.pallas_call(
        kernel,
        out_shape=out_shape,
        in_specs=[VMEM] * (3 + len(got)),
        out_specs=jax.tree.map(lambda _: VMEM, out_shape),
        compiler_params=limits(seeds, own, totals, *got, own, own),
    )(seeds, own, totals, *got)


def after(value, *earlier):
    return lax.optimization_barrier((value, *earlier))[0]


def on_device(embeddings, seed_labels, pattern):
    layout = Layout(lax.axis_size("row"), lax.axis_size("col"))
    size = layout.sizes
    m, c = embeddings.shape[0], seed_labels.shape[1]
    sub = math.gcd(BLOCK, m // 4) if m % (2 * BLOCK) == 0 else min(m, BLOCK)
    other = {k: range(1, size[k]) for k in size}
    chunks = [(0, 3 * m // 4), (3 * m // 4, m // 4)] if m % (2 * BLOCK) == 0 else [(0, m)]

    def fetch(values, axis, *earlier):
        return [
            layout.fetch(after(v, *earlier), **{axis: k}) for k in other[axis] for v in values
        ]

    units, packed, parts = unit_rows(embeddings, seed_labels, chunks)

    t_index = {(b, a): b * size["x"] + a for b in range(size["zl"]) for a in range(size["x"])}
    t_layout = [(t_index[0, a], 0, m) for a in range(size["x"])]
    t_groups = [len(t_layout)]
    for start, rows in chunks:
        t_layout += [(t_index[b, 0], start, rows) for b in other["zl"]]
        t_groups.append(len(t_layout))
        t_layout += [(t_index[b, a], start, rows) for a in other["x"] for b in other["zl"]]
        t_groups.append(len(t_layout))
    both = [0] + list(other["core"])
    groups = [[(0, a, k, 0, m) for a in range(size["y"]) for k in both]]
    for start, rows in chunks:
        group = [(b, 0, k, start, rows) for k in both for b in other["zh"]]
        group += [(b, a, k, start, rows) for k in both for a in other["y"] for b in other["zh"]]
        groups.append(group)
    s_layout = [piece for group in groups for piece in group]
    whole = [(0, a, k) for a in range(size["y"]) for k in both]
    whole += [(b, 0, k) for k in both for b in other["zh"]]
    whole += [(b, a, k) for k in both for a in other["y"] for b in other["zh"]]
    p_map = [(whole.index(piece[:3]), *piece[3:]) for piece in s_layout]

    t_offsets = [dict(zl=b, x=a) for b, a in t_index]
    unit = sub
    t_parts = [
        (t_offsets[i], start + k) for i, start, rows in t_layout for k in range(0, rows, sub)
    ]
    s_parts = [
        (dict(zh=b, y=a, core=k), start + at)
        for b, a, k, start, rows in s_layout
        for at in range(0, rows, unit)
    ]
    t_pieces, kerns, accs, rects = [], [], [], []
    s_pieces = [None] * len(groups)

    def rectangle(first, last, g0, g1):
        t0, t1 = (sum(rows for _, _, rows in t_layout[:i]) for i in (first, last))
        c0, c1 = (sum(p[4] for group in groups[:g] for p in group) for g in (g0, g1))
        if t0 == t1 or c0 == c1:
            return []
        kern, acc = gram_call(
            flags,
            t_pieces[first:last],
            [p for g in range(g0, g1) for p in s_pieces[g]],
            sub,
            t0,
            c0,
        )
        kerns.append(kern)
        accs.append(acc)
        rects.append((t0, t1, c0, c1))
        return [acc]

    zh, zl = fetch(parts[0], "zh"), fetch(parts[0], "zl")
    x, y = fetch([units], "x"), fetch([packed], "y")
    own_core = fetch([packed], "core")
    t_pieces += [units] + x + zl
    flags = flags_call(layout, m, t_parts, s_parts, unit, after(pattern, *zh, *zl))
    done = zh + zl + x + y + own_core + [flags]
    zh_next, zl_next = fetch(parts[1], "zh", *done), fetch(parts[1], "zl", *done)
    zh_y, zl_x = fetch(zh, "y", *done), fetch(zl, "x", *done)
    y_core = [fetch([v], "core", *done) for v in y]
    t_pieces += zl_x
    s_pieces[0] = [packed] + own_core + [p for v, w in zip(y, y_core) for p in [v] + w]
    first = rectangle(0, t_groups[1], 0, 1)
    zh_core = fetch(zh, "core", *done, *[p for w in y_core for p in w])
    last = len(t_layout)
    if zh_next:
        done = zh_next + zl_next + zh_y + zl_x + zh_core + first
        zh_next_y, zl_next_x = fetch(zh_next, "y", *done), fetch(zl_next, "x", *done)
        zh_y_core, zh_next_core = fetch(zh_y, "core", *done), fetch(zh_next, "core", *done)
        seeds_zh = fetch([seed_labels], "zh", *done)
        t_pieces += zl_next + zl_next_x
        s_pieces[1] = zh + zh_core + zh_y + zh_y_core
        second = rectangle(t_groups[1], t_groups[2], 0, 1) + rectangle(0, t_groups[2], 1, 2)
        done = zh_next_y + zl_next_x + zh_next_core + zh_y_core + second
        zh_next_y_core = fetch(zh_next_y, "core", *done)
        s_pieces[2] = zh_next + zh_next_core + zh_next_y + zh_next_y_core
        rectangle(t_groups[2], last, 0, 2)
        rectangle(0, last, 2, 3)
    else:
        seeds_zh, zh_y_core = fetch([seed_labels], "zh", *done), fetch(zh_y, "core", *done)
        s_pieces[1] = zh + zh_core + zh_y + zh_y_core
        rectangle(t_groups[1], last, 0, 1)
        rectangle(0, last, 1, 2)
        done = []
    seeds_y, seeds_core = fetch(seeds_zh, "y", *done), fetch(seeds_zh, "core", *done)
    seeds_y_core = fetch(seeds_y, "core")
    plan = (m, t_layout, rects, p_map)

    def home(values):
        return [
            layout.fetch(v, **{k: -d for k, d in o.items()})
            for v, o in zip(values, t_offsets[1:])
        ]

    def panels(panel):
        far, near = fetch([panel], "zh"), fetch([panel], "y")
        far_y = fetch(far, "y")
        near = [p for v in [panel] + near for p in [v] + fetch([v], "core")]
        return near + far + fetch(far, "core") + far_y + fetch(far_y, "core")

    seeds = s_pieces[0] + seeds_zh + seeds_core + seeds_y + seeds_y_core
    own, totals, *others = spread_call(kerns, accs, seeds, c, plan)
    panel, totals = update(
        first_update_kernel,
        seed_labels,
        own,
        totals,
        home(others),
        [
            jax.ShapeDtypeStruct((m, c), jnp.bfloat16),
            jax.ShapeDtypeStruct((m, BLOCK), jnp.float32),
        ],
    )
    own, *others = spread_call(kerns, [], panels(panel), c, plan)
    return update(
        last_update_kernel,
        seed_labels,
        own,
        totals,
        home(others),
        jax.ShapeDtypeStruct((m, c), jnp.float32),
    )


def solution(mesh):
    return jax.shard_map(
        on_device,
        mesh=mesh,
        in_specs=(P(("col", "row"), None), P(("col", "row"), None), P()),
        out_specs=P(("col", "row"), None),
        check_vma=False,
    )
```

```python
import functools
import math

import jax
import jax.numpy as jnp
from jax import lax
from jax.experimental import pallas as pl
from jax.experimental.pallas import tpu as pltpu
from jax.sharding import PartitionSpec as P

BLOCK = 128
AXES = ("row", "col")

sharpness = 30.0
mixing = 0.8
epsilon = 1e-06


def split_two(n):
    low = max(d for d in range(1, math.isqrt(n) + 1) if n % d == 0)
    return n // low, low


class Layout:
    def __init__(self, rows, cols):
        core = 2 if cols % 2 == 0 else 1
        ny, nx = split_two(rows)
        nzh, nzl = split_two(cols // core)
        self.sizes = dict(y=ny, x=nx, zh=nzh, zl=nzl, core=core)
        self.rows, self.cols = rows, cols

    def coords(self, row, col):
        s = self.sizes
        return dict(
            y=row // s["x"],
            x=row % s["x"],
            zh=col // (s["zl"] * s["core"]),
            zl=col // s["core"] % s["zl"],
            core=col % s["core"],
        )

    def moved(self, at, offset):
        return {k: (at[k] + offset.get(k, 0)) % self.sizes[k] for k in at}

    def row_col(self, at):
        s = self.sizes
        return at["y"] * s["x"] + at["x"], (at["zh"] * s["zl"] + at["zl"]) * s["core"] + at["core"]

    def fetch(self, value, **offset):
        if all(v % self.sizes[k] == 0 for k, v in offset.items()):
            return value
        pairs = []
        for row in range(self.rows):
            for col in range(self.cols):
                r, c = self.row_col(self.moved(self.coords(row, col), offset))
                pairs.append((r * self.cols + c, row * self.cols + col))
        return lax.ppermute(value, AXES, pairs)

    def device(self, offset):
        at = self.coords(lax.axis_index("row"), lax.axis_index("col"))
        row, col = self.row_col(self.moved(at, offset))
        return col * self.rows + row


VMEM = pl.BlockSpec(memory_space=pltpu.VMEM)


def limits(*arrays, mib=3):
    total = sum(max(math.prod(a.shape), 8 * BLOCK) * a.dtype.itemsize for a in arrays)
    return pltpu.CompilerParams(vmem_limit_bytes=total * 5 // 4 + mib * 2**20)


def shape(dims, dtype=jnp.bfloat16):
    return jax.ShapeDtypeStruct(dims, dtype)


def unit_of(values):
    values = values.astype(jnp.float32)
    mean_square = jnp.mean(values * values, axis=1, keepdims=True)
    scaled = values * lax.rsqrt(mean_square + epsilon) * values.shape[1] ** (-0.5)
    return scaled.astype(jnp.bfloat16)


def unit_kernel(emb_ref, seed_ref, unit_ref, packed_ref):
    d = emb_ref.shape[1]
    unit = unit_of(emb_ref[...])
    unit_ref[...] = unit
    packed_ref[:, :d] = unit
    packed_ref[:, d:] = seed_ref[...]


def unit_rows(embeddings, seeds):
    (m, d), c = embeddings.shape, seeds.shape[1]
    outs = [shape((m, d)), shape((m, d + c))]
    return pl.pallas_call(
        unit_kernel,
        out_shape=outs,
        out_specs=[VMEM] * 2,
        compiler_params=limits(embeddings, embeddings, seeds, seeds, *outs, embeddings),
    )(embeddings, seeds)


def flags_kernel(layout, m, t_parts, s_parts, unit, place_ref, pattern_ref, out_ref, block_ref):
    at = layout.coords(place_ref[0], place_ref[1])

    def block(offset, start):
        row, col = layout.row_col(layout.moved(at, offset))
        return ((col * layout.rows + row) * m + start) // BLOCK

    for k, (offset, start) in enumerate(s_parts):
        block_ref[:, k * unit : (k + 1) * unit] = jnp.full((1, unit), block(offset, start), jnp.int32)
    blocks = block_ref[...]
    for r, (offset, start) in enumerate(t_parts):
        target = block(offset, start)
        hits = blocks == pattern_ref[0, target]
        for k in range(1, pattern_ref.shape[0]):
            hits = hits | (blocks == pattern_ref[k, target])
        out_ref[r : r + 1, :] = jnp.where(hits, 1, 0)


def flags_call(layout, m, t_parts, s_parts, unit, pattern):
    place = jnp.stack([lax.axis_index("row"), lax.axis_index("col")]).astype(jnp.int32)
    out = shape((len(t_parts), len(s_parts) * unit), jnp.int32)
    smem = pl.BlockSpec(memory_space=pltpu.SMEM)
    return pl.pallas_call(
        functools.partial(flags_kernel, layout, m, t_parts, s_parts, unit),
        out_shape=out,
        in_specs=[smem] * 2,
        out_specs=VMEM,
        scratch_shapes=[pltpu.VMEM((1, out.shape[1]), jnp.int32)],
        compiler_params=limits(out, out),
        cost_estimate=pl.CostEstimate(flops=0, bytes_accessed=256 * 2**20, transcendentals=0),
    )(place, pattern.T)


def tiles_of(refs, scratch, d):
    tiles, held = [], 0
    for ref in refs:
        rows = ref.shape[0]
        if rows % (2 * BLOCK) == 0:
            tiles += [(ref, k, 2 * BLOCK) for k in range(0, rows, 2 * BLOCK)]
        else:
            scratch[held : held + rows, :] = ref[:, :d]
            held += rows
    k = 0
    while k < held:
        rows = next(w for w in (2 * BLOCK, BLOCK, BLOCK // 2) if held - k >= w)
        tiles.append((scratch, k, rows))
        k += rows
    return tiles


def gram_kernel(nt, ns, sub, d, t_first, s_first, flags, *refs):
    t_in, s_in, refs = refs[:nt], refs[nt : nt + ns], refs[nt + ns :]
    kern, acc, t_join, s_join = refs
    t_tiles, s_tiles = tiles_of(t_in, t_join, d), tiles_of(s_in, s_join, d)
    rows, cols = kern.shape
    col = 0
    for s_ref, s_at, width in s_tiles:
        row = 0
        for t_ref, t_at, tall in t_tiles:
            scores = lax.dot_general(
                t_ref[t_at : t_at + tall, :],
                s_ref[s_at : s_at + width, :d],
                (((1,), (1,)), ((), ())),
                preferred_element_type=jnp.float32,
            )
            value = jnp.exp(sharpness * scores).astype(jnp.bfloat16).astype(jnp.float32)
            for a in range(tall // sub):
                at = row + a * sub
                flag = flags[
                    (t_first + at) // sub : (t_first + at) // sub + 1,
                    s_first + col : s_first + col + width,
                ]
                part = jnp.where(flag > 0, value[a * sub : (a + 1) * sub], 0.0)
                kern[at : at + sub, col : col + width] = part.astype(jnp.bfloat16)
                if width % BLOCK:
                    if col == 0:
                        acc[at : at + sub, :] = jnp.zeros((sub, BLOCK), jnp.float32)
                    acc[at : at + sub, :width] += part
                    continue
                total = part[:, :BLOCK]
                for b in range(1, width // BLOCK):
                    total = total + part[:, b * BLOCK : (b + 1) * BLOCK]
                if col > 0:
                    total = total + acc[at : at + sub, :]
                acc[at : at + sub, :] = total
            row += tall
        col += width


def gram_call(flags, t_pieces, s_pieces, sub, t_first, s_first):
    rows, cols = (sum(p.shape[0] for p in pieces) for pieces in (t_pieces, s_pieces))
    d = t_pieces[0].shape[1]
    join = [
        shape((max(16, sum(p.shape[0] for p in pieces if p.shape[0] % (2 * BLOCK))), d))
        for pieces in (t_pieces, s_pieces)
    ]
    outs = [shape((rows, cols)), shape((rows, BLOCK), jnp.float32)]
    return pl.pallas_call(
        functools.partial(
            gram_kernel, len(t_pieces), len(s_pieces), sub, d, t_first, s_first
        ),
        out_shape=outs,
        in_specs=[VMEM] * (1 + len(t_pieces) + len(s_pieces)),
        out_specs=[VMEM] * 2,
        scratch_shapes=[pltpu.VMEM(j.shape, j.dtype) for j in join],
        compiler_params=limits(flags, *t_pieces, *s_pieces, *outs, *join),
        cost_estimate=pl.CostEstimate(
            flops=2 * rows * cols * d,
            bytes_accessed=2 * (rows + cols) * d,
            transcendentals=rows * cols,
        ),
    )(flags, *t_pieces, *s_pieces)


def spread_kernel(plan, nk, na, ns, *refs):
    m, t_layout, rects, p_map = plan
    kerns, refs = refs[:nk], refs[nk:]
    accs, refs = refs[:na], refs[na:]
    p_in, refs = refs[:ns], refs[ns:]
    outs, pcat = refs[:-1], refs[-1]
    own_ref, other_refs = outs[0], outs[2:] if na else outs[1:]
    c = pcat.shape[1]
    at = 0
    for index, start, rows in p_map:
        ref = p_in[index]
        pcat[at : at + rows, :] = ref[start : start + rows, ref.shape[1] - c :]
        at += rows
    row = 0
    for piece, start, rows in t_layout:
        part = None
        for kern, (t0, t1, c0, c1) in zip(kerns, rects):
            if t0 <= row < t1:
                term = jnp.dot(
                    kern[row - t0 : row - t0 + rows, :],
                    pcat[c0:c1, :],
                    preferred_element_type=jnp.float32,
                )
                part = term if part is None else part + term
        if piece == 0:
            own_ref[start : start + rows, :] = part
        else:
            other_refs[piece - 1][start : start + rows, :] = part.astype(jnp.bfloat16)
        step = math.gcd(rows, BLOCK)
        for lane in range(0, rows if na else 0, step):
            total = None
            for acc, (t0, t1, c0, c1) in zip(accs, rects):
                if t0 <= row < t1:
                    first = row - t0 + lane
                    term = acc[first : first + step, :]
                    total = term if total is None else total + term
            total = jnp.sum(total.T, axis=0, keepdims=True)
            lanes = slice(start + lane, start + lane + step)
            if piece == 0:
                outs[1][:, lanes] = total
            else:
                high = total.astype(jnp.bfloat16).astype(jnp.float32)
                mid = (total - high).astype(jnp.bfloat16).astype(jnp.float32)
                low = total - high - mid
                index = lax.broadcasted_iota(jnp.int32, (16, step), 0)
                terms = jnp.where(index == 0, high, jnp.where(index == 1, mid, low))
                terms = jnp.where(index < 3, terms, 0.0)
                other_refs[piece - 1][m:, lanes] = terms.astype(jnp.bfloat16)
        row += rows


def spread_call(kerns, accs, p_pieces, c, plan):
    m, t_layout, rects, p_map = plan
    nt = 1 + max(piece for piece, _, _ in t_layout)
    cols = sum(rows for _, _, rows in p_map)
    extra = 16 if accs else 0
    outs = [jax.ShapeDtypeStruct((m, c), jnp.float32)]
    if accs:
        outs.append(jax.ShapeDtypeStruct((1, m), jnp.float32))
    outs += [jax.ShapeDtypeStruct((m + extra, c), jnp.bfloat16)] * (nt - 1)
    return pl.pallas_call(
        functools.partial(spread_kernel, plan, len(kerns), len(accs), len(p_pieces)),
        out_shape=outs,
        in_specs=[VMEM] * (len(kerns) + len(accs) + len(p_pieces)),
        out_specs=[VMEM] * len(outs),
        scratch_shapes=[pltpu.VMEM((cols, c), jnp.bfloat16)],
        compiler_params=limits(*kerns, *accs, *p_pieces, *outs, shape((cols, c))),
        cost_estimate=pl.CostEstimate(
            flops=2 * nt * m * cols * c,
            bytes_accessed=2 * (nt * m * cols + cols * c),
            transcendentals=0,
        ),
    )(*kerns, *accs, *p_pieces)


def first_update_kernel(seed_ref, own_ref, own_total_ref, *refs):
    got, (panel_ref, total_ref) = refs[:-2], refs[-2:]
    m = seed_ref.shape[0]
    numerators = own_ref[...]
    for ref in got:
        numerators = numerators + ref[:m, :].astype(jnp.float32)
    totals = own_total_ref[...]
    for ref in got:
        terms = ref[m:, :m].astype(jnp.float32)
        totals = totals + jnp.sum(terms, axis=0, keepdims=True)
    step = min(m, BLOCK)
    for k in range(0, m, step):
        total_ref[k : k + step, :] = jnp.broadcast_to(totals[:, k : k + step], (BLOCK, step)).T
    for k in range(0, seed_ref.shape[1], BLOCK):
        labels = mixing * numerators[:, k : k + BLOCK] / total_ref[...] + (
            1.0 - mixing
        ) * seed_ref[:, k : k + BLOCK].astype(jnp.float32)
        panel_ref[:, k : k + BLOCK] = labels.astype(jnp.bfloat16)


def last_update_kernel(seed_ref, own_ref, total_ref, *refs):
    got, out_ref = refs[:-1], refs[-1]
    numerators = own_ref[...]
    for ref in got:
        numerators = numerators + ref[...].astype(jnp.float32)
    for k in range(0, seed_ref.shape[1], BLOCK):
        out_ref[:, k : k + BLOCK] = mixing * numerators[:, k : k + BLOCK] / total_ref[...] + (
            1.0 - mixing
        ) * seed_ref[:, k : k + BLOCK].astype(jnp.float32)


def update(kernel, seeds, own, totals, got, out_shape):
    return pl.pallas_call(
        kernel,
        out_shape=out_shape,
        in_specs=[VMEM] * (3 + len(got)),
        out_specs=jax.tree.map(lambda _: VMEM, out_shape),
        compiler_params=limits(seeds, own, totals, *got, own, own),
    )(seeds, own, totals, *got)


def after(value, *earlier):
    return lax.optimization_barrier((value, *earlier))[0]


def on_device(embeddings, seed_labels, pattern):
    layout = Layout(lax.axis_size("row"), lax.axis_size("col"))
    size = layout.sizes
    m, c = embeddings.shape[0], seed_labels.shape[1]
    sub = min(m, BLOCK)
    other = {k: range(1, size[k]) for k in size}

    def fetch(values, axis, *earlier):
        return [
            layout.fetch(after(v, *earlier), **{axis: k}) for k in other[axis] for v in values
        ]

    t_offsets = [dict(zl=b, x=a) for b in range(size["zl"]) for a in range(size["x"])]
    near_t = [i for i, o in enumerate(t_offsets) if o["x"] == 0 or o["zl"] == 0]
    t_order = near_t + [i for i in range(len(t_offsets)) if i not in near_t]
    t_layout = [(i, 0, m) for i in t_order]
    both = [0] + list(other["core"])
    groups = [
        [(0, a, k) for a in range(size["y"]) for k in both],
        [(b, 0, k) for k in both for b in other["zh"]],
        [(b, a, 0) for a in other["y"] for b in other["zh"]],
        [(b, a, k) for k in other["core"] for a in other["y"] for b in other["zh"]],
    ]
    s_layout = [dict(zh=b, y=a, core=k) for group in groups for b, a, k in group]
    p_map = [(i, 0, m) for i in range(len(s_layout))]
    t_parts = [(t_offsets[i], k) for i in t_order for k in range(0, m, sub)]
    s_parts = [(o, k) for o in s_layout for k in range(0, m, sub)]
    units, packed = unit_rows(embeddings, seed_labels)

    t_pieces, kerns, accs, rects = [], [], [], []
    s_pieces = [None] * len(groups)

    def rectangle(first, last, g0, g1):
        t0, t1 = first * m, last * m
        c0, c1 = (m * sum(len(group) for group in groups[:g]) for g in (g0, g1))
        if t0 == t1 or c0 == c1:
            return []
        kern, acc = gram_call(
            flags,
            t_pieces[first:last],
            [p for g in range(g0, g1) for p in s_pieces[g]],
            sub,
            t0,
            c0,
        )
        kerns.append(kern)
        accs.append(acc)
        rects.append((t0, t1, c0, c1))
        return [acc]

    zh, zl, x = fetch([units], "zh"), fetch([units], "zl"), fetch([units], "x")
    y, own_core = fetch([packed], "y"), fetch([packed], "core")
    flags = flags_call(layout, m, t_parts, s_parts, sub, after(pattern, *zh))
    done = zh + zl + x + y + own_core + [flags]
    zh_y, zl_x = fetch(zh, "y", *done), fetch(zl, "x", *done)
    y_core = [fetch([v], "core", *done) for v in y]
    zh_core = fetch(zh, "core", *done)
    seeds_zh = fetch([seed_labels], "zh", *done)
    by_offset = {(0, 0): units}
    by_offset.update({(0, a): v for a, v in zip(other["x"], x)})
    by_offset.update({(b, 0): v for b, v in zip(other["zl"], zl)})
    by_offset.update({(b, a): v for (a, b), v in zip([(a, b) for a in other["x"] for b in other["zl"]], zl_x)})
    t_pieces += [by_offset[t_offsets[i]["zl"], t_offsets[i]["x"]] for i in t_order]
    s_pieces[0] = [packed] + own_core + [p for v, w in zip(y, y_core) for p in [v] + w]
    s_pieces[1] = zh + zh_core
    s_pieces[2] = zh_y
    early, last = len(near_t), len(t_order)
    gram = rectangle(0, early, 0, 1) + rectangle(0, early, 1, 2)
    done = zh_y + zl_x + zh_core + seeds_zh + gram
    zh_y_core = fetch(zh_y, "core", *done)
    s_pieces[3] = zh_y_core
    seeds_y, seeds_core = fetch(seeds_zh, "y", *done), fetch(seeds_zh, "core", *done)
    seeds_y_core = fetch(seeds_y, "core")
    rectangle(early, last, 0, 2)
    rectangle(0, last, 2, 3)
    rectangle(0, last, 3, 4)
    plan = (m, t_layout, rects, p_map)

    def home(values):
        return [
            layout.fetch(v, **{k: -d for k, d in o.items()})
            for v, o in zip(values, t_offsets[1:])
        ]

    def panels(panel):
        far, near = fetch([panel], "zh"), fetch([panel], "y")
        far_y = fetch(far, "y")
        near = [p for v in [panel] + near for p in [v] + fetch([v], "core")]
        return near + far + fetch(far, "core") + far_y + fetch(far_y, "core")

    seeds = s_pieces[0] + seeds_zh + seeds_core + seeds_y + seeds_y_core
    own, totals, *others = spread_call(kerns, accs, seeds, c, plan)
    panel, totals = update(
        first_update_kernel,
        seed_labels,
        own,
        totals,
        home(others),
        [
            jax.ShapeDtypeStruct((m, c), jnp.bfloat16),
            jax.ShapeDtypeStruct((m, BLOCK), jnp.float32),
        ],
    )
    own, *others = spread_call(kerns, [], panels(panel), c, plan)
    return update(
        last_update_kernel,
        seed_labels,
        own,
        totals,
        home(others),
        jax.ShapeDtypeStruct((m, c), jnp.float32),
    )


def solution(mesh):
    return jax.shard_map(
        on_device,
        mesh=mesh,
        in_specs=(P(("col", "row"), None), P(("col", "row"), None), P()),
        out_specs=P(("col", "row"), None),
        check_vma=False,
    )
```

```python
import functools
import math

import jax
import jax.numpy as jnp
from jax import lax
from jax.experimental import pallas as pl
from jax.experimental.pallas import tpu as pltpu
from jax.sharding import PartitionSpec as P

BLOCK = 128
AXES = ("row", "col")

sharpness = 30.0
mixing = 0.8
epsilon = 1e-06


def split_two(n):
    low = max(d for d in range(1, math.isqrt(n) + 1) if n % d == 0)
    return n // low, low


class Layout:
    def __init__(self, rows, cols):
        core = 2 if cols % 2 == 0 else 1
        ny, nx = split_two(rows)
        nzh, nzl = split_two(cols // core)
        self.sizes = dict(y=ny, x=nx, zh=nzh, zl=nzl, core=core)
        self.rows, self.cols = rows, cols

    def coords(self, row, col):
        s = self.sizes
        return dict(
            y=row // s["x"],
            x=row % s["x"],
            zh=col // (s["zl"] * s["core"]),
            zl=col // s["core"] % s["zl"],
            core=col % s["core"],
        )

    def moved(self, at, offset):
        return {k: (at[k] + offset.get(k, 0)) % self.sizes[k] for k in at}

    def row_col(self, at):
        s = self.sizes
        return at["y"] * s["x"] + at["x"], (at["zh"] * s["zl"] + at["zl"]) * s["core"] + at["core"]

    def fetch(self, value, **offset):
        if all(v % self.sizes[k] == 0 for k, v in offset.items()):
            return value
        pairs = []
        for row in range(self.rows):
            for col in range(self.cols):
                r, c = self.row_col(self.moved(self.coords(row, col), offset))
                pairs.append((r * self.cols + c, row * self.cols + col))
        return lax.ppermute(value, AXES, pairs)

    def device(self, offset):
        at = self.coords(lax.axis_index("row"), lax.axis_index("col"))
        row, col = self.row_col(self.moved(at, offset))
        return col * self.rows + row


VMEM = pl.BlockSpec(memory_space=pltpu.VMEM)


def limits(*arrays, mib=3):
    total = sum(max(math.prod(a.shape), 8 * BLOCK) * a.dtype.itemsize for a in arrays)
    return pltpu.CompilerParams(vmem_limit_bytes=total * 5 // 4 + mib * 2**20)


def shape(dims, dtype=jnp.bfloat16):
    return jax.ShapeDtypeStruct(dims, dtype)


def unit_of(values):
    values = values.astype(jnp.float32)
    mean_square = jnp.mean(values * values, axis=1, keepdims=True)
    scaled = values * lax.rsqrt(mean_square + epsilon) * values.shape[1] ** (-0.5)
    return scaled.astype(jnp.bfloat16)


def unit_kernel(chunks, emb_ref, seed_ref, unit_ref, packed_ref, *outs):
    d = emb_ref.shape[1]
    unit = unit_of(emb_ref[...])
    unit_ref[...] = unit
    packed_ref[:, :d] = unit
    packed_ref[:, d:] = seed_ref[...]
    for out, (start, rows) in zip(outs, chunks):
        out[:, :d] = unit_ref[start : start + rows, :]
        for k in range((out.shape[1] - d) // seed_ref.shape[1]):
            at = d + k * seed_ref.shape[1]
            out[:, at : at + seed_ref.shape[1]] = seed_ref[k * rows : (k + 1) * rows, :]


def unit_rows(embeddings, seeds, chunks, carrier):
    (m, d), c = embeddings.shape, seeds.shape[1]
    outs = [shape((m, d)), shape((m, d + c))]
    outs += [
        shape((rows, d + m // rows * c if i == carrier else d)) for i, (_, rows) in enumerate(chunks)
    ]
    units, packed, *parts = pl.pallas_call(
        functools.partial(unit_kernel, chunks),
        out_shape=outs,
        out_specs=[VMEM] * len(outs),
        compiler_params=limits(*[embeddings, seeds] * 2, *outs, embeddings),
    )(embeddings, seeds)
    return units, packed, parts


def flags_kernel(layout, m, t_parts, s_parts, unit, place_ref, pattern_ref, out_ref, block_ref):
    at = layout.coords(place_ref[0], place_ref[1])

    def block(offset, start):
        row, col = layout.row_col(layout.moved(at, offset))
        return ((col * layout.rows + row) * m + start) // BLOCK

    for k, (offset, start) in enumerate(s_parts):
        block_ref[:, k * unit : (k + 1) * unit] = jnp.full((1, unit), block(offset, start), jnp.int32)
    blocks = block_ref[...]
    for r, (offset, start) in enumerate(t_parts):
        target = block(offset, start)
        hits = blocks == pattern_ref[0, target]
        for k in range(1, pattern_ref.shape[0]):
            hits = hits | (blocks == pattern_ref[k, target])
        out_ref[r : r + 1, :] = jnp.where(hits, 1, 0)


def flags_call(layout, m, t_parts, s_parts, unit, pattern):
    place = jnp.stack([lax.axis_index("row"), lax.axis_index("col")]).astype(jnp.int32)
    out = shape((len(t_parts), len(s_parts) * unit), jnp.int32)
    smem = pl.BlockSpec(memory_space=pltpu.SMEM)
    return pl.pallas_call(
        functools.partial(flags_kernel, layout, m, t_parts, s_parts, unit),
        out_shape=out,
        in_specs=[smem] * 2,
        out_specs=VMEM,
        scratch_shapes=[pltpu.VMEM((1, out.shape[1]), jnp.int32)],
        compiler_params=limits(out, out),
    )(place, pattern.T)


def tiles_of(refs, scratch, d):
    tiles, held = [], 0
    for ref in refs:
        rows = ref.shape[0]
        if rows % (2 * BLOCK) == 0:
            tiles += [(ref, k, 2 * BLOCK) for k in range(0, rows, 2 * BLOCK)]
        else:
            scratch[held : held + rows, :] = ref[:, :d]
            held += rows
    k = 0
    while k < held:
        rows = next(w for w in (2 * BLOCK, BLOCK, BLOCK // 2) if held - k >= w)
        tiles.append((scratch, k, rows))
        k += rows
    return tiles


def gram_kernel(nt, ns, sub, d, t_first, s_first, flags, *refs):
    t_in, s_in, refs = refs[:nt], refs[nt : nt + ns], refs[nt + ns :]
    kern, acc, t_join, s_join = refs
    t_tiles, s_tiles = tiles_of(t_in, t_join, d), tiles_of(s_in, s_join, d)
    rows, cols = kern.shape
    col = 0
    for s_ref, s_at, width in s_tiles:
        row = 0
        for t_ref, t_at, tall in t_tiles:
            scores = lax.dot_general(
                t_ref[t_at : t_at + tall, :],
                s_ref[s_at : s_at + width, :d],
                (((1,), (1,)), ((), ())),
                preferred_element_type=jnp.float32,
            )
            value = jnp.exp(sharpness * scores).astype(jnp.bfloat16).astype(jnp.float32)
            for a in range(tall // sub):
                at = row + a * sub
                flag = flags[
                    (t_first + at) // sub : (t_first + at) // sub + 1,
                    s_first + col : s_first + col + width,
                ]
                part = jnp.where(flag > 0, value[a * sub : (a + 1) * sub], 0.0)
                kern[at : at + sub, col : col + width] = part.astype(jnp.bfloat16)
                if width % BLOCK:
                    if col == 0:
                        acc[at : at + sub, :] = jnp.zeros((sub, BLOCK), jnp.float32)
                    acc[at : at + sub, :width] += part
                    continue
                total = part[:, :BLOCK]
                for b in range(1, width // BLOCK):
                    total = total + part[:, b * BLOCK : (b + 1) * BLOCK]
                if col > 0:
                    total = total + acc[at : at + sub, :]
                acc[at : at + sub, :] = total
            row += tall
        col += width


def gram_call(flags, t_pieces, s_pieces, sub, t_first, s_first):
    rows, cols = (sum(p.shape[0] for p in pieces) for pieces in (t_pieces, s_pieces))
    d = t_pieces[0].shape[1]
    join = [
        shape((max(16, sum(p.shape[0] for p in pieces if p.shape[0] % (2 * BLOCK))), d))
        for pieces in (t_pieces, s_pieces)
    ]
    outs = [shape((rows, cols)), shape((rows, BLOCK), jnp.float32)]
    return pl.pallas_call(
        functools.partial(
            gram_kernel, len(t_pieces), len(s_pieces), sub, d, t_first, s_first
        ),
        out_shape=outs,
        in_specs=[VMEM] * (1 + len(t_pieces) + len(s_pieces)),
        out_specs=[VMEM] * 2,
        scratch_shapes=[pltpu.VMEM(j.shape, j.dtype) for j in join],
        compiler_params=limits(flags, *t_pieces, *s_pieces, *outs, *join),
        cost_estimate=pl.CostEstimate(
            flops=2 * rows * cols * d,
            bytes_accessed=2 * (rows + cols) * d,
            transcendentals=rows * cols,
        ),
    )(flags, *t_pieces, *s_pieces)


def spread_kernel(plan, nk, na, ns, *refs):
    m, t_layout, rects, p_map = plan
    kerns, refs = refs[:nk], refs[nk:]
    accs, refs = refs[:na], refs[na:]
    p_in, refs = refs[:ns], refs[ns:]
    outs, pcat = refs[:-1], refs[-1]
    own_ref, other_refs = outs[0], outs[2:] if na else outs[1:]
    c = pcat.shape[1]
    at = 0
    for index, start, rows, lane in p_map:
        pcat[at : at + rows, :] = p_in[index][start : start + rows, lane : lane + c]
        at += rows
    row = 0
    for piece, start, rows in t_layout:
        part = None
        for kern, (t0, t1, c0, c1) in zip(kerns, rects):
            if t0 <= row < t1:
                term = jnp.dot(
                    kern[row - t0 : row - t0 + rows, :],
                    pcat[c0:c1, :],
                    preferred_element_type=jnp.float32,
                )
                part = term if part is None else part + term
        if piece == 0:
            own_ref[start : start + rows, :] = part
        else:
            other_refs[piece - 1][start : start + rows, :] = part.astype(jnp.bfloat16)
        step = math.gcd(rows, BLOCK)
        for lane in range(0, rows if na else 0, step):
            total = None
            for acc, (t0, t1, c0, c1) in zip(accs, rects):
                if t0 <= row < t1:
                    first = row - t0 + lane
                    term = acc[first : first + step, :]
                    total = term if total is None else total + term
            total = jnp.sum(total.T, axis=0, keepdims=True)
            lanes = slice(start + lane, start + lane + step)
            if piece == 0:
                outs[1][:, lanes] = total
            else:
                high = total.astype(jnp.bfloat16).astype(jnp.float32)
                mid = (total - high).astype(jnp.bfloat16).astype(jnp.float32)
                low = total - high - mid
                index = lax.broadcasted_iota(jnp.int32, (16, step), 0)
                terms = jnp.where(index == 0, high, jnp.where(index == 1, mid, low))
                terms = jnp.where(index < 3, terms, 0.0)
                other_refs[piece - 1][m:, lanes] = terms.astype(jnp.bfloat16)
        row += rows


def spread_call(kerns, accs, p_pieces, c, plan):
    m, t_layout, rects, p_map = plan
    nt = 1 + max(piece for piece, _, _ in t_layout)
    cols = sum(rows for _, _, rows, _ in p_map)
    extra = 16 if accs else 0
    outs = [jax.ShapeDtypeStruct((m, c), jnp.float32)]
    if accs:
        outs.append(jax.ShapeDtypeStruct((1, m), jnp.float32))
    outs += [jax.ShapeDtypeStruct((m + extra, c), jnp.bfloat16)] * (nt - 1)
    return pl.pallas_call(
        functools.partial(spread_kernel, plan, len(kerns), len(accs), len(p_pieces)),
        out_shape=outs,
        in_specs=[VMEM] * (len(kerns) + len(accs) + len(p_pieces)),
        out_specs=[VMEM] * len(outs),
        scratch_shapes=[pltpu.VMEM((cols, c), jnp.bfloat16)],
        compiler_params=limits(*kerns, *accs, *p_pieces, *outs, shape((cols, c))),
        cost_estimate=pl.CostEstimate(
            flops=2 * nt * m * cols * c,
            bytes_accessed=2 * (nt * m * cols + cols * c),
            transcendentals=0,
        ),
    )(*kerns, *accs, *p_pieces)


def first_update_kernel(seed_ref, own_ref, own_total_ref, *refs):
    got, (panel_ref, total_ref) = refs[:-2], refs[-2:]
    m = seed_ref.shape[0]
    numerators = own_ref[...]
    for ref in got:
        numerators = numerators + ref[:m, :].astype(jnp.float32)
    totals = own_total_ref[...]
    for ref in got:
        terms = ref[m:, :m].astype(jnp.float32)
        totals = totals + jnp.sum(terms, axis=0, keepdims=True)
    step = min(m, BLOCK)
    for k in range(0, m, step):
        total_ref[k : k + step, :] = jnp.broadcast_to(totals[:, k : k + step], (BLOCK, step)).T
    for k in range(0, seed_ref.shape[1], BLOCK):
        labels = mixing * numerators[:, k : k + BLOCK] / total_ref[...] + (
            1.0 - mixing
        ) * seed_ref[:, k : k + BLOCK].astype(jnp.float32)
        panel_ref[:, k : k + BLOCK] = labels.astype(jnp.bfloat16)


def last_update_kernel(seed_ref, own_ref, total_ref, *refs):
    got, out_ref = refs[:-1], refs[-1]
    numerators = own_ref[...]
    for ref in got:
        numerators = numerators + ref[...].astype(jnp.float32)
    for k in range(0, seed_ref.shape[1], BLOCK):
        out_ref[:, k : k + BLOCK] = mixing * numerators[:, k : k + BLOCK] / total_ref[...] + (
            1.0 - mixing
        ) * seed_ref[:, k : k + BLOCK].astype(jnp.float32)


def update(kernel, seeds, own, totals, got, out_shape):
    return pl.pallas_call(
        kernel,
        out_shape=out_shape,
        in_specs=[VMEM] * (3 + len(got)),
        out_specs=jax.tree.map(lambda _: VMEM, out_shape),
        compiler_params=limits(seeds, own, totals, *got, own, own),
    )(seeds, own, totals, *got)


def after(value, *earlier):
    return lax.optimization_barrier((value, *earlier))[0]


def on_device(embeddings, seed_labels, pattern):
    layout = Layout(lax.axis_size("row"), lax.axis_size("col"))
    size = layout.sizes
    m, c = embeddings.shape[0], seed_labels.shape[1]
    zh_chunks = zl_chunks = [(0, m)]
    sub = min(m, BLOCK)
    if m % (2 * BLOCK) == 0:
        zh_chunks = [(0, 3 * m // 4), (3 * m // 4, m // 4)]
        zl_chunks = [(0, m // 2), (m // 2, m // 2)]
        sub = math.gcd(BLOCK, m // 4)
    other = {k: range(1, size[k]) for k in size}

    def fetch(values, axis, *earlier):
        return [
            layout.fetch(after(v, *earlier), **{axis: k}) for k in other[axis] for v in values
        ]

    units, packed, parts = unit_rows(
        embeddings, seed_labels, zh_chunks + zl_chunks, len(zh_chunks) - 1
    )
    zh_parts, zl_parts = parts[: len(zh_chunks)], parts[len(zh_chunks) :]

    t_index = {(b, a): b * size["x"] + a for b in range(size["zl"]) for a in range(size["x"])}
    t_layout = [(t_index[0, a], 0, m) for a in range(size["x"])]
    t_groups = [len(t_layout)]
    for start, rows in zl_chunks:
        t_layout += [(t_index[b, 0], start, rows) for b in other["zl"]]
        t_groups.append(len(t_layout))
        t_layout += [(t_index[b, a], start, rows) for a in other["x"] for b in other["zl"]]
        t_groups.append(len(t_layout))
    both = [0] + list(other["core"])
    groups = [[(0, a, k, 0, m) for a in range(size["y"]) for k in both]]
    for start, rows in zh_chunks:
        group = [(b, 0, k, start, rows) for k in both for b in other["zh"]]
        group += [(b, a, k, start, rows) for k in both for a in other["y"] for b in other["zh"]]
        groups.append(group)
    s_layout = [piece for group in groups for piece in group]
    whole = [(0, a, k) for a in range(size["y"]) for k in both]
    whole += [(b, 0, k) for k in both for b in other["zh"]]
    whole += [(b, a, k) for k in both for a in other["y"] for b in other["zh"]]
    d, tail = embeddings.shape[1], zh_chunks[-1][1]
    p_map = [(whole.index(piece[:3]), *piece[3:], 0) for piece in s_layout]
    seeds_map = []
    for piece in s_layout:
        index, (start, rows) = whole.index(piece[:3]), piece[3:]
        if index < len(groups[0]):
            seeds_map.append((index, start, rows, d))
        else:
            blocks = range(start // tail, (start + rows) // tail)
            seeds_map += [(index, 0, tail, d + k * c) for k in blocks]

    t_offsets = [dict(zl=b, x=a) for b, a in t_index]
    unit = sub
    t_parts = [
        (t_offsets[i], start + k) for i, start, rows in t_layout for k in range(0, rows, sub)
    ]
    s_parts = [
        (dict(zh=b, y=a, core=k), start + at)
        for b, a, k, start, rows in s_layout
        for at in range(0, rows, unit)
    ]
    t_pieces, kerns, accs, rects = [], [], [], []
    s_pieces = [None] * len(groups)

    def rectangle(first, last, g0, g1):
        t0, t1 = (sum(rows for _, _, rows in t_layout[:i]) for i in (first, last))
        c0, c1 = (sum(p[4] for group in groups[:g] for p in group) for g in (g0, g1))
        if t0 == t1 or c0 == c1:
            return []
        kern, acc = gram_call(
            flags,
            t_pieces[first:last],
            [p for g in range(g0, g1) for p in s_pieces[g]],
            sub,
            t0,
            c0,
        )
        kerns.append(kern)
        accs.append(acc)
        rects.append((t0, t1, c0, c1))
        return [acc]

    flags = flags_call(layout, m, t_parts, s_parts, sub, pattern)
    zh, zl = fetch(zh_parts[:1], "zh"), fetch(zl_parts[:1], "zl")
    x, y = fetch([units], "x"), fetch([packed], "y")
    own_core = fetch([packed], "core")
    t_pieces += [units] + x + zl
    done = zh + zl + x + y + own_core
    zh_next, zl_next = fetch(zh_parts[1:], "zh", *done), fetch(zl_parts[1:], "zl", *done)
    zh_y, zl_x = fetch(zh, "y", *done), fetch(zl, "x", *done)
    y_core = [fetch([v], "core", *done) for v in y]
    t_pieces += zl_x
    s_pieces[0] = [packed] + own_core + [p for v, w in zip(y, y_core) for p in [v] + w]
    gram = rectangle(0, t_groups[1], 0, 1) + rectangle(t_groups[1], t_groups[2], 0, 1)
    zh_core = fetch(zh, "core", *done, *[p for w in y_core for p in w])
    last = len(t_layout)
    done = zh_next + zl_next + zh_y + zl_x + zh_core + gram
    zh_y_core = fetch(zh_y, "core", *done)
    s_pieces[1] = zh + zh_core + zh_y + zh_y_core
    gram = rectangle(0, t_groups[2], 1, 2)
    if zh_next:
        zh_next_y, zl_next_x = fetch(zh_next, "y", *done), fetch(zl_next, "x", *done)
        zh_next_core = fetch(zh_next, "core", *done)
        t_pieces += zl_next + zl_next_x
        done = zh_next_y + zl_next_x + zh_next_core + zh_y_core + gram
        zh_next_y_core = fetch(zh_next_y, "core", *done)
        s_pieces[2] = zh_next + zh_next_core + zh_next_y + zh_next_y_core
        rectangle(t_groups[2], last, 0, 2)
        rectangle(0, last, 2, 3)
    plan = (m, t_layout, rects)

    def home(values):
        return [
            layout.fetch(v, **{k: -d for k, d in o.items()})
            for v, o in zip(values, t_offsets[1:])
        ]

    def panels(panel):
        far, near = fetch([panel], "zh"), fetch([panel], "y")
        far_y = fetch(far, "y")
        near = [p for v in [panel] + near for p in [v] + fetch([v], "core")]
        return near + far + fetch(far, "core") + far_y + fetch(far_y, "core")

    seeds = s_pieces[0] + s_pieces[-1]
    own, totals, *others = spread_call(kerns, accs, seeds, c, (*plan, seeds_map))
    panel, totals = update(
        first_update_kernel,
        seed_labels,
        own,
        totals,
        home(others),
        [
            jax.ShapeDtypeStruct((m, c), jnp.bfloat16),
            jax.ShapeDtypeStruct((m, BLOCK), jnp.float32),
        ],
    )
    own, *others = spread_call(kerns, [], panels(panel), c, (*plan, p_map))
    return update(
        last_update_kernel,
        seed_labels,
        own,
        totals,
        home(others),
        jax.ShapeDtypeStruct((m, c), jnp.float32),
    )


def solution(mesh):
    return jax.shard_map(
        on_device,
        mesh=mesh,
        in_specs=(P(("col", "row"), None), P(("col", "row"), None), P()),
        out_specs=P(("col", "row"), None),
        check_vma=False,
    )
```

```python
import functools
import math

import jax
import jax.numpy as jnp
from jax import lax
from jax.experimental import pallas as pl
from jax.experimental.pallas import tpu as pltpu
from jax.sharding import PartitionSpec as P

BLOCK = 128
AXES = ("row", "col")

sharpness = 30.0
mixing = 0.8
epsilon = 1e-06


def split_two(n):
    low = max(d for d in range(1, math.isqrt(n) + 1) if n % d == 0)
    return n // low, low


class Layout:
    def __init__(self, rows, cols):
        core = 2 if cols % 2 == 0 else 1
        ny, nx = split_two(rows)
        nzh, nzl = split_two(cols // core)
        self.sizes = dict(y=ny, x=nx, zh=nzh, zl=nzl, core=core)
        self.rows, self.cols = rows, cols

    def coords(self, row, col):
        s = self.sizes
        return dict(
            y=row // s["x"],
            x=row % s["x"],
            zh=col // (s["zl"] * s["core"]),
            zl=col // s["core"] % s["zl"],
            core=col % s["core"],
        )

    def moved(self, at, offset):
        return {k: (at[k] + offset.get(k, 0)) % self.sizes[k] for k in at}

    def row_col(self, at):
        s = self.sizes
        return at["y"] * s["x"] + at["x"], (at["zh"] * s["zl"] + at["zl"]) * s["core"] + at["core"]

    def fetch(self, value, **offset):
        if all(v % self.sizes[k] == 0 for k, v in offset.items()):
            return value
        pairs = []
        for row in range(self.rows):
            for col in range(self.cols):
                r, c = self.row_col(self.moved(self.coords(row, col), offset))
                pairs.append((r * self.cols + c, row * self.cols + col))
        return lax.ppermute(value, AXES, pairs)

    def device(self, offset):
        at = self.coords(lax.axis_index("row"), lax.axis_index("col"))
        row, col = self.row_col(self.moved(at, offset))
        return col * self.rows + row


VMEM = pl.BlockSpec(memory_space=pltpu.VMEM)


def limits(*arrays, mib=3):
    total = sum(max(math.prod(a.shape), 8 * BLOCK) * a.dtype.itemsize for a in arrays)
    return pltpu.CompilerParams(vmem_limit_bytes=total * 5 // 4 + mib * 2**20)


def shape(dims, dtype=jnp.bfloat16):
    return jax.ShapeDtypeStruct(dims, dtype)


def unit_of(values):
    values = values.astype(jnp.float32)
    mean_square = jnp.mean(values * values, axis=1, keepdims=True)
    scaled = values * lax.rsqrt(mean_square + epsilon) * values.shape[1] ** (-0.5)
    return scaled.astype(jnp.bfloat16)


def unit_kernel(emb_ref, seed_ref, unit_ref, packed_ref):
    d = emb_ref.shape[1]
    unit = unit_of(emb_ref[...])
    unit_ref[...] = unit
    packed_ref[:, :d] = unit
    packed_ref[:, d:] = seed_ref[...]


def unit_rows(embeddings, seeds):
    (m, d), c = embeddings.shape, seeds.shape[1]
    outs = [shape((m, d)), shape((m, d + c))]
    return pl.pallas_call(
        unit_kernel,
        out_shape=outs,
        out_specs=[VMEM] * 2,
        compiler_params=limits(embeddings, embeddings, seeds, seeds, *outs, embeddings),
    )(embeddings, seeds)


def stack_kernel(seed_ref, *refs):
    *packed, out_ref = refs
    m, c = seed_ref.shape
    out_ref[:m, :] = seed_ref[...]
    for k, ref in enumerate(packed):
        out_ref[(k + 1) * m : (k + 2) * m, :] = ref[:, ref.shape[1] - c :]


def stack_seeds(seeds, packed):
    m, c = seeds.shape
    out = shape(((len(packed) + 1) * m, c))
    return pl.pallas_call(
        stack_kernel,
        out_shape=out,
        in_specs=[VMEM] * (len(packed) + 1),
        out_specs=VMEM,
        compiler_params=limits(seeds, *packed, out),
    )(seeds, *packed)


def flags_kernel(layout, m, t_parts, s_parts, unit, place_ref, pattern_ref, out_ref, block_ref):
    at = layout.coords(place_ref[0], place_ref[1])

    def block(offset, start):
        row, col = layout.row_col(layout.moved(at, offset))
        return ((col * layout.rows + row) * m + start) // BLOCK

    for k, (offset, start) in enumerate(s_parts):
        block_ref[:, k * unit : (k + 1) * unit] = jnp.full((1, unit), block(offset, start), jnp.int32)
    blocks = block_ref[...]
    for r, (offset, start) in enumerate(t_parts):
        target = block(offset, start)
        hits = blocks == pattern_ref[0, target]
        for k in range(1, pattern_ref.shape[0]):
            hits = hits | (blocks == pattern_ref[k, target])
        out_ref[r : r + 1, :] = jnp.where(hits, 1, 0)


def flags_call(layout, m, t_parts, s_parts, unit, pattern, *earlier):
    place = jnp.stack([lax.axis_index("row"), lax.axis_index("col")]).astype(jnp.int32)
    place = after(place, *earlier)
    out = shape((len(t_parts), len(s_parts) * unit), jnp.int32)
    smem = pl.BlockSpec(memory_space=pltpu.SMEM)
    return pl.pallas_call(
        functools.partial(flags_kernel, layout, m, t_parts, s_parts, unit),
        out_shape=out,
        in_specs=[smem] * 2,
        out_specs=VMEM,
        scratch_shapes=[pltpu.VMEM((1, out.shape[1]), jnp.int32)],
        compiler_params=limits(out, out),
        cost_estimate=pl.CostEstimate(flops=2 * 10**10, bytes_accessed=2**20, transcendentals=0),
    )(place, pattern.T)


def tiles_of(refs, scratch, d):
    tiles, held = [], 0
    for ref in refs:
        rows = ref.shape[0]
        if rows % (2 * BLOCK) == 0:
            tiles += [(ref, k, 2 * BLOCK) for k in range(0, rows, 2 * BLOCK)]
        else:
            scratch[held : held + rows, :] = ref[:, :d]
            held += rows
    k = 0
    while k < held:
        rows = next(w for w in (2 * BLOCK, BLOCK, BLOCK // 2) if held - k >= w)
        tiles.append((scratch, k, rows))
        k += rows
    return tiles


def gram_kernel(nt, ns, sub, d, t_first, s_first, flags, *refs):
    t_in, s_in, refs = refs[:nt], refs[nt : nt + ns], refs[nt + ns :]
    kern, acc, t_join, s_join = refs
    t_tiles, s_tiles = tiles_of(t_in, t_join, d), tiles_of(s_in, s_join, d)
    rows, cols = kern.shape
    col = 0
    for s_ref, s_at, width in s_tiles:
        row = 0
        for t_ref, t_at, tall in t_tiles:
            scores = lax.dot_general(
                t_ref[t_at : t_at + tall, :],
                s_ref[s_at : s_at + width, :d],
                (((1,), (1,)), ((), ())),
                preferred_element_type=jnp.float32,
            )
            value = jnp.exp(sharpness * scores).astype(jnp.bfloat16).astype(jnp.float32)
            for a in range(tall // sub):
                at = row + a * sub
                flag = flags[
                    (t_first + at) // sub : (t_first + at) // sub + 1,
                    s_first + col : s_first + col + width,
                ]
                part = jnp.where(flag > 0, value[a * sub : (a + 1) * sub], 0.0)
                kern[at : at + sub, col : col + width] = part.astype(jnp.bfloat16)
                if width % BLOCK:
                    if col == 0:
                        acc[at : at + sub, :] = jnp.zeros((sub, BLOCK), jnp.float32)
                    acc[at : at + sub, :width] += part
                    continue
                total = part[:, :BLOCK]
                for b in range(1, width // BLOCK):
                    total = total + part[:, b * BLOCK : (b + 1) * BLOCK]
                if col > 0:
                    total = total + acc[at : at + sub, :]
                acc[at : at + sub, :] = total
            row += tall
        col += width


def gram_call(flags, t_pieces, s_pieces, sub, t_first, s_first):
    rows, cols = (sum(p.shape[0] for p in pieces) for pieces in (t_pieces, s_pieces))
    d = t_pieces[0].shape[1]
    join = [
        shape((max(16, sum(p.shape[0] for p in pieces if p.shape[0] % (2 * BLOCK))), d))
        for pieces in (t_pieces, s_pieces)
    ]
    outs = [shape((rows, cols)), shape((rows, BLOCK), jnp.float32)]
    return pl.pallas_call(
        functools.partial(
            gram_kernel, len(t_pieces), len(s_pieces), sub, d, t_first, s_first
        ),
        out_shape=outs,
        in_specs=[VMEM] * (1 + len(t_pieces) + len(s_pieces)),
        out_specs=[VMEM] * 2,
        scratch_shapes=[pltpu.VMEM(j.shape, j.dtype) for j in join],
        compiler_params=limits(flags, *t_pieces, *s_pieces, *outs, *join),
        cost_estimate=pl.CostEstimate(
            flops=2 * rows * cols * d,
            bytes_accessed=2 * (rows + cols) * d,
            transcendentals=rows * cols,
        ),
    )(flags, *t_pieces, *s_pieces)


def spread_kernel(plan, nk, na, ns, *refs):
    m, t_layout, rects, p_map = plan
    kerns, refs = refs[:nk], refs[nk:]
    accs, refs = refs[:na], refs[na:]
    p_in, refs = refs[:ns], refs[ns:]
    outs, pcat = refs[:-1], refs[-1]
    own_ref, other_refs = outs[0], outs[2:] if na else outs[1:]
    c = pcat.shape[1]
    at = 0
    for index, start, rows, lane in p_map:
        pcat[at : at + rows, :] = p_in[index][start : start + rows, lane : lane + c]
        at += rows
    row = 0
    for piece, start, rows in t_layout:
        part = None
        for kern, (t0, t1, c0, c1) in zip(kerns, rects):
            if t0 <= row < t1:
                term = jnp.dot(
                    kern[row - t0 : row - t0 + rows, :],
                    pcat[c0:c1, :],
                    preferred_element_type=jnp.float32,
                )
                part = term if part is None else part + term
        if piece == 0:
            own_ref[start : start + rows, :] = part
        else:
            other_refs[piece - 1][start : start + rows, :] = part.astype(jnp.bfloat16)
        step = math.gcd(rows, BLOCK)
        for lane in range(0, rows if na else 0, step):
            total = None
            for acc, (t0, t1, c0, c1) in zip(accs, rects):
                if t0 <= row < t1:
                    first = row - t0 + lane
                    term = acc[first : first + step, :]
                    total = term if total is None else total + term
            total = jnp.sum(total.T, axis=0, keepdims=True)
            lanes = slice(start + lane, start + lane + step)
            if piece == 0:
                outs[1][:, lanes] = total
            else:
                high = total.astype(jnp.bfloat16).astype(jnp.float32)
                mid = (total - high).astype(jnp.bfloat16).astype(jnp.float32)
                low = total - high - mid
                index = lax.broadcasted_iota(jnp.int32, (16, step), 0)
                terms = jnp.where(index == 0, high, jnp.where(index == 1, mid, low))
                terms = jnp.where(index < 3, terms, 0.0)
                other_refs[piece - 1][m:, lanes] = terms.astype(jnp.bfloat16)
        row += rows


def spread_call(kerns, accs, p_pieces, c, plan):
    m, t_layout, rects, p_map = plan
    nt = 1 + max(piece for piece, _, _ in t_layout)
    cols = sum(rows for _, _, rows, _ in p_map)
    extra = 16 if accs else 0
    outs = [jax.ShapeDtypeStruct((m, c), jnp.float32)]
    if accs:
        outs.append(jax.ShapeDtypeStruct((1, m), jnp.float32))
    outs += [jax.ShapeDtypeStruct((m + extra, c), jnp.bfloat16)] * (nt - 1)
    return pl.pallas_call(
        functools.partial(spread_kernel, plan, len(kerns), len(accs), len(p_pieces)),
        out_shape=outs,
        in_specs=[VMEM] * (len(kerns) + len(accs) + len(p_pieces)),
        out_specs=[VMEM] * len(outs),
        scratch_shapes=[pltpu.VMEM((cols, c), jnp.bfloat16)],
        compiler_params=limits(*kerns, *accs, *p_pieces, *outs, shape((cols, c))),
        cost_estimate=pl.CostEstimate(
            flops=2 * nt * m * cols * c,
            bytes_accessed=2 * (nt * m * cols + cols * c),
            transcendentals=0,
        ),
    )(*kerns, *accs, *p_pieces)


def first_update_kernel(seed_ref, own_ref, own_total_ref, *refs):
    got, (panel_ref, total_ref) = refs[:-2], refs[-2:]
    m = seed_ref.shape[0]
    numerators = own_ref[...]
    for ref in got:
        numerators = numerators + ref[:m, :].astype(jnp.float32)
    totals = own_total_ref[...]
    for ref in got:
        terms = ref[m:, :m].astype(jnp.float32)
        totals = totals + jnp.sum(terms, axis=0, keepdims=True)
    step = min(m, BLOCK)
    for k in range(0, m, step):
        total_ref[k : k + step, :] = jnp.broadcast_to(totals[:, k : k + step], (BLOCK, step)).T
    for k in range(0, seed_ref.shape[1], BLOCK):
        labels = mixing * numerators[:, k : k + BLOCK] / total_ref[...] + (
            1.0 - mixing
        ) * seed_ref[:, k : k + BLOCK].astype(jnp.float32)
        panel_ref[:, k : k + BLOCK] = labels.astype(jnp.bfloat16)


def last_update_kernel(seed_ref, own_ref, total_ref, *refs):
    got, out_ref = refs[:-1], refs[-1]
    numerators = own_ref[...]
    for ref in got:
        numerators = numerators + ref[...].astype(jnp.float32)
    for k in range(0, seed_ref.shape[1], BLOCK):
        out_ref[:, k : k + BLOCK] = mixing * numerators[:, k : k + BLOCK] / total_ref[...] + (
            1.0 - mixing
        ) * seed_ref[:, k : k + BLOCK].astype(jnp.float32)


def update(kernel, seeds, own, totals, got, out_shape):
    return pl.pallas_call(
        kernel,
        out_shape=out_shape,
        in_specs=[VMEM] * (3 + len(got)),
        out_specs=jax.tree.map(lambda _: VMEM, out_shape),
        compiler_params=limits(seeds, own, totals, *got, own, own),
    )(seeds, own, totals, *got)


def after(value, *earlier):
    return lax.optimization_barrier((value, *earlier))[0]


def on_device(embeddings, seed_labels, pattern):
    layout = Layout(lax.axis_size("row"), lax.axis_size("col"))
    size = layout.sizes
    m, c = embeddings.shape[0], seed_labels.shape[1]
    sub = min(m, BLOCK)
    other = {k: range(1, size[k]) for k in size}

    def fetch(values, axis, *earlier):
        return [
            layout.fetch(after(v, *earlier), **{axis: k}) for k in other[axis] for v in values
        ]

    t_offsets = [dict(zl=b, x=a) for b in range(size["zl"]) for a in range(size["x"])]
    near_t = [i for i, o in enumerate(t_offsets) if o["x"] == 0 or o["zl"] == 0]
    t_order = near_t + [i for i in range(len(t_offsets)) if i not in near_t]
    t_layout = [(i, 0, m) for i in t_order]
    both = [0] + list(other["core"])
    groups = [
        [(0, a, k) for a in range(size["y"]) for k in both],
        [(b, 0, k) for k in both for b in other["zh"]],
        [(b, a, 0) for a in other["y"] for b in other["zh"]],
        [(b, a, k) for k in other["core"] for a in other["y"] for b in other["zh"]],
    ]
    s_layout = [dict(zh=b, y=a, core=k) for group in groups for b, a, k in group]
    p_map = [(i, 0, m, 0) for i in range(len(s_layout))]
    seeds_map = []
    for i, o in enumerate(s_layout):
        if o["zh"] == 0:
            seeds_map.append((i, 0, m, embeddings.shape[1]))
        else:
            stack = len(groups[0]) + o["core"] * (size["zh"] - 1) + o["zh"] - 1
            seeds_map.append((stack, o["y"] * m, m, 0))
    t_parts = [(t_offsets[i], k) for i in t_order for k in range(0, m, sub)]
    s_parts = [(o, k) for o in s_layout for k in range(0, m, sub)]
    units, packed = unit_rows(embeddings, seed_labels)

    t_pieces, kerns, accs, rects = [], [], [], []
    s_pieces = [None] * len(groups)

    def rectangle(first, last, g0, g1):
        t0, t1 = first * m, last * m
        c0, c1 = (m * sum(len(group) for group in groups[:g]) for g in (g0, g1))
        if t0 == t1 or c0 == c1:
            return []
        kern, acc = gram_call(
            flags,
            t_pieces[first:last],
            [p for g in range(g0, g1) for p in s_pieces[g]],
            sub,
            t0,
            c0,
        )
        kerns.append(kern)
        accs.append(acc)
        rects.append((t0, t1, c0, c1))
        return [acc]

    zh, zl, x = fetch([units], "zh"), fetch([units], "zl"), fetch([units], "x")
    y, own_core = fetch([packed], "y"), fetch([packed], "core")
    flags = flags_call(layout, m, t_parts, s_parts, sub, pattern, *zh)
    done = zh + zl + x + y + own_core + [flags]
    zh_y, zl_x = fetch(zh, "y", *done), fetch(zl, "x", *done)
    y_core = [fetch([v], "core", *done) for v in y]
    zh_core = fetch(zh, "core", *done)
    seeds_zh = fetch([stack_seeds(seed_labels, y)], "zh", *done)
    by_offset = {(0, 0): units}
    by_offset.update({(0, a): v for a, v in zip(other["x"], x)})
    by_offset.update({(b, 0): v for b, v in zip(other["zl"], zl)})
    by_offset.update({(b, a): v for (a, b), v in zip([(a, b) for a in other["x"] for b in other["zl"]], zl_x)})
    t_pieces += [by_offset[t_offsets[i]["zl"], t_offsets[i]["x"]] for i in t_order]
    s_pieces[0] = [packed] + own_core + [p for v, w in zip(y, y_core) for p in [v] + w]
    s_pieces[1] = zh + zh_core
    s_pieces[2] = zh_y
    early, last = len(near_t), len(t_order)
    gram = rectangle(0, early, 0, 1) + rectangle(0, early, 1, 2)
    done = zh_y + zl_x + zh_core + seeds_zh + gram
    zh_y_core = fetch(zh_y, "core", *done)
    s_pieces[3] = zh_y_core
    seeds_core = fetch(seeds_zh, "core", *done)
    rectangle(early, last, 0, 3)
    rectangle(0, early, 2, 3)
    rectangle(0, last, 3, 4)
    plan = (m, t_layout, rects)

    def home(values):
        return [
            layout.fetch(v, **{k: -d for k, d in o.items()})
            for v, o in zip(values, t_offsets[1:])
        ]

    def panels(panel):
        far, near = fetch([panel], "zh"), fetch([panel], "y")
        far_y = fetch(far, "y")
        near = [p for v in [panel] + near for p in [v] + fetch([v], "core")]
        return near + far + fetch(far, "core") + far_y + fetch(far_y, "core")

    seeds = s_pieces[0] + seeds_zh + seeds_core
    own, totals, *others = spread_call(kerns, accs, seeds, c, (*plan, seeds_map))
    panel, totals = update(
        first_update_kernel,
        seed_labels,
        own,
        totals,
        home(others),
        [
            jax.ShapeDtypeStruct((m, c), jnp.bfloat16),
            jax.ShapeDtypeStruct((m, BLOCK), jnp.float32),
        ],
    )
    own, *others = spread_call(kerns, [], panels(panel), c, (*plan, p_map))
    return update(
        last_update_kernel,
        seed_labels,
        own,
        totals,
        home(others),
        jax.ShapeDtypeStruct((m, c), jnp.float32),
    )


def solution(mesh):
    return jax.shard_map(
        on_device,
        mesh=mesh,
        in_specs=(P(("col", "row"), None), P(("col", "row"), None), P()),
        out_specs=P(("col", "row"), None),
        check_vma=False,
    )
```

```python
import functools
import math

import jax
import jax.numpy as jnp
from jax import lax
from jax.experimental import pallas as pl
from jax.experimental.pallas import tpu as pltpu
from jax.sharding import PartitionSpec as P

BLOCK = 128
AXES = ("row", "col")

sharpness = 30.0
mixing = 0.8
epsilon = 1e-06


def split_two(n):
    low = max(d for d in range(1, math.isqrt(n) + 1) if n % d == 0)
    return n // low, low


class Layout:
    def __init__(self, rows, cols):
        core = 2 if cols % 2 == 0 else 1
        ny, nx = split_two(rows)
        nzh, nzl = split_two(cols // core)
        self.sizes = dict(y=ny, x=nx, zh=nzh, zl=nzl, core=core)
        self.rows, self.cols = rows, cols

    def coords(self, row, col):
        s = self.sizes
        return dict(
            y=row // s["x"],
            x=row % s["x"],
            zh=col // (s["zl"] * s["core"]),
            zl=col // s["core"] % s["zl"],
            core=col % s["core"],
        )

    def moved(self, at, offset):
        return {k: (at[k] + offset.get(k, 0)) % self.sizes[k] for k in at}

    def row_col(self, at):
        s = self.sizes
        return at["y"] * s["x"] + at["x"], (at["zh"] * s["zl"] + at["zl"]) * s["core"] + at["core"]

    def fetch(self, value, **offset):
        if all(v % self.sizes[k] == 0 for k, v in offset.items()):
            return value
        pairs = []
        for row in range(self.rows):
            for col in range(self.cols):
                r, c = self.row_col(self.moved(self.coords(row, col), offset))
                pairs.append((r * self.cols + c, row * self.cols + col))
        return lax.ppermute(value, AXES, pairs)

    def device(self, offset):
        at = self.coords(lax.axis_index("row"), lax.axis_index("col"))
        row, col = self.row_col(self.moved(at, offset))
        return col * self.rows + row


VMEM = pl.BlockSpec(memory_space=pltpu.VMEM)


def limits(*arrays, mib=3):
    total = sum(max(math.prod(a.shape), 8 * BLOCK) * a.dtype.itemsize for a in arrays)
    return pltpu.CompilerParams(vmem_limit_bytes=total * 5 // 4 + mib * 2**20)


def shape(dims, dtype=jnp.bfloat16):
    return jax.ShapeDtypeStruct(dims, dtype)


def unit_of(values):
    values = values.astype(jnp.float32)
    mean_square = jnp.mean(values * values, axis=1, keepdims=True)
    scaled = values * lax.rsqrt(mean_square + epsilon) * values.shape[1] ** (-0.5)
    return scaled.astype(jnp.bfloat16)


def unit_kernel(emb_ref, seed_ref, unit_ref, packed_ref):
    d = emb_ref.shape[1]
    unit = unit_of(emb_ref[...])
    unit_ref[...] = unit
    packed_ref[:, :d] = unit
    packed_ref[:, d:] = seed_ref[...]


def unit_rows(embeddings, seeds):
    (m, d), c = embeddings.shape, seeds.shape[1]
    outs = [shape((m, d)), shape((m, d + c))]
    return pl.pallas_call(
        unit_kernel,
        out_shape=outs,
        out_specs=[VMEM] * 2,
        compiler_params=limits(embeddings, embeddings, seeds, seeds, *outs, embeddings),
    )(embeddings, seeds)


def stack_kernel(seed_ref, *refs):
    *packed, out_ref = refs
    m, c = seed_ref.shape
    out_ref[:m, :] = seed_ref[...]
    for k, ref in enumerate(packed):
        out_ref[(k + 1) * m : (k + 2) * m, :] = ref[:, ref.shape[1] - c :]


def stack_seeds(seeds, packed, work=0):
    m, c = seeds.shape
    out = shape(((len(packed) + 1) * m, c))
    return pl.pallas_call(
        stack_kernel,
        out_shape=out,
        in_specs=[VMEM] * (len(packed) + 1),
        out_specs=VMEM,
        compiler_params=limits(seeds, *packed, out),
        cost_estimate=pl.CostEstimate(flops=work, bytes_accessed=2 * m * c, transcendentals=0),
    )(seeds, *packed)


def flags_kernel(layout, m, t_parts, s_parts, unit, place_ref, pattern_ref, out_ref, block_ref):
    at = layout.coords(place_ref[0], place_ref[1])

    def block(offset, start):
        row, col = layout.row_col(layout.moved(at, offset))
        return ((col * layout.rows + row) * m + start) // BLOCK

    for k, (offset, start) in enumerate(s_parts):
        block_ref[:, k * unit : (k + 1) * unit] = jnp.full((1, unit), block(offset, start), jnp.int32)
    blocks = block_ref[...]
    for r, (offset, start) in enumerate(t_parts):
        target = block(offset, start)
        hits = blocks == pattern_ref[0, target]
        for k in range(1, pattern_ref.shape[0]):
            hits = hits | (blocks == pattern_ref[k, target])
        out_ref[r : r + 1, :] = jnp.where(hits, 1, 0)


def flags_call(layout, m, t_parts, s_parts, unit, pattern, place):
    out = shape((len(t_parts), len(s_parts) * unit), jnp.int32)
    smem = pl.BlockSpec(memory_space=pltpu.SMEM)
    return pl.pallas_call(
        functools.partial(flags_kernel, layout, m, t_parts, s_parts, unit),
        out_shape=out,
        in_specs=[smem] * 2,
        out_specs=VMEM,
        scratch_shapes=[pltpu.VMEM((1, out.shape[1]), jnp.int32)],
        compiler_params=limits(out, out),
        cost_estimate=pl.CostEstimate(flops=2 * 10**10, bytes_accessed=2**20, transcendentals=0),
    )(place, pattern.T)


def tiles_of(refs, scratch, d):
    tiles, held = [], 0
    for ref in refs:
        rows = ref.shape[0]
        if rows % (2 * BLOCK) == 0:
            tiles += [(ref, k, 2 * BLOCK) for k in range(0, rows, 2 * BLOCK)]
        else:
            scratch[held : held + rows, :] = ref[:, :d]
            held += rows
    k = 0
    while k < held:
        rows = next(w for w in (2 * BLOCK, BLOCK, BLOCK // 2) if held - k >= w)
        tiles.append((scratch, k, rows))
        k += rows
    return tiles


def gram_kernel(nt, ns, sub, d, t_first, s_first, flags, *refs):
    t_in, s_in, refs = refs[:nt], refs[nt : nt + ns], refs[nt + ns :]
    kern, acc, t_join, s_join = refs
    t_tiles, s_tiles = tiles_of(t_in, t_join, d), tiles_of(s_in, s_join, d)
    rows, cols = kern.shape
    col = 0
    for s_ref, s_at, width in s_tiles:
        row = 0
        for t_ref, t_at, tall in t_tiles:
            scores = lax.dot_general(
                t_ref[t_at : t_at + tall, :],
                s_ref[s_at : s_at + width, :d],
                (((1,), (1,)), ((), ())),
                preferred_element_type=jnp.float32,
            )
            value = jnp.exp(sharpness * scores).astype(jnp.bfloat16).astype(jnp.float32)
            for a in range(tall // sub):
                at = row + a * sub
                flag = flags[
                    (t_first + at) // sub : (t_first + at) // sub + 1,
                    s_first + col : s_first + col + width,
                ]
                part = jnp.where(flag > 0, value[a * sub : (a + 1) * sub], 0.0)
                kern[at : at + sub, col : col + width] = part.astype(jnp.bfloat16)
                if width % BLOCK:
                    if col == 0:
                        acc[at : at + sub, :] = jnp.zeros((sub, BLOCK), jnp.float32)
                    acc[at : at + sub, :width] += part
                    continue
                total = part[:, :BLOCK]
                for b in range(1, width // BLOCK):
                    total = total + part[:, b * BLOCK : (b + 1) * BLOCK]
                if col > 0:
                    total = total + acc[at : at + sub, :]
                acc[at : at + sub, :] = total
            row += tall
        col += width


def gram_call(flags, t_pieces, s_pieces, sub, t_first, s_first):
    rows, cols = (sum(p.shape[0] for p in pieces) for pieces in (t_pieces, s_pieces))
    d = t_pieces[0].shape[1]
    join = [
        shape((max(16, sum(p.shape[0] for p in pieces if p.shape[0] % (2 * BLOCK))), d))
        for pieces in (t_pieces, s_pieces)
    ]
    outs = [shape((rows, cols)), shape((rows, BLOCK), jnp.float32)]
    return pl.pallas_call(
        functools.partial(
            gram_kernel, len(t_pieces), len(s_pieces), sub, d, t_first, s_first
        ),
        out_shape=outs,
        in_specs=[VMEM] * (1 + len(t_pieces) + len(s_pieces)),
        out_specs=[VMEM] * 2,
        scratch_shapes=[pltpu.VMEM(j.shape, j.dtype) for j in join],
        compiler_params=limits(flags, *t_pieces, *s_pieces, *outs, *join),
        cost_estimate=pl.CostEstimate(
            flops=2 * rows * cols * d,
            bytes_accessed=2 * (rows + cols) * d,
            transcendentals=rows * cols,
        ),
    )(flags, *t_pieces, *s_pieces)


def spread_kernel(plan, nk, na, ns, *refs):
    m, t_layout, rects, p_map = plan
    kerns, refs = refs[:nk], refs[nk:]
    accs, refs = refs[:na], refs[na:]
    p_in, refs = refs[:ns], refs[ns:]
    outs, pcat = refs[:-1], refs[-1]
    own_ref, other_refs = outs[0], outs[2:] if na else outs[1:]
    c = pcat.shape[1]
    at = 0
    for index, start, rows, lane in p_map:
        pcat[at : at + rows, :] = p_in[index][start : start + rows, lane : lane + c]
        at += rows
    row = 0
    for piece, start, rows in t_layout:
        part = None
        for kern, (t0, t1, c0, c1) in zip(kerns, rects):
            if t0 <= row < t1:
                term = jnp.dot(
                    kern[row - t0 : row - t0 + rows, :],
                    pcat[c0:c1, :],
                    preferred_element_type=jnp.float32,
                )
                part = term if part is None else part + term
        if piece == 0:
            own_ref[start : start + rows, :] = part
        else:
            other_refs[piece - 1][start : start + rows, :] = part.astype(jnp.bfloat16)
        step = math.gcd(rows, BLOCK)
        for lane in range(0, rows if na else 0, step):
            total = None
            for acc, (t0, t1, c0, c1) in zip(accs, rects):
                if t0 <= row < t1:
                    first = row - t0 + lane
                    term = acc[first : first + step, :]
                    total = term if total is None else total + term
            total = jnp.sum(total.T, axis=0, keepdims=True)
            lanes = slice(start + lane, start + lane + step)
            if piece == 0:
                outs[1][:, lanes] = total
            else:
                high = total.astype(jnp.bfloat16).astype(jnp.float32)
                mid = (total - high).astype(jnp.bfloat16).astype(jnp.float32)
                low = total - high - mid
                index = lax.broadcasted_iota(jnp.int32, (16, step), 0)
                terms = jnp.where(index == 0, high, jnp.where(index == 1, mid, low))
                terms = jnp.where(index < 3, terms, 0.0)
                other_refs[piece - 1][m:, lanes] = terms.astype(jnp.bfloat16)
        row += rows


def spread_call(kerns, accs, p_pieces, c, plan):
    m, t_layout, rects, p_map = plan
    nt = 1 + max(piece for piece, _, _ in t_layout)
    cols = sum(rows for _, _, rows, _ in p_map)
    extra = 16 if accs else 0
    outs = [jax.ShapeDtypeStruct((m, c), jnp.float32)]
    if accs:
        outs.append(jax.ShapeDtypeStruct((1, m), jnp.float32))
    outs += [jax.ShapeDtypeStruct((m + extra, c), jnp.bfloat16)] * (nt - 1)
    return pl.pallas_call(
        functools.partial(spread_kernel, plan, len(kerns), len(accs), len(p_pieces)),
        out_shape=outs,
        in_specs=[VMEM] * (len(kerns) + len(accs) + len(p_pieces)),
        out_specs=[VMEM] * len(outs),
        scratch_shapes=[pltpu.VMEM((cols, c), jnp.bfloat16)],
        compiler_params=limits(*kerns, *accs, *p_pieces, *outs, shape((cols, c))),
        cost_estimate=pl.CostEstimate(
            flops=2 * nt * m * cols * c,
            bytes_accessed=2 * (nt * m * cols + cols * c),
            transcendentals=0,
        ),
    )(*kerns, *accs, *p_pieces)


def first_update_kernel(seed_ref, own_ref, own_total_ref, *refs):
    got, (panel_ref, total_ref) = refs[:-2], refs[-2:]
    m = seed_ref.shape[0]
    numerators = own_ref[...]
    for ref in got:
        numerators = numerators + ref[:m, :].astype(jnp.float32)
    totals = own_total_ref[...]
    for ref in got:
        terms = ref[m:, :m].astype(jnp.float32)
        totals = totals + jnp.sum(terms, axis=0, keepdims=True)
    step = min(m, BLOCK)
    for k in range(0, m, step):
        total_ref[k : k + step, :] = jnp.broadcast_to(totals[:, k : k + step], (BLOCK, step)).T
    for k in range(0, seed_ref.shape[1], BLOCK):
        labels = mixing * numerators[:, k : k + BLOCK] / total_ref[...] + (
            1.0 - mixing
        ) * seed_ref[:, k : k + BLOCK].astype(jnp.float32)
        panel_ref[:, k : k + BLOCK] = labels.astype(jnp.bfloat16)


def last_update_kernel(seed_ref, own_ref, total_ref, *refs):
    got, out_ref = refs[:-1], refs[-1]
    numerators = own_ref[...]
    for ref in got:
        numerators = numerators + ref[...].astype(jnp.float32)
    for k in range(0, seed_ref.shape[1], BLOCK):
        out_ref[:, k : k + BLOCK] = mixing * numerators[:, k : k + BLOCK] / total_ref[...] + (
            1.0 - mixing
        ) * seed_ref[:, k : k + BLOCK].astype(jnp.float32)


def update(kernel, seeds, own, totals, got, out_shape):
    return pl.pallas_call(
        kernel,
        out_shape=out_shape,
        in_specs=[VMEM] * (3 + len(got)),
        out_specs=jax.tree.map(lambda _: VMEM, out_shape),
        compiler_params=limits(seeds, own, totals, *got, own, own),
    )(seeds, own, totals, *got)


def after(value, *earlier):
    return lax.optimization_barrier((value, *earlier))[0]


def on_device(embeddings, seed_labels, pattern):
    layout = Layout(lax.axis_size("row"), lax.axis_size("col"))
    size = layout.sizes
    m, c = embeddings.shape[0], seed_labels.shape[1]
    sub = min(m, BLOCK)
    other = {k: range(1, size[k]) for k in size}

    def fetch(values, axis, *earlier):
        return [
            layout.fetch(after(v, *earlier), **{axis: k}) for k in other[axis] for v in values
        ]

    t_offsets = [dict(zl=b, x=a) for b in range(size["zl"]) for a in range(size["x"])]
    near_t = [i for i, o in enumerate(t_offsets) if o["x"] == 0 or o["zl"] == 0]
    t_order = near_t + [i for i in range(len(t_offsets)) if i not in near_t]
    t_layout = [(i, 0, m) for i in t_order]
    both = [0] + list(other["core"])
    groups = [
        [(0, a, k) for a in range(size["y"]) for k in both],
        [(b, 0, k) for k in both for b in other["zh"]],
        [(b, a, 0) for a in other["y"] for b in other["zh"]],
        [(b, a, k) for k in other["core"] for a in other["y"] for b in other["zh"]],
    ]
    s_layout = [dict(zh=b, y=a, core=k) for group in groups for b, a, k in group]
    p_map = [(i, 0, m, 0) for i in range(len(s_layout))]
    seeds_map = []
    for i, o in enumerate(s_layout):
        if o["zh"] == 0:
            seeds_map.append((i, 0, m, embeddings.shape[1]))
        else:
            stack = len(groups[0]) + o["core"] * (size["zh"] - 1) + o["zh"] - 1
            seeds_map.append((stack, o["y"] * m, m, 0))
    t_parts = [(t_offsets[i], k) for i in t_order for k in range(0, m, sub)]
    s_parts = [(o, k) for o in s_layout for k in range(0, m, sub)]
    place = jnp.stack([lax.axis_index("row"), lax.axis_index("col")]).astype(jnp.int32)
    units, packed = unit_rows(after(embeddings, place), seed_labels)

    t_pieces, kerns, accs, rects = [], [], [], []
    s_pieces = [None] * len(groups)

    def rectangle(first, last, g0, g1):
        t0, t1 = first * m, last * m
        c0, c1 = (m * sum(len(group) for group in groups[:g]) for g in (g0, g1))
        if t0 == t1 or c0 == c1:
            return []
        kern, acc = gram_call(
            flags,
            t_pieces[first:last],
            [p for g in range(g0, g1) for p in s_pieces[g]],
            sub,
            t0,
            c0,
        )
        kerns.append(kern)
        accs.append(acc)
        rects.append((t0, t1, c0, c1))
        return [acc]

    zh, zl, x = fetch([units], "zh"), fetch([units], "zl"), fetch([units], "x")
    y, own_core = fetch([packed], "y"), fetch([packed], "core")
    flags = flags_call(layout, m, t_parts, s_parts, sub, pattern, after(place, *zh))
    done = zh + zl + x + y + own_core + [flags]
    zh_y, zl_x = fetch(zh, "y", *done), fetch(zl, "x", *done)
    y_core = [fetch([v], "core", *done) for v in y]
    zh_core = fetch(zh, "core", *done)
    seeds_zh = fetch([stack_seeds(seed_labels, y)], "zh", *done)
    by_offset = {(0, 0): units}
    by_offset.update({(0, a): v for a, v in zip(other["x"], x)})
    by_offset.update({(b, 0): v for b, v in zip(other["zl"], zl)})
    by_offset.update({(b, a): v for (a, b), v in zip([(a, b) for a in other["x"] for b in other["zl"]], zl_x)})
    t_pieces += [by_offset[t_offsets[i]["zl"], t_offsets[i]["x"]] for i in t_order]
    s_pieces[0] = [packed] + own_core + [p for v, w in zip(y, y_core) for p in [v] + w]
    s_pieces[1] = zh + zh_core
    s_pieces[2] = zh_y
    early, last = len(near_t), len(t_order)
    gram = rectangle(0, early, 0, 1) + rectangle(0, early, 1, 2)
    seeds_zh = [stack_seeds(after(v, *gram), [], 2 * 10**10) for v in seeds_zh]
    done = zh_y + zl_x + zh_core + gram + seeds_zh
    zh_y_core = fetch(zh_y, "core", *done)
    s_pieces[3] = zh_y_core
    seeds_core = fetch(seeds_zh, "core", *done)
    rectangle(early, last, 0, 3)
    rectangle(0, early, 2, 3)
    rectangle(0, last, 3, 4)
    plan = (m, t_layout, rects)

    def home(values):
        return [
            layout.fetch(v, **{k: -d for k, d in o.items()})
            for v, o in zip(values, t_offsets[1:])
        ]

    def panels(panel):
        far, near = fetch([panel], "zh"), fetch([panel], "y")
        far_y = fetch(far, "y")
        near = [p for v in [panel] + near for p in [v] + fetch([v], "core")]
        return near + far + fetch(far, "core") + far_y + fetch(far_y, "core")

    seeds = s_pieces[0] + seeds_zh + seeds_core
    own, totals, *others = spread_call(kerns, accs, seeds, c, (*plan, seeds_map))
    panel, totals = update(
        first_update_kernel,
        seed_labels,
        own,
        totals,
        home(others),
        [
            jax.ShapeDtypeStruct((m, c), jnp.bfloat16),
            jax.ShapeDtypeStruct((m, BLOCK), jnp.float32),
        ],
    )
    own, *others = spread_call(kerns, [], panels(panel), c, (*plan, p_map))
    return update(
        last_update_kernel,
        seed_labels,
        own,
        totals,
        home(others),
        jax.ShapeDtypeStruct((m, c), jnp.float32),
    )


def solution(mesh):
    return jax.shard_map(
        on_device,
        mesh=mesh,
        in_specs=(P(("col", "row"), None), P(("col", "row"), None), P()),
        out_specs=P(("col", "row"), None),
        check_vma=False,
    )
```

```python
import functools
import math

import jax
import jax.numpy as jnp
from jax import lax
from jax.experimental import pallas as pl
from jax.experimental.pallas import tpu as pltpu
from jax.sharding import PartitionSpec as P

BLOCK = 128
AXES = ("row", "col")

sharpness = 30.0
mixing = 0.8
epsilon = 1e-06


def split_two(n):
    low = max(d for d in range(1, math.isqrt(n) + 1) if n % d == 0)
    return n // low, low


class Layout:
    def __init__(self, rows, cols):
        core = 2 if cols % 2 == 0 else 1
        ny, nx = split_two(rows)
        nzh, nzl = split_two(cols // core)
        self.sizes = dict(y=ny, x=nx, zh=nzh, zl=nzl, core=core)
        self.rows, self.cols = rows, cols

    def coords(self, row, col):
        s = self.sizes
        return dict(
            y=row // s["x"],
            x=row % s["x"],
            zh=col // (s["zl"] * s["core"]),
            zl=col // s["core"] % s["zl"],
            core=col % s["core"],
        )

    def moved(self, at, offset):
        return {k: (at[k] + offset.get(k, 0)) % self.sizes[k] for k in at}

    def row_col(self, at):
        s = self.sizes
        return at["y"] * s["x"] + at["x"], (at["zh"] * s["zl"] + at["zl"]) * s["core"] + at["core"]

    def fetch(self, value, **offset):
        if all(v % self.sizes[k] == 0 for k, v in offset.items()):
            return value
        pairs = []
        for row in range(self.rows):
            for col in range(self.cols):
                r, c = self.row_col(self.moved(self.coords(row, col), offset))
                pairs.append((r * self.cols + c, row * self.cols + col))
        return lax.ppermute(value, AXES, pairs)

    def device(self, offset):
        at = self.coords(lax.axis_index("row"), lax.axis_index("col"))
        row, col = self.row_col(self.moved(at, offset))
        return col * self.rows + row


VMEM = pl.BlockSpec(memory_space=pltpu.VMEM)


def limits(*arrays, mib=3):
    total = sum(max(math.prod(a.shape), 8 * BLOCK) * a.dtype.itemsize for a in arrays)
    return pltpu.CompilerParams(vmem_limit_bytes=total * 5 // 4 + mib * 2**20)


def shape(dims, dtype=jnp.bfloat16):
    return jax.ShapeDtypeStruct(dims, dtype)


def unit_of(values):
    values = values.astype(jnp.float32)
    mean_square = jnp.mean(values * values, axis=1, keepdims=True)
    scaled = values * lax.rsqrt(mean_square + epsilon) * values.shape[1] ** (-0.5)
    return scaled.astype(jnp.bfloat16)


def unit_kernel(chunks, emb_ref, seed_ref, unit_ref, packed_ref, *outs):
    d = emb_ref.shape[1]
    unit = unit_of(emb_ref[...])
    unit_ref[...] = unit
    packed_ref[:, :d] = unit
    packed_ref[:, d:] = seed_ref[...]
    for out, (start, rows) in zip(outs, chunks):
        out[:, :d] = unit_ref[start : start + rows, :]
        for k in range((out.shape[1] - d) // seed_ref.shape[1]):
            at = d + k * seed_ref.shape[1]
            out[:, at : at + seed_ref.shape[1]] = seed_ref[k * rows : (k + 1) * rows, :]


def unit_rows(embeddings, seeds, chunks, carrier):
    (m, d), c = embeddings.shape, seeds.shape[1]
    outs = [shape((m, d)), shape((m, d + c))]
    outs += [
        shape((rows, d + m // rows * c if i == carrier else d)) for i, (_, rows) in enumerate(chunks)
    ]
    units, packed, *parts = pl.pallas_call(
        functools.partial(unit_kernel, chunks),
        out_shape=outs,
        out_specs=[VMEM] * len(outs),
        compiler_params=limits(*[embeddings, seeds] * 2, *outs, embeddings),
    )(embeddings, seeds)
    return units, packed, parts


def copy_kernel(in_ref, out_ref):
    out_ref[...] = in_ref[...]


def copied(value, work):
    return pl.pallas_call(
        copy_kernel,
        out_shape=shape(value.shape, value.dtype),
        in_specs=[VMEM],
        out_specs=VMEM,
        compiler_params=limits(value, value),
        cost_estimate=pl.CostEstimate(
            flops=work, bytes_accessed=4 * value.size, transcendentals=0
        ),
    )(value)


def flags_kernel(layout, m, t_parts, s_parts, unit, place_ref, pattern_ref, out_ref, block_ref):
    at = layout.coords(place_ref[0], place_ref[1])

    def block(offset, start):
        row, col = layout.row_col(layout.moved(at, offset))
        return ((col * layout.rows + row) * m + start) // BLOCK

    for k, (offset, start) in enumerate(s_parts):
        block_ref[:, k * unit : (k + 1) * unit] = jnp.full((1, unit), block(offset, start), jnp.int32)
    blocks = block_ref[...]
    for r, (offset, start) in enumerate(t_parts):
        target = block(offset, start)
        hits = blocks == pattern_ref[0, target]
        for k in range(1, pattern_ref.shape[0]):
            hits = hits | (blocks == pattern_ref[k, target])
        out_ref[r : r + 1, :] = jnp.where(hits, 1, 0)


def flags_call(layout, m, t_parts, s_parts, unit, pattern, place):
    out = shape((len(t_parts), len(s_parts) * unit), jnp.int32)
    smem = pl.BlockSpec(memory_space=pltpu.SMEM)
    return pl.pallas_call(
        functools.partial(flags_kernel, layout, m, t_parts, s_parts, unit),
        out_shape=out,
        in_specs=[smem] * 2,
        out_specs=VMEM,
        scratch_shapes=[pltpu.VMEM((1, out.shape[1]), jnp.int32)],
        compiler_params=limits(out, out),
    )(place, pattern.T)


def tiles_of(refs, scratch, d):
    tiles, held = [], 0
    for ref in refs:
        rows = ref.shape[0]
        if rows % (2 * BLOCK) == 0:
            tiles += [(ref, k, 2 * BLOCK) for k in range(0, rows, 2 * BLOCK)]
        else:
            scratch[held : held + rows, :] = ref[:, :d]
            held += rows
    k = 0
    while k < held:
        rows = next(w for w in (2 * BLOCK, BLOCK, BLOCK // 2) if held - k >= w)
        tiles.append((scratch, k, rows))
        k += rows
    return tiles


def gram_kernel(nt, ns, sub, d, t_first, s_first, flags, *refs):
    t_in, s_in, refs = refs[:nt], refs[nt : nt + ns], refs[nt + ns :]
    kern, acc, t_join, s_join = refs
    t_tiles, s_tiles = tiles_of(t_in, t_join, d), tiles_of(s_in, s_join, d)
    rows, cols = kern.shape
    col = 0
    for s_ref, s_at, width in s_tiles:
        row = 0
        for t_ref, t_at, tall in t_tiles:
            scores = lax.dot_general(
                t_ref[t_at : t_at + tall, :],
                s_ref[s_at : s_at + width, :d],
                (((1,), (1,)), ((), ())),
                preferred_element_type=jnp.float32,
            )
            value = jnp.exp(sharpness * scores).astype(jnp.bfloat16).astype(jnp.float32)
            for a in range(tall // sub):
                at = row + a * sub
                flag = flags[
                    (t_first + at) // sub : (t_first + at) // sub + 1,
                    s_first + col : s_first + col + width,
                ]
                part = jnp.where(flag > 0, value[a * sub : (a + 1) * sub], 0.0)
                kern[at : at + sub, col : col + width] = part.astype(jnp.bfloat16)
                if width % BLOCK:
                    if col == 0:
                        acc[at : at + sub, :] = jnp.zeros((sub, BLOCK), jnp.float32)
                    acc[at : at + sub, :width] += part
                    continue
                total = part[:, :BLOCK]
                for b in range(1, width // BLOCK):
                    total = total + part[:, b * BLOCK : (b + 1) * BLOCK]
                if col > 0:
                    total = total + acc[at : at + sub, :]
                acc[at : at + sub, :] = total
            row += tall
        col += width


def gram_call(flags, t_pieces, s_pieces, sub, t_first, s_first):
    rows, cols = (sum(p.shape[0] for p in pieces) for pieces in (t_pieces, s_pieces))
    d = t_pieces[0].shape[1]
    join = [
        shape((max(16, sum(p.shape[0] for p in pieces if p.shape[0] % (2 * BLOCK))), d))
        for pieces in (t_pieces, s_pieces)
    ]
    outs = [shape((rows, cols)), shape((rows, BLOCK), jnp.float32)]
    return pl.pallas_call(
        functools.partial(
            gram_kernel, len(t_pieces), len(s_pieces), sub, d, t_first, s_first
        ),
        out_shape=outs,
        in_specs=[VMEM] * (1 + len(t_pieces) + len(s_pieces)),
        out_specs=[VMEM] * 2,
        scratch_shapes=[pltpu.VMEM(j.shape, j.dtype) for j in join],
        compiler_params=limits(flags, *t_pieces, *s_pieces, *outs, *join),
        cost_estimate=pl.CostEstimate(
            flops=2 * rows * cols * d,
            bytes_accessed=2 * (rows + cols) * d,
            transcendentals=rows * cols,
        ),
    )(flags, *t_pieces, *s_pieces)


def spread_kernel(plan, nk, na, ns, *refs):
    m, t_layout, rects, p_map = plan
    kerns, refs = refs[:nk], refs[nk:]
    accs, refs = refs[:na], refs[na:]
    p_in, refs = refs[:ns], refs[ns:]
    outs, pcat = refs[:-1], refs[-1]
    own_ref, other_refs = outs[0], outs[2:] if na else outs[1:]
    c = pcat.shape[1]
    at = 0
    for index, start, rows, lane in p_map:
        pcat[at : at + rows, :] = p_in[index][start : start + rows, lane : lane + c]
        at += rows
    row = 0
    for piece, start, rows in t_layout:
        part = None
        for kern, (t0, t1, c0, c1) in zip(kerns, rects):
            if t0 <= row < t1:
                term = jnp.dot(
                    kern[row - t0 : row - t0 + rows, :],
                    pcat[c0:c1, :],
                    preferred_element_type=jnp.float32,
                )
                part = term if part is None else part + term
        if piece == 0:
            own_ref[start : start + rows, :] = part
        else:
            other_refs[piece - 1][start : start + rows, :] = part.astype(jnp.bfloat16)
        step = math.gcd(rows, BLOCK)
        for lane in range(0, rows if na else 0, step):
            total = None
            for acc, (t0, t1, c0, c1) in zip(accs, rects):
                if t0 <= row < t1:
                    first = row - t0 + lane
                    term = acc[first : first + step, :]
                    total = term if total is None else total + term
            total = jnp.sum(total.T, axis=0, keepdims=True)
            lanes = slice(start + lane, start + lane + step)
            if piece == 0:
                outs[1][:, lanes] = total
            else:
                high = total.astype(jnp.bfloat16).astype(jnp.float32)
                mid = (total - high).astype(jnp.bfloat16).astype(jnp.float32)
                low = total - high - mid
                index = lax.broadcasted_iota(jnp.int32, (16, step), 0)
                terms = jnp.where(index == 0, high, jnp.where(index == 1, mid, low))
                terms = jnp.where(index < 3, terms, 0.0)
                other_refs[piece - 1][m:, lanes] = terms.astype(jnp.bfloat16)
        row += rows


def spread_call(kerns, accs, p_pieces, c, plan):
    m, t_layout, rects, p_map = plan
    nt = 1 + max(piece for piece, _, _ in t_layout)
    cols = sum(rows for _, _, rows, _ in p_map)
    extra = 16 if accs else 0
    outs = [jax.ShapeDtypeStruct((m, c), jnp.float32)]
    if accs:
        outs.append(jax.ShapeDtypeStruct((1, m), jnp.float32))
    outs += [jax.ShapeDtypeStruct((m + extra, c), jnp.bfloat16)] * (nt - 1)
    return pl.pallas_call(
        functools.partial(spread_kernel, plan, len(kerns), len(accs), len(p_pieces)),
        out_shape=outs,
        in_specs=[VMEM] * (len(kerns) + len(accs) + len(p_pieces)),
        out_specs=[VMEM] * len(outs),
        scratch_shapes=[pltpu.VMEM((cols, c), jnp.bfloat16)],
        compiler_params=limits(*kerns, *accs, *p_pieces, *outs, shape((cols, c))),
        cost_estimate=pl.CostEstimate(
            flops=2 * nt * m * cols * c,
            bytes_accessed=2 * (nt * m * cols + cols * c),
            transcendentals=0,
        ),
    )(*kerns, *accs, *p_pieces)


def first_update_kernel(seed_ref, own_ref, own_total_ref, *refs):
    got, (panel_ref, total_ref) = refs[:-2], refs[-2:]
    m = seed_ref.shape[0]
    numerators = own_ref[...]
    for ref in got:
        numerators = numerators + ref[:m, :].astype(jnp.float32)
    totals = own_total_ref[...]
    for ref in got:
        terms = ref[m:, :m].astype(jnp.float32)
        totals = totals + jnp.sum(terms, axis=0, keepdims=True)
    step = min(m, BLOCK)
    for k in range(0, m, step):
        total_ref[k : k + step, :] = jnp.broadcast_to(totals[:, k : k + step], (BLOCK, step)).T
    for k in range(0, seed_ref.shape[1], BLOCK):
        labels = mixing * numerators[:, k : k + BLOCK] / total_ref[...] + (
            1.0 - mixing
        ) * seed_ref[:, k : k + BLOCK].astype(jnp.float32)
        panel_ref[:, k : k + BLOCK] = labels.astype(jnp.bfloat16)


def last_update_kernel(seed_ref, own_ref, total_ref, *refs):
    got, out_ref = refs[:-1], refs[-1]
    numerators = own_ref[...]
    for ref in got:
        numerators = numerators + ref[...].astype(jnp.float32)
    for k in range(0, seed_ref.shape[1], BLOCK):
        out_ref[:, k : k + BLOCK] = mixing * numerators[:, k : k + BLOCK] / total_ref[...] + (
            1.0 - mixing
        ) * seed_ref[:, k : k + BLOCK].astype(jnp.float32)


def update(kernel, seeds, own, totals, got, out_shape):
    return pl.pallas_call(
        kernel,
        out_shape=out_shape,
        in_specs=[VMEM] * (3 + len(got)),
        out_specs=jax.tree.map(lambda _: VMEM, out_shape),
        compiler_params=limits(seeds, own, totals, *got, own, own),
    )(seeds, own, totals, *got)


def after(value, *earlier):
    return lax.optimization_barrier((value, *earlier))[0]


def on_device(embeddings, seed_labels, pattern):
    layout = Layout(lax.axis_size("row"), lax.axis_size("col"))
    size = layout.sizes
    m, c = embeddings.shape[0], seed_labels.shape[1]
    zh_chunks = zl_chunks = [(0, m)]
    sub = min(m, BLOCK)
    if m % (2 * BLOCK) == 0:
        zh_chunks = [(0, 3 * m // 4), (3 * m // 4, m // 4)]
        zl_chunks = [(0, m // 2), (m // 2, m // 2)]
        sub = math.gcd(BLOCK, m // 4)
    other = {k: range(1, size[k]) for k in size}

    def fetch(values, axis, *earlier):
        return [
            layout.fetch(after(v, *earlier), **{axis: k}) for k in other[axis] for v in values
        ]

    place = jnp.stack([lax.axis_index("row"), lax.axis_index("col")]).astype(jnp.int32)
    units, packed, parts = unit_rows(
        after(embeddings, place), seed_labels, zh_chunks + zl_chunks, len(zh_chunks) - 1
    )
    zh_parts, zl_parts = parts[: len(zh_chunks)], parts[len(zh_chunks) :]

    t_index = {(b, a): b * size["x"] + a for b in range(size["zl"]) for a in range(size["x"])}
    t_layout = [(t_index[0, a], 0, m) for a in range(size["x"])]
    t_groups = [len(t_layout)]
    for start, rows in zl_chunks:
        t_layout += [(t_index[b, 0], start, rows) for b in other["zl"]]
        t_groups.append(len(t_layout))
        t_layout += [(t_index[b, a], start, rows) for a in other["x"] for b in other["zl"]]
        t_groups.append(len(t_layout))
    both = [0] + list(other["core"])
    groups = [[(0, a, k, 0, m) for a in range(size["y"]) for k in both]]
    for start, rows in zh_chunks:
        group = [(b, 0, k, start, rows) for k in both for b in other["zh"]]
        group += [(b, a, k, start, rows) for k in both for a in other["y"] for b in other["zh"]]
        groups.append(group)
    s_layout = [piece for group in groups for piece in group]
    whole = [(0, a, k) for a in range(size["y"]) for k in both]
    whole += [(b, 0, k) for k in both for b in other["zh"]]
    whole += [(b, a, k) for k in both for a in other["y"] for b in other["zh"]]
    d, tail = embeddings.shape[1], zh_chunks[-1][1]
    p_map = [(whole.index(piece[:3]), *piece[3:], 0) for piece in s_layout]
    seeds_map = []
    for piece in s_layout:
        index, (start, rows) = whole.index(piece[:3]), piece[3:]
        if index < len(groups[0]):
            seeds_map.append((index, start, rows, d))
        else:
            blocks = range(start // tail, (start + rows) // tail)
            seeds_map += [(index, 0, tail, d + k * c) for k in blocks]

    t_offsets = [dict(zl=b, x=a) for b, a in t_index]
    unit = sub
    t_parts = [
        (t_offsets[i], start + k) for i, start, rows in t_layout for k in range(0, rows, sub)
    ]
    s_parts = [
        (dict(zh=b, y=a, core=k), start + at)
        for b, a, k, start, rows in s_layout
        for at in range(0, rows, unit)
    ]
    t_pieces, kerns, accs, rects = [], [], [], []
    s_pieces = [None] * len(groups)

    def rectangle(first, last, g0, g1):
        t0, t1 = (sum(rows for _, _, rows in t_layout[:i]) for i in (first, last))
        c0, c1 = (sum(p[4] for group in groups[:g] for p in group) for g in (g0, g1))
        if t0 == t1 or c0 == c1:
            return []
        kern, acc = gram_call(
            flags,
            t_pieces[first:last],
            [p for g in range(g0, g1) for p in s_pieces[g]],
            sub,
            t0,
            c0,
        )
        kerns.append(kern)
        accs.append(acc)
        rects.append((t0, t1, c0, c1))
        return [acc]

    flags = flags_call(layout, m, t_parts, s_parts, sub, pattern, place)
    zh, zl = fetch(zh_parts[:1], "zh"), fetch(zl_parts[:1], "zl")
    x, y = fetch([units], "x"), fetch([packed], "y")
    own_core = fetch([packed], "core")
    t_pieces += [units] + x + zl
    seeds = copied(after(seed_labels, *zh), 2 * 10**10)
    done = zh + zl + x + y + own_core + [seeds]
    zh_next, zl_next = fetch(zh_parts[1:], "zh", *done), fetch(zl_parts[1:], "zl", *done)
    zh_y, zl_x = fetch(zh, "y", *done), fetch(zl, "x", *done)
    y_core = [fetch([v], "core", *done) for v in y]
    t_pieces += zl_x
    s_pieces[0] = [packed] + own_core + [p for v, w in zip(y, y_core) for p in [v] + w]
    gram = rectangle(0, t_groups[1], 0, 1) + rectangle(t_groups[1], t_groups[2], 0, 1)
    zh_core = fetch(zh, "core", *done, *[p for w in y_core for p in w])
    last = len(t_layout)
    zh_next = [copied(after(v, *gram), 2 * 10**10) for v in zh_next]
    done = zh_next + zl_next + zh_y + zl_x + zh_core + gram
    zh_y_core = fetch(zh_y, "core", *done)
    s_pieces[1] = zh + zh_core + zh_y + zh_y_core
    gram = rectangle(0, t_groups[2], 1, 2)
    if zh_next:
        zh_next_y, zl_next_x = fetch(zh_next, "y", *done), fetch(zl_next, "x", *done)
        zh_next_core = fetch(zh_next, "core", *done)
        t_pieces += zl_next + zl_next_x
        done = zh_next_y + zl_next_x + zh_next_core + zh_y_core + gram
        zh_next_y_core = fetch(zh_next_y, "core", *done)
        s_pieces[2] = zh_next + zh_next_core + zh_next_y + zh_next_y_core
        rectangle(t_groups[2], last, 0, 2)
        rectangle(0, last, 2, 3)
    plan = (m, t_layout, rects)

    def home(values):
        return [
            layout.fetch(v, **{k: -d for k, d in o.items()})
            for v, o in zip(values, t_offsets[1:])
        ]

    def panels(panel):
        far, near = fetch([panel], "zh"), fetch([panel], "y")
        far_y = fetch(far, "y")
        near = [p for v in [panel] + near for p in [v] + fetch([v], "core")]
        return near + far + fetch(far, "core") + far_y + fetch(far_y, "core")

    panels_in = s_pieces[0] + s_pieces[-1]
    own, totals, *others = spread_call(kerns, accs, panels_in, c, (*plan, seeds_map))
    panel, totals = update(
        first_update_kernel,
        seeds,
        own,
        totals,
        home(others),
        [
            jax.ShapeDtypeStruct((m, c), jnp.bfloat16),
            jax.ShapeDtypeStruct((m, BLOCK), jnp.float32),
        ],
    )
    own, *others = spread_call(kerns, [], panels(panel), c, (*plan, p_map))
    return update(
        last_update_kernel,
        seeds,
        own,
        totals,
        home(others),
        jax.ShapeDtypeStruct((m, c), jnp.float32),
    )


def solution(mesh):
    return jax.shard_map(
        on_device,
        mesh=mesh,
        in_specs=(P(("col", "row"), None), P(("col", "row"), None), P()),
        out_specs=P(("col", "row"), None),
        check_vma=False,
    )
```

```python
import functools
import math

import jax
import jax.numpy as jnp
from jax import lax
from jax.experimental import pallas as pl
from jax.experimental.pallas import tpu as pltpu
from jax.sharding import PartitionSpec as P

BLOCK = 128
AXES = ("row", "col")

sharpness = 30.0
mixing = 0.8
epsilon = 1e-06


def split_two(n):
    low = max(d for d in range(1, math.isqrt(n) + 1) if n % d == 0)
    return n // low, low


class Layout:
    def __init__(self, rows, cols):
        core = 2 if cols % 2 == 0 else 1
        ny, nx = split_two(rows)
        nzh, nzl = split_two(cols // core)
        self.sizes = dict(y=ny, x=nx, zh=nzh, zl=nzl, core=core)
        self.rows, self.cols = rows, cols

    def coords(self, row, col):
        s = self.sizes
        return dict(
            y=row // s["x"],
            x=row % s["x"],
            zh=col // (s["zl"] * s["core"]),
            zl=col // s["core"] % s["zl"],
            core=col % s["core"],
        )

    def moved(self, at, offset):
        return {k: (at[k] + offset.get(k, 0)) % self.sizes[k] for k in at}

    def row_col(self, at):
        s = self.sizes
        return at["y"] * s["x"] + at["x"], (at["zh"] * s["zl"] + at["zl"]) * s["core"] + at["core"]

    def fetch(self, value, **offset):
        if all(v % self.sizes[k] == 0 for k, v in offset.items()):
            return value
        pairs = []
        for row in range(self.rows):
            for col in range(self.cols):
                r, c = self.row_col(self.moved(self.coords(row, col), offset))
                pairs.append((r * self.cols + c, row * self.cols + col))
        return lax.ppermute(value, AXES, pairs)

    def device(self, offset):
        at = self.coords(lax.axis_index("row"), lax.axis_index("col"))
        row, col = self.row_col(self.moved(at, offset))
        return col * self.rows + row


VMEM = pl.BlockSpec(memory_space=pltpu.VMEM)


def limits(*arrays, mib=3):
    total = sum(max(math.prod(a.shape), 8 * BLOCK) * a.dtype.itemsize for a in arrays)
    return pltpu.CompilerParams(vmem_limit_bytes=total * 5 // 4 + mib * 2**20)


def shape(dims, dtype=jnp.bfloat16):
    return jax.ShapeDtypeStruct(dims, dtype)


def unit_of(values):
    values = values.astype(jnp.float32)
    mean_square = jnp.mean(values * values, axis=1, keepdims=True)
    scaled = values * lax.rsqrt(mean_square + epsilon) * values.shape[1] ** (-0.5)
    return scaled.astype(jnp.bfloat16)


def unit_kernel(emb_ref, unit_ref):
    unit_ref[...] = unit_of(emb_ref[...])


def unit_rows(embeddings):
    out = shape(embeddings.shape)
    return pl.pallas_call(
        unit_kernel,
        out_shape=out,
        in_specs=[VMEM],
        out_specs=VMEM,
        compiler_params=limits(*[out] * 4),
    )(embeddings)


def pack_kernel(unit_ref, seed_ref, packed_ref):
    d = unit_ref.shape[1]
    packed_ref[:, :d] = unit_ref[...]
    packed_ref[:, d:] = seed_ref[...]


def pack_rows(units, seeds):
    out = shape((units.shape[0], units.shape[1] + seeds.shape[1]))
    return pl.pallas_call(
        pack_kernel,
        out_shape=out,
        in_specs=[VMEM] * 2,
        out_specs=VMEM,
        compiler_params=limits(out, out),
    )(units, seeds)


def stack_kernel(seed_ref, *refs):
    *packed, out_ref = refs
    m, c = seed_ref.shape
    out_ref[:m, :] = seed_ref[...]
    for k, ref in enumerate(packed):
        out_ref[(k + 1) * m : (k + 2) * m, :] = ref[:, ref.shape[1] - c :]


def stack_seeds(seeds, packed, work=0):
    m, c = seeds.shape
    out = shape(((len(packed) + 1) * m, c))
    return pl.pallas_call(
        stack_kernel,
        out_shape=out,
        in_specs=[VMEM] * (len(packed) + 1),
        out_specs=VMEM,
        compiler_params=limits(seeds, *packed, out),
        cost_estimate=pl.CostEstimate(flops=work, bytes_accessed=2 * m * c, transcendentals=0),
    )(seeds, *packed)


def flags_kernel(layout, m, t_parts, s_parts, unit, place_ref, pattern_ref, out_ref, block_ref):
    at = layout.coords(place_ref[0], place_ref[1])

    def block(offset, start):
        row, col = layout.row_col(layout.moved(at, offset))
        return ((col * layout.rows + row) * m + start) // BLOCK

    for k, (offset, start) in enumerate(s_parts):
        block_ref[:, k * unit : (k + 1) * unit] = jnp.full((1, unit), block(offset, start), jnp.int32)
    blocks = block_ref[...]
    for r, (offset, start) in enumerate(t_parts):
        target = block(offset, start)
        hits = blocks == pattern_ref[0, target]
        for k in range(1, pattern_ref.shape[0]):
            hits = hits | (blocks == pattern_ref[k, target])
        out_ref[r : r + 1, :] = jnp.where(hits, 1, 0)


def flags_call(layout, m, t_parts, s_parts, unit, pattern, place):
    out = shape((len(t_parts), len(s_parts) * unit), jnp.int32)
    smem = pl.BlockSpec(memory_space=pltpu.SMEM)
    return pl.pallas_call(
        functools.partial(flags_kernel, layout, m, t_parts, s_parts, unit),
        out_shape=out,
        in_specs=[smem] * 2,
        out_specs=VMEM,
        scratch_shapes=[pltpu.VMEM((1, out.shape[1]), jnp.int32)],
        compiler_params=limits(out, out),
        cost_estimate=pl.CostEstimate(flops=10**7, bytes_accessed=2**20, transcendentals=0),
    )(place, pattern.T)


def tiles_of(refs, scratch, d):
    tiles, held = [], 0
    for ref in refs:
        rows = ref.shape[0]
        if rows % (2 * BLOCK) == 0:
            tiles += [(ref, k, 2 * BLOCK) for k in range(0, rows, 2 * BLOCK)]
        else:
            scratch[held : held + rows, :] = ref[:, :d]
            held += rows
    k = 0
    while k < held:
        rows = next(w for w in (2 * BLOCK, BLOCK, BLOCK // 2) if held - k >= w)
        tiles.append((scratch, k, rows))
        k += rows
    return tiles


def gram_kernel(nt, ns, sub, d, t_first, s_first, flags, *refs):
    t_in, s_in, refs = refs[:nt], refs[nt : nt + ns], refs[nt + ns :]
    kern, acc, t_join, s_join = refs
    t_tiles, s_tiles = tiles_of(t_in, t_join, d), tiles_of(s_in, s_join, d)
    rows, cols = kern.shape
    col = 0
    for s_ref, s_at, width in s_tiles:
        row = 0
        for t_ref, t_at, tall in t_tiles:
            scores = lax.dot_general(
                t_ref[t_at : t_at + tall, :],
                s_ref[s_at : s_at + width, :d],
                (((1,), (1,)), ((), ())),
                preferred_element_type=jnp.float32,
            )
            value = jnp.exp(sharpness * scores).astype(jnp.bfloat16).astype(jnp.float32)
            for a in range(tall // sub):
                at = row + a * sub
                flag = flags[
                    (t_first + at) // sub : (t_first + at) // sub + 1,
                    s_first + col : s_first + col + width,
                ]
                part = jnp.where(flag > 0, value[a * sub : (a + 1) * sub], 0.0)
                kern[at : at + sub, col : col + width] = part.astype(jnp.bfloat16)
                if width % BLOCK:
                    if col == 0:
                        acc[at : at + sub, :] = jnp.zeros((sub, BLOCK), jnp.float32)
                    acc[at : at + sub, :width] += part
                    continue
                total = part[:, :BLOCK]
                for b in range(1, width // BLOCK):
                    total = total + part[:, b * BLOCK : (b + 1) * BLOCK]
                if col > 0:
                    total = total + acc[at : at + sub, :]
                acc[at : at + sub, :] = total
            row += tall
        col += width


def gram_call(flags, t_pieces, s_pieces, sub, t_first, s_first):
    rows, cols = (sum(p.shape[0] for p in pieces) for pieces in (t_pieces, s_pieces))
    d = t_pieces[0].shape[1]
    join = [
        shape((max(16, sum(p.shape[0] for p in pieces if p.shape[0] % (2 * BLOCK))), d))
        for pieces in (t_pieces, s_pieces)
    ]
    outs = [shape((rows, cols)), shape((rows, BLOCK), jnp.float32)]
    return pl.pallas_call(
        functools.partial(
            gram_kernel, len(t_pieces), len(s_pieces), sub, d, t_first, s_first
        ),
        out_shape=outs,
        in_specs=[VMEM] * (1 + len(t_pieces) + len(s_pieces)),
        out_specs=[VMEM] * 2,
        scratch_shapes=[pltpu.VMEM(j.shape, j.dtype) for j in join],
        compiler_params=limits(flags, *t_pieces, *s_pieces, *outs, *join),
        cost_estimate=pl.CostEstimate(
            flops=2 * rows * cols * d,
            bytes_accessed=2 * (rows + cols) * d,
            transcendentals=rows * cols,
        ),
    )(flags, *t_pieces, *s_pieces)


def spread_kernel(plan, nk, na, ns, *refs):
    m, t_layout, rects, p_map = plan
    kerns, refs = refs[:nk], refs[nk:]
    accs, refs = refs[:na], refs[na:]
    p_in, refs = refs[:ns], refs[ns:]
    outs, pcat = refs[:-1], refs[-1]
    own_ref, other_refs = outs[0], outs[2:] if na else outs[1:]
    c = pcat.shape[1]
    at = 0
    for index, start, rows, lane in p_map:
        pcat[at : at + rows, :] = p_in[index][start : start + rows, lane : lane + c]
        at += rows
    row = 0
    for piece, start, rows in t_layout:
        part = None
        for kern, (t0, t1, c0, c1) in zip(kerns, rects):
            if t0 <= row < t1:
                term = jnp.dot(
                    kern[row - t0 : row - t0 + rows, :],
                    pcat[c0:c1, :],
                    preferred_element_type=jnp.float32,
                )
                part = term if part is None else part + term
        if piece == 0:
            own_ref[start : start + rows, :] = part
        else:
            other_refs[piece - 1][start : start + rows, :] = part.astype(jnp.bfloat16)
        step = math.gcd(rows, BLOCK)
        for lane in range(0, rows if na else 0, step):
            total = None
            for acc, (t0, t1, c0, c1) in zip(accs, rects):
                if t0 <= row < t1:
                    first = row - t0 + lane
                    term = acc[first : first + step, :]
                    total = term if total is None else total + term
            total = jnp.sum(total.T, axis=0, keepdims=True)
            lanes = slice(start + lane, start + lane + step)
            if piece == 0:
                outs[1][:, lanes] = total
            else:
                high = total.astype(jnp.bfloat16).astype(jnp.float32)
                mid = (total - high).astype(jnp.bfloat16).astype(jnp.float32)
                low = total - high - mid
                index = lax.broadcasted_iota(jnp.int32, (16, step), 0)
                terms = jnp.where(index == 0, high, jnp.where(index == 1, mid, low))
                terms = jnp.where(index < 3, terms, 0.0)
                other_refs[piece - 1][m:, lanes] = terms.astype(jnp.bfloat16)
        row += rows


def spread_call(kerns, accs, p_pieces, c, plan):
    m, t_layout, rects, p_map = plan
    nt = 1 + max(piece for piece, _, _ in t_layout)
    cols = sum(rows for _, _, rows, _ in p_map)
    extra = 16 if accs else 0
    outs = [jax.ShapeDtypeStruct((m, c), jnp.float32)]
    if accs:
        outs.append(jax.ShapeDtypeStruct((1, m), jnp.float32))
    outs += [jax.ShapeDtypeStruct((m + extra, c), jnp.bfloat16)] * (nt - 1)
    return pl.pallas_call(
        functools.partial(spread_kernel, plan, len(kerns), len(accs), len(p_pieces)),
        out_shape=outs,
        in_specs=[VMEM] * (len(kerns) + len(accs) + len(p_pieces)),
        out_specs=[VMEM] * len(outs),
        scratch_shapes=[pltpu.VMEM((cols, c), jnp.bfloat16)],
        compiler_params=limits(*kerns, *accs, *p_pieces, *outs, shape((cols, c))),
        cost_estimate=pl.CostEstimate(
            flops=2 * nt * m * cols * c,
            bytes_accessed=2 * (nt * m * cols + cols * c),
            transcendentals=0,
        ),
    )(*kerns, *accs, *p_pieces)


def first_update_kernel(seed_ref, own_ref, own_total_ref, *refs):
    got, (panel_ref, total_ref) = refs[:-2], refs[-2:]
    m = seed_ref.shape[0]
    numerators = own_ref[...]
    for ref in got:
        numerators = numerators + ref[:m, :].astype(jnp.float32)
    totals = own_total_ref[...]
    for ref in got:
        terms = ref[m:, :m].astype(jnp.float32)
        totals = totals + jnp.sum(terms, axis=0, keepdims=True)
    step = min(m, BLOCK)
    for k in range(0, m, step):
        total_ref[k : k + step, :] = jnp.broadcast_to(totals[:, k : k + step], (BLOCK, step)).T
    for k in range(0, seed_ref.shape[1], BLOCK):
        labels = mixing * numerators[:, k : k + BLOCK] / total_ref[...] + (
            1.0 - mixing
        ) * seed_ref[:, k : k + BLOCK].astype(jnp.float32)
        panel_ref[:, k : k + BLOCK] = labels.astype(jnp.bfloat16)


def last_update_kernel(seed_ref, own_ref, total_ref, *refs):
    got, out_ref = refs[:-1], refs[-1]
    numerators = own_ref[...]
    for ref in got:
        numerators = numerators + ref[...].astype(jnp.float32)
    for k in range(0, seed_ref.shape[1], BLOCK):
        out_ref[:, k : k + BLOCK] = mixing * numerators[:, k : k + BLOCK] / total_ref[...] + (
            1.0 - mixing
        ) * seed_ref[:, k : k + BLOCK].astype(jnp.float32)


def update(kernel, seeds, own, totals, got, out_shape):
    return pl.pallas_call(
        kernel,
        out_shape=out_shape,
        in_specs=[VMEM] * (3 + len(got)),
        out_specs=jax.tree.map(lambda _: VMEM, out_shape),
        compiler_params=limits(seeds, own, totals, *got, own, own),
    )(seeds, own, totals, *got)


def after(value, *earlier):
    return lax.optimization_barrier((value, *earlier))[0]


def on_device(embeddings, seed_labels, pattern):
    layout = Layout(lax.axis_size("row"), lax.axis_size("col"))
    size = layout.sizes
    m, c = embeddings.shape[0], seed_labels.shape[1]
    sub = min(m, BLOCK)
    other = {k: range(1, size[k]) for k in size}

    def fetch(values, axis, *earlier):
        return [
            layout.fetch(after(v, *earlier), **{axis: k}) for k in other[axis] for v in values
        ]

    t_offsets = [dict(zl=b, x=a) for b in range(size["zl"]) for a in range(size["x"])]
    near_t = [i for i, o in enumerate(t_offsets) if o["x"] == 0 or o["zl"] == 0]
    t_order = near_t + [i for i in range(len(t_offsets)) if i not in near_t]
    t_layout = [(i, 0, m) for i in t_order]
    both = [0] + list(other["core"])
    groups = [
        [(0, a, k) for a in range(size["y"]) for k in both],
        [(b, 0, k) for k in both for b in other["zh"]],
        [(b, a, 0) for a in other["y"] for b in other["zh"]],
        [(b, a, k) for k in other["core"] for a in other["y"] for b in other["zh"]],
    ]
    s_layout = [dict(zh=b, y=a, core=k) for group in groups for b, a, k in group]
    p_map = [(i, 0, m, 0) for i in range(len(s_layout))]
    seeds_map = []
    for i, o in enumerate(s_layout):
        if o["zh"] == 0:
            seeds_map.append((i, 0, m, embeddings.shape[1]))
        else:
            stack = len(groups[0]) + o["core"] * (size["zh"] - 1) + o["zh"] - 1
            seeds_map.append((stack, o["y"] * m, m, 0))
    t_parts = [(t_offsets[i], k) for i in t_order for k in range(0, m, sub)]
    s_parts = [(o, k) for o in s_layout for k in range(0, m, sub)]
    place = jnp.stack([lax.axis_index("row"), lax.axis_index("col")]).astype(jnp.int32)
    units = unit_rows(after(embeddings, place))
    packed = pack_rows(units, seed_labels)

    t_pieces, kerns, accs, rects = [], [], [], []
    s_pieces = [None] * len(groups)

    def rectangle(first, last, g0, g1):
        t0, t1 = first * m, last * m
        c0, c1 = (m * sum(len(group) for group in groups[:g]) for g in (g0, g1))
        if t0 == t1 or c0 == c1:
            return []
        kern, acc = gram_call(
            flags,
            t_pieces[first:last],
            [p for g in range(g0, g1) for p in s_pieces[g]],
            sub,
            t0,
            c0,
        )
        kerns.append(kern)
        accs.append(acc)
        rects.append((t0, t1, c0, c1))
        return [acc]

    zh, zl, x = fetch([units], "zh"), fetch([units], "zl"), fetch([units], "x")
    y, own_core = fetch([packed], "y"), fetch([packed], "core")
    flags = flags_call(layout, m, t_parts, s_parts, sub, pattern, place)
    held = stack_seeds(after(seed_labels, flags, *zh), [], 2 * 10**10)
    done = zh + zl + x + y + own_core + [held]
    zh_y, zl_x = fetch(zh, "y", *done), fetch(zl, "x", *done)
    y_core = [fetch([v], "core", *done) for v in y]
    zh_core = fetch(zh, "core", *done)
    seeds_zh = fetch([stack_seeds(held, y)], "zh", *done)
    by_offset = {(0, 0): units}
    by_offset.update({(0, a): v for a, v in zip(other["x"], x)})
    by_offset.update({(b, 0): v for b, v in zip(other["zl"], zl)})
    by_offset.update({(b, a): v for (a, b), v in zip([(a, b) for a in other["x"] for b in other["zl"]], zl_x)})
    t_pieces += [by_offset[t_offsets[i]["zl"], t_offsets[i]["x"]] for i in t_order]
    s_pieces[0] = [packed] + own_core + [p for v, w in zip(y, y_core) for p in [v] + w]
    s_pieces[1] = zh + zh_core
    s_pieces[2] = zh_y
    early, last = len(near_t), len(t_order)
    gram = rectangle(0, early, 0, 1) + rectangle(0, early, 1, 2)
    seeds_zh = [stack_seeds(after(v, *gram), [], 2 * 10**10) for v in seeds_zh]
    done = zh_y + zl_x + zh_core + gram + seeds_zh
    zh_y_core = fetch(zh_y, "core", *done)
    s_pieces[3] = zh_y_core
    seeds_core = fetch(seeds_zh, "core", *done)
    rectangle(early, last, 0, 3)
    rectangle(0, early, 2, 3)
    rectangle(0, last, 3, 4)
    plan = (m, t_layout, rects)

    def home(values):
        return [
            layout.fetch(v, **{k: -d for k, d in o.items()})
            for v, o in zip(values, t_offsets[1:])
        ]

    def panels(panel):
        far, near = fetch([panel], "zh"), fetch([panel], "y")
        far_y = fetch(far, "y")
        near = [p for v in [panel] + near for p in [v] + fetch([v], "core")]
        return near + far + fetch(far, "core") + far_y + fetch(far_y, "core")

    seeds = s_pieces[0] + seeds_zh + seeds_core
    own, totals, *others = spread_call(kerns, accs, seeds, c, (*plan, seeds_map))
    panel, totals = update(
        first_update_kernel,
        held,
        own,
        totals,
        home(others),
        [
            jax.ShapeDtypeStruct((m, c), jnp.bfloat16),
            jax.ShapeDtypeStruct((m, BLOCK), jnp.float32),
        ],
    )
    own, *others = spread_call(kerns, [], panels(panel), c, (*plan, p_map))
    return update(
        last_update_kernel,
        held,
        own,
        totals,
        home(others),
        jax.ShapeDtypeStruct((m, c), jnp.float32),
    )


def solution(mesh):
    return jax.shard_map(
        on_device,
        mesh=mesh,
        in_specs=(P(("col", "row"), None), P(("col", "row"), None), P()),
        out_specs=P(("col", "row"), None),
        check_vma=False,
    )
```

```python
import functools
import math

import jax
import jax.numpy as jnp
from jax import lax
from jax.experimental import pallas as pl
from jax.experimental.pallas import tpu as pltpu
from jax.sharding import PartitionSpec as P

BLOCK = 128
AXES = ("row", "col")

sharpness = 30.0
mixing = 0.8
epsilon = 1e-06


def split_two(n):
    low = max(d for d in range(1, math.isqrt(n) + 1) if n % d == 0)
    return n // low, low


class Layout:
    def __init__(self, rows, cols):
        core = 2 if cols % 2 == 0 else 1
        ny, nx = split_two(rows)
        nzh, nzl = split_two(cols // core)
        self.sizes = dict(y=ny, x=nx, zh=nzh, zl=nzl, core=core)
        self.rows, self.cols = rows, cols

    def coords(self, row, col):
        s = self.sizes
        return dict(
            y=row // s["x"],
            x=row % s["x"],
            zh=col // (s["zl"] * s["core"]),
            zl=col // s["core"] % s["zl"],
            core=col % s["core"],
        )

    def moved(self, at, offset):
        return {k: (at[k] + offset.get(k, 0)) % self.sizes[k] for k in at}

    def row_col(self, at):
        s = self.sizes
        return at["y"] * s["x"] + at["x"], (at["zh"] * s["zl"] + at["zl"]) * s["core"] + at["core"]

    def fetch(self, value, **offset):
        if all(v % self.sizes[k] == 0 for k, v in offset.items()):
            return value
        pairs = []
        for row in range(self.rows):
            for col in range(self.cols):
                r, c = self.row_col(self.moved(self.coords(row, col), offset))
                pairs.append((r * self.cols + c, row * self.cols + col))
        return lax.ppermute(value, AXES, pairs)

    def device(self, offset):
        at = self.coords(lax.axis_index("row"), lax.axis_index("col"))
        row, col = self.row_col(self.moved(at, offset))
        return col * self.rows + row


VMEM = pl.BlockSpec(memory_space=pltpu.VMEM)


def limits(*arrays, mib=3):
    total = sum(max(math.prod(a.shape), 8 * BLOCK) * a.dtype.itemsize for a in arrays)
    return pltpu.CompilerParams(vmem_limit_bytes=total * 5 // 4 + mib * 2**20)


def shape(dims, dtype=jnp.bfloat16):
    return jax.ShapeDtypeStruct(dims, dtype)


def unit_of(values):
    values = values.astype(jnp.float32)
    mean_square = jnp.mean(values * values, axis=1, keepdims=True)
    scaled = values * lax.rsqrt(mean_square + epsilon) * values.shape[1] ** (-0.5)
    return scaled.astype(jnp.bfloat16)


def unit_kernel(emb_ref, unit_ref):
    unit_ref[...] = unit_of(emb_ref[...])


def unit_rows(embeddings):
    out = shape(embeddings.shape)
    return pl.pallas_call(
        unit_kernel,
        out_shape=out,
        in_specs=[VMEM],
        out_specs=VMEM,
        compiler_params=limits(*[out] * 4),
    )(embeddings)


def pack_kernel(unit_ref, seed_ref, packed_ref):
    d = unit_ref.shape[1]
    packed_ref[:, :d] = unit_ref[...]
    packed_ref[:, d:] = seed_ref[...]


def pack_rows(units, seeds):
    out = shape((units.shape[0], units.shape[1] + seeds.shape[1]))
    return pl.pallas_call(
        pack_kernel,
        out_shape=out,
        in_specs=[VMEM] * 2,
        out_specs=VMEM,
        compiler_params=limits(out, out),
    )(units, seeds)


def stack_kernel(seed_ref, *refs):
    *packed, out_ref = refs
    m, c = seed_ref.shape
    out_ref[:m, :] = seed_ref[...]
    for k, ref in enumerate(packed):
        out_ref[(k + 1) * m : (k + 2) * m, :] = ref[:, ref.shape[1] - c :]


def stack_seeds(seeds, packed, work=0):
    m, c = seeds.shape
    out = shape(((len(packed) + 1) * m, c))
    return pl.pallas_call(
        stack_kernel,
        out_shape=out,
        in_specs=[VMEM] * (len(packed) + 1),
        out_specs=VMEM,
        compiler_params=limits(seeds, *packed, out),
        cost_estimate=pl.CostEstimate(flops=work, bytes_accessed=2 * m * c, transcendentals=0),
    )(seeds, *packed)


def flags_kernel(layout, m, t_parts, s_parts, unit, place_ref, pattern_ref, out_ref, block_ref):
    at = layout.coords(place_ref[0], place_ref[1])

    def block(offset, start):
        row, col = layout.row_col(layout.moved(at, offset))
        return ((col * layout.rows + row) * m + start) // BLOCK

    for k, (offset, start) in enumerate(s_parts):
        block_ref[:, k * unit : (k + 1) * unit] = jnp.full((1, unit), block(offset, start), jnp.int32)
    blocks = block_ref[...]
    for r, (offset, start) in enumerate(t_parts):
        target = block(offset, start)
        hits = blocks == pattern_ref[0, target]
        for k in range(1, pattern_ref.shape[0]):
            hits = hits | (blocks == pattern_ref[k, target])
        out_ref[r : r + 1, :] = jnp.where(hits, 1, 0)


def flags_call(layout, m, t_parts, s_parts, unit, pattern, place):
    out = shape((len(t_parts), len(s_parts) * unit), jnp.int32)
    smem = pl.BlockSpec(memory_space=pltpu.SMEM)
    return pl.pallas_call(
        functools.partial(flags_kernel, layout, m, t_parts, s_parts, unit),
        out_shape=out,
        in_specs=[smem] * 2,
        out_specs=VMEM,
        scratch_shapes=[pltpu.VMEM((1, out.shape[1]), jnp.int32)],
        compiler_params=limits(out, out),
        cost_estimate=pl.CostEstimate(flops=10**7, bytes_accessed=2**20, transcendentals=0),
    )(place, pattern.T)


def tiles_of(refs, scratch, d):
    tiles, held = [], 0
    for ref in refs:
        rows = ref.shape[0]
        if rows % (2 * BLOCK) == 0:
            tiles += [(ref, k, 2 * BLOCK) for k in range(0, rows, 2 * BLOCK)]
        else:
            scratch[held : held + rows, :] = ref[:, :d]
            held += rows
    k = 0
    while k < held:
        rows = next(w for w in (2 * BLOCK, BLOCK, BLOCK // 2) if held - k >= w)
        tiles.append((scratch, k, rows))
        k += rows
    return tiles


def gram_kernel(nt, ns, sub, d, t_first, s_first, flags, *refs):
    t_in, s_in, refs = refs[:nt], refs[nt : nt + ns], refs[nt + ns :]
    kern, acc, t_join, s_join = refs
    t_tiles, s_tiles = tiles_of(t_in, t_join, d), tiles_of(s_in, s_join, d)
    rows, cols = kern.shape
    col = 0
    for s_ref, s_at, width in s_tiles:
        row = 0
        for t_ref, t_at, tall in t_tiles:
            scores = lax.dot_general(
                t_ref[t_at : t_at + tall, :],
                s_ref[s_at : s_at + width, :d],
                (((1,), (1,)), ((), ())),
                preferred_element_type=jnp.float32,
            )
            value = jnp.exp(sharpness * scores).astype(jnp.bfloat16).astype(jnp.float32)
            for a in range(tall // sub):
                at = row + a * sub
                flag = flags[
                    (t_first + at) // sub : (t_first + at) // sub + 1,
                    s_first + col : s_first + col + width,
                ]
                part = jnp.where(flag > 0, value[a * sub : (a + 1) * sub], 0.0)
                kern[at : at + sub, col : col + width] = part.astype(jnp.bfloat16)
                if width % BLOCK:
                    if col == 0:
                        acc[at : at + sub, :] = jnp.zeros((sub, BLOCK), jnp.float32)
                    acc[at : at + sub, :width] += part
                    continue
                total = part[:, :BLOCK]
                for b in range(1, width // BLOCK):
                    total = total + part[:, b * BLOCK : (b + 1) * BLOCK]
                if col > 0:
                    total = total + acc[at : at + sub, :]
                acc[at : at + sub, :] = total
            row += tall
        col += width


def gram_call(flags, t_pieces, s_pieces, sub, t_first, s_first):
    rows, cols = (sum(p.shape[0] for p in pieces) for pieces in (t_pieces, s_pieces))
    d = t_pieces[0].shape[1]
    join = [
        shape((max(16, sum(p.shape[0] for p in pieces if p.shape[0] % (2 * BLOCK))), d))
        for pieces in (t_pieces, s_pieces)
    ]
    outs = [shape((rows, cols)), shape((rows, BLOCK), jnp.float32)]
    return pl.pallas_call(
        functools.partial(
            gram_kernel, len(t_pieces), len(s_pieces), sub, d, t_first, s_first
        ),
        out_shape=outs,
        in_specs=[VMEM] * (1 + len(t_pieces) + len(s_pieces)),
        out_specs=[VMEM] * 2,
        scratch_shapes=[pltpu.VMEM(j.shape, j.dtype) for j in join],
        compiler_params=limits(flags, *t_pieces, *s_pieces, *outs, *join),
        cost_estimate=pl.CostEstimate(
            flops=2 * rows * cols * d,
            bytes_accessed=2 * (rows + cols) * d,
            transcendentals=rows * cols,
        ),
    )(flags, *t_pieces, *s_pieces)


def row_sums(kerns, rects, pcat, row, rows, lo, hi):
    part = None
    for kern, (t0, t1, c0, c1) in zip(kerns, rects):
        first, last = max(c0, lo), min(c1, hi)
        if t0 <= row < t1 and first < last:
            term = jnp.dot(
                kern[row - t0 : row - t0 + rows, first - c0 : last - c0],
                pcat[first - lo : last - lo, :],
                preferred_element_type=jnp.float32,
            )
            part = term if part is None else part + term
    return part


def base_kernel(t_layout, rects, nk, *refs):
    kerns, p_in, (out_ref, pcat) = refs[:nk], refs[nk:-2], refs[-2:]
    at = 0
    for ref in p_in:
        pcat[at : at + ref.shape[0], :] = ref[...]
        at += ref.shape[0]
    row = 0
    for _, _, rows in t_layout:
        out_ref[row : row + rows, :] = row_sums(kerns, rects, pcat, row, rows, 0, at)
        row += rows


def base_call(kerns, p_pieces, t_layout, rects):
    m, c = p_pieces[0].shape
    rows, cols = sum(r for _, _, r in t_layout), m * len(p_pieces)
    out = shape((rows, c), jnp.float32)
    return pl.pallas_call(
        functools.partial(base_kernel, t_layout, rects, len(kerns)),
        out_shape=out,
        in_specs=[VMEM] * (len(kerns) + len(p_pieces)),
        out_specs=VMEM,
        scratch_shapes=[pltpu.VMEM((cols, c), jnp.bfloat16)],
        compiler_params=limits(*kerns, *p_pieces, out, shape((cols, c))),
        cost_estimate=pl.CostEstimate(
            flops=2 * rows * cols * c, bytes_accessed=2 * rows * cols, transcendentals=0
        ),
    )(*kerns, *p_pieces)


def spread_kernel(plan, nk, na, ns, *refs):
    m, t_layout, rects, p_map, lo = plan
    kerns, refs = refs[:nk], refs[nk:]
    base, refs = (refs[0], refs[1:]) if lo else (None, refs)
    accs, refs = refs[:na], refs[na:]
    p_in, refs = refs[:ns], refs[ns:]
    outs, pcat = refs[:-1], refs[-1]
    own_ref, other_refs = outs[0], outs[2:] if na else outs[1:]
    c = pcat.shape[1]
    at = 0
    for index, start, rows, lane in p_map:
        pcat[at : at + rows, :] = p_in[index][start : start + rows, lane : lane + c]
        at += rows
    row = 0
    for piece, start, rows in t_layout:
        part = row_sums(kerns, rects, pcat, row, rows, lo, lo + pcat.shape[0])
        if lo:
            part = part + base[row : row + rows, :]
        if piece == 0:
            own_ref[start : start + rows, :] = part
        else:
            other_refs[piece - 1][start : start + rows, :] = part.astype(jnp.bfloat16)
        step = math.gcd(rows, BLOCK)
        for lane in range(0, rows if na else 0, step):
            total = None
            for acc, (t0, t1, c0, c1) in zip(accs, rects):
                if t0 <= row < t1:
                    first = row - t0 + lane
                    term = acc[first : first + step, :]
                    total = term if total is None else total + term
            total = jnp.sum(total.T, axis=0, keepdims=True)
            lanes = slice(start + lane, start + lane + step)
            if piece == 0:
                outs[1][:, lanes] = total
            else:
                high = total.astype(jnp.bfloat16).astype(jnp.float32)
                mid = (total - high).astype(jnp.bfloat16).astype(jnp.float32)
                low = total - high - mid
                index = lax.broadcasted_iota(jnp.int32, (16, step), 0)
                terms = jnp.where(index == 0, high, jnp.where(index == 1, mid, low))
                terms = jnp.where(index < 3, terms, 0.0)
                other_refs[piece - 1][m:, lanes] = terms.astype(jnp.bfloat16)
        row += rows


def spread_call(kerns, accs, p_pieces, c, plan, base=()):
    m, t_layout, rects, p_map, lo = plan
    nt = 1 + max(piece for piece, _, _ in t_layout)
    cols = sum(rows for _, _, rows, _ in p_map)
    extra = 16 if accs else 0
    outs = [jax.ShapeDtypeStruct((m, c), jnp.float32)]
    if accs:
        outs.append(jax.ShapeDtypeStruct((1, m), jnp.float32))
    outs += [jax.ShapeDtypeStruct((m + extra, c), jnp.bfloat16)] * (nt - 1)
    return pl.pallas_call(
        functools.partial(spread_kernel, plan, len(kerns), len(accs), len(p_pieces)),
        out_shape=outs,
        in_specs=[VMEM] * (len(kerns) + len(base) + len(accs) + len(p_pieces)),
        out_specs=[VMEM] * len(outs),
        scratch_shapes=[pltpu.VMEM((cols, c), jnp.bfloat16)],
        compiler_params=limits(*kerns, *base, *accs, *p_pieces, *outs, shape((cols, c))),
        cost_estimate=pl.CostEstimate(
            flops=2 * nt * m * cols * c,
            bytes_accessed=2 * (nt * m * cols + cols * c),
            transcendentals=0,
        ),
    )(*kerns, *base, *accs, *p_pieces)


def first_update_kernel(seed_ref, own_ref, own_total_ref, *refs):
    got, (panel_ref, total_ref) = refs[:-2], refs[-2:]
    m = seed_ref.shape[0]
    numerators = own_ref[...]
    for ref in got:
        numerators = numerators + ref[:m, :].astype(jnp.float32)
    totals = own_total_ref[...]
    for ref in got:
        terms = ref[m:, :m].astype(jnp.float32)
        totals = totals + jnp.sum(terms, axis=0, keepdims=True)
    step = min(m, BLOCK)
    for k in range(0, m, step):
        total_ref[k : k + step, :] = jnp.broadcast_to(totals[:, k : k + step], (BLOCK, step)).T
    for k in range(0, seed_ref.shape[1], BLOCK):
        labels = mixing * numerators[:, k : k + BLOCK] / total_ref[...] + (
            1.0 - mixing
        ) * seed_ref[:, k : k + BLOCK].astype(jnp.float32)
        panel_ref[:, k : k + BLOCK] = labels.astype(jnp.bfloat16)


def last_update_kernel(seed_ref, own_ref, total_ref, *refs):
    got, out_ref = refs[:-1], refs[-1]
    numerators = own_ref[...]
    for ref in got:
        numerators = numerators + ref[...].astype(jnp.float32)
    for k in range(0, seed_ref.shape[1], BLOCK):
        out_ref[:, k : k + BLOCK] = mixing * numerators[:, k : k + BLOCK] / total_ref[...] + (
            1.0 - mixing
        ) * seed_ref[:, k : k + BLOCK].astype(jnp.float32)


def update(kernel, seeds, own, totals, got, out_shape):
    return pl.pallas_call(
        kernel,
        out_shape=out_shape,
        in_specs=[VMEM] * (3 + len(got)),
        out_specs=jax.tree.map(lambda _: VMEM, out_shape),
        compiler_params=limits(seeds, own, totals, *got, own, own),
    )(seeds, own, totals, *got)


def after(value, *earlier):
    return lax.optimization_barrier((value, *earlier))[0]


def on_device(embeddings, seed_labels, pattern):
    layout = Layout(lax.axis_size("row"), lax.axis_size("col"))
    size = layout.sizes
    m, c = embeddings.shape[0], seed_labels.shape[1]
    sub = min(m, BLOCK)
    other = {k: range(1, size[k]) for k in size}

    def fetch(values, axis, *earlier):
        return [
            layout.fetch(after(v, *earlier), **{axis: k}) for k in other[axis] for v in values
        ]

    t_offsets = [dict(zl=b, x=a) for b in range(size["zl"]) for a in range(size["x"])]
    near_t = [i for i, o in enumerate(t_offsets) if o["x"] == 0 or o["zl"] == 0]
    t_order = near_t + [i for i in range(len(t_offsets)) if i not in near_t]
    t_layout = [(i, 0, m) for i in t_order]
    both = [0] + list(other["core"])
    groups = [
        [(0, a, k) for a in range(size["y"]) for k in both],
        [(b, 0, k) for k in both for b in other["zh"]],
        [(b, a, 0) for a in other["y"] for b in other["zh"]],
        [(b, a, k) for k in other["core"] for a in other["y"] for b in other["zh"]],
    ]
    s_layout = [dict(zh=b, y=a, core=k) for group in groups for b, a, k in group]
    seeds_map = []
    for i, o in enumerate(s_layout):
        if o["zh"] == 0:
            seeds_map.append((i, 0, m, embeddings.shape[1]))
        else:
            stack = len(groups[0]) + o["core"] * (size["zh"] - 1) + o["zh"] - 1
            seeds_map.append((stack, o["y"] * m, m, 0))
    t_parts = [(t_offsets[i], k) for i in t_order for k in range(0, m, sub)]
    s_parts = [(o, k) for o in s_layout for k in range(0, m, sub)]
    place = jnp.stack([lax.axis_index("row"), lax.axis_index("col")]).astype(jnp.int32)
    units = unit_rows(after(embeddings, place))
    packed = pack_rows(units, seed_labels)

    t_pieces, kerns, accs, rects = [], [], [], []
    s_pieces = [None] * len(groups)

    def rectangle(first, last, g0, g1):
        t0, t1 = first * m, last * m
        c0, c1 = (m * sum(len(group) for group in groups[:g]) for g in (g0, g1))
        if t0 == t1 or c0 == c1:
            return []
        kern, acc = gram_call(
            flags,
            t_pieces[first:last],
            [p for g in range(g0, g1) for p in s_pieces[g]],
            sub,
            t0,
            c0,
        )
        kerns.append(kern)
        accs.append(acc)
        rects.append((t0, t1, c0, c1))
        return [acc]

    zh, zl, x = fetch([units], "zh"), fetch([units], "zl"), fetch([units], "x")
    y, own_core = fetch([packed], "y"), fetch([packed], "core")
    flags = flags_call(layout, m, t_parts, s_parts, sub, pattern, place)
    held = stack_seeds(after(seed_labels, flags, *zh), [], 2 * 10**10)
    done = zh + zl + x + y + own_core + [held]
    zh_y, zl_x = fetch(zh, "y", *done), fetch(zl, "x", *done)
    y_core = [fetch([v], "core", *done) for v in y]
    zh_core = fetch(zh, "core", *done)
    seeds_zh = fetch([stack_seeds(held, y)], "zh", *done)
    by_offset = {(0, 0): units}
    by_offset.update({(0, a): v for a, v in zip(other["x"], x)})
    by_offset.update({(b, 0): v for b, v in zip(other["zl"], zl)})
    by_offset.update({(b, a): v for (a, b), v in zip([(a, b) for a in other["x"] for b in other["zl"]], zl_x)})
    t_pieces += [by_offset[t_offsets[i]["zl"], t_offsets[i]["x"]] for i in t_order]
    s_pieces[0] = [packed] + own_core + [p for v, w in zip(y, y_core) for p in [v] + w]
    s_pieces[1] = zh + zh_core
    s_pieces[2] = zh_y
    early, last = len(near_t), len(t_order)
    gram = rectangle(0, early, 0, 1) + rectangle(0, early, 1, 2)
    seeds_zh = [stack_seeds(after(v, *gram), [], 2 * 10**10) for v in seeds_zh]
    done = zh_y + zh_core + gram + seeds_zh
    zh_y_core = fetch(zh_y, "core", *done)
    s_pieces[3] = zh_y_core
    seeds_core = fetch(seeds_zh, "core", *done)
    rectangle(early, last, 0, 3)
    rectangle(0, early, 2, 3)
    rectangle(0, last, 3, 4)
    plan = (m, t_layout, rects)

    def home(values):
        return [
            layout.fetch(v, **{k: -d for k, d in o.items()})
            for v, o in zip(values, t_offsets[1:])
        ]

    def panels(panel):
        far, near = fetch([panel], "zh"), fetch([panel], "y")
        far_y = fetch(far, "y")
        near = [p for v in [panel] + near for p in [v] + fetch([v], "core")]
        return near + far + fetch(far, "core") + far_y + fetch(far_y, "core")

    seeds = s_pieces[0] + seeds_zh + seeds_core
    own, totals, *others = spread_call(kerns, accs, seeds, c, (*plan, seeds_map, 0))
    panel, totals = update(
        first_update_kernel,
        held,
        own,
        totals,
        home(others),
        [
            jax.ShapeDtypeStruct((m, c), jnp.bfloat16),
            jax.ShapeDtypeStruct((m, BLOCK), jnp.float32),
        ],
    )
    pieces = panels(panel)
    first = len(groups[0]) + len(groups[1])
    base = base_call(kerns, pieces[:first], t_layout, rects)
    rest = [(i, 0, m, 0) for i in range(len(pieces) - first)]
    own, *others = spread_call(kerns, [], pieces[first:], c, (*plan, rest, first * m), [base])
    return update(
        last_update_kernel,
        held,
        own,
        totals,
        home(others),
        jax.ShapeDtypeStruct((m, c), jnp.float32),
    )


def solution(mesh):
    return jax.shard_map(
        on_device,
        mesh=mesh,
        in_specs=(P(("col", "row"), None), P(("col", "row"), None), P()),
        out_specs=P(("col", "row"), None),
        check_vma=False,
    )
```

```python
import functools
import math

import jax
import jax.numpy as jnp
from jax import lax
from jax.experimental import pallas as pl
from jax.experimental.pallas import tpu as pltpu
from jax.sharding import PartitionSpec as P

BLOCK = 128
AXES = ("row", "col")

sharpness = 30.0
mixing = 0.8
epsilon = 1e-06


def split_two(n):
    low = max(d for d in range(1, math.isqrt(n) + 1) if n % d == 0)
    return n // low, low


class Layout:
    def __init__(self, rows, cols):
        core = 2 if cols % 2 == 0 else 1
        ny, nx = split_two(rows)
        nzh, nzl = split_two(cols // core)
        self.sizes = dict(y=ny, x=nx, zh=nzh, zl=nzl, core=core)
        self.rows, self.cols = rows, cols

    def coords(self, row, col):
        s = self.sizes
        return dict(
            y=row // s["x"],
            x=row % s["x"],
            zh=col // (s["zl"] * s["core"]),
            zl=col // s["core"] % s["zl"],
            core=col % s["core"],
        )

    def moved(self, at, offset):
        return {k: (at[k] + offset.get(k, 0)) % self.sizes[k] for k in at}

    def row_col(self, at):
        s = self.sizes
        return at["y"] * s["x"] + at["x"], (at["zh"] * s["zl"] + at["zl"]) * s["core"] + at["core"]

    def fetch(self, value, **offset):
        if all(v % self.sizes[k] == 0 for k, v in offset.items()):
            return value
        pairs = []
        for row in range(self.rows):
            for col in range(self.cols):
                r, c = self.row_col(self.moved(self.coords(row, col), offset))
                pairs.append((r * self.cols + c, row * self.cols + col))
        return lax.ppermute(value, AXES, pairs)

    def device(self, offset):
        at = self.coords(lax.axis_index("row"), lax.axis_index("col"))
        row, col = self.row_col(self.moved(at, offset))
        return col * self.rows + row


VMEM = pl.BlockSpec(memory_space=pltpu.VMEM)


def limits(*arrays, mib=3):
    total = sum(max(math.prod(a.shape), 8 * BLOCK) * a.dtype.itemsize for a in arrays)
    return pltpu.CompilerParams(vmem_limit_bytes=total * 5 // 4 + mib * 2**20)


def shape(dims, dtype=jnp.bfloat16):
    return jax.ShapeDtypeStruct(dims, dtype)


def unit_of(values):
    values = values.astype(jnp.float32)
    mean_square = jnp.mean(values * values, axis=1, keepdims=True)
    scaled = values * lax.rsqrt(mean_square + epsilon) * values.shape[1] ** (-0.5)
    return scaled.astype(jnp.bfloat16)


def unit_kernel(emb_ref, unit_ref):
    unit_ref[...] = unit_of(emb_ref[...])


def unit_rows(embeddings):
    out = shape(embeddings.shape)
    return pl.pallas_call(
        unit_kernel,
        out_shape=out,
        in_specs=[VMEM],
        out_specs=VMEM,
        compiler_params=limits(*[out] * 4),
    )(embeddings)


def pack_kernel(unit_ref, seed_ref, packed_ref):
    d = unit_ref.shape[1]
    packed_ref[:, :d] = unit_ref[...]
    packed_ref[:, d:] = seed_ref[...]


def pack_rows(units, seeds):
    out = shape((units.shape[0], units.shape[1] + seeds.shape[1]))
    return pl.pallas_call(
        pack_kernel,
        out_shape=out,
        in_specs=[VMEM] * 2,
        out_specs=VMEM,
        compiler_params=limits(out, out),
    )(units, seeds)


def stack_kernel(seed_ref, *refs):
    *packed, out_ref = refs
    m, c = seed_ref.shape
    out_ref[:m, :] = seed_ref[...]
    for k, ref in enumerate(packed):
        out_ref[(k + 1) * m : (k + 2) * m, :] = ref[:, ref.shape[1] - c :]


def stack_seeds(seeds, packed, work=0):
    m, c = seeds.shape
    out = shape(((len(packed) + 1) * m, c))
    return pl.pallas_call(
        stack_kernel,
        out_shape=out,
        in_specs=[VMEM] * (len(packed) + 1),
        out_specs=VMEM,
        compiler_params=limits(seeds, *packed, out),
        cost_estimate=pl.CostEstimate(flops=work, bytes_accessed=2 * m * c, transcendentals=0),
    )(seeds, *packed)


def flags_kernel(layout, m, t_parts, s_parts, unit, place_ref, pattern_ref, out_ref, block_ref):
    at = layout.coords(place_ref[0], place_ref[1])

    def block(offset, start):
        row, col = layout.row_col(layout.moved(at, offset))
        return ((col * layout.rows + row) * m + start) // BLOCK

    for k, (offset, start) in enumerate(s_parts):
        block_ref[:, k * unit : (k + 1) * unit] = jnp.full((1, unit), block(offset, start), jnp.int32)
    blocks = block_ref[...]
    for r, (offset, start) in enumerate(t_parts):
        target = block(offset, start)
        hits = blocks == pattern_ref[0, target]
        for k in range(1, pattern_ref.shape[0]):
            hits = hits | (blocks == pattern_ref[k, target])
        out_ref[r : r + 1, :] = jnp.where(hits, 1, 0)


def flags_call(layout, m, t_parts, s_parts, unit, pattern, place):
    out = shape((len(t_parts), len(s_parts) * unit), jnp.int32)
    smem = pl.BlockSpec(memory_space=pltpu.SMEM)
    return pl.pallas_call(
        functools.partial(flags_kernel, layout, m, t_parts, s_parts, unit),
        out_shape=out,
        in_specs=[smem] * 2,
        out_specs=VMEM,
        scratch_shapes=[pltpu.VMEM((1, out.shape[1]), jnp.int32)],
        compiler_params=limits(out, out),
        cost_estimate=pl.CostEstimate(flops=10**7, bytes_accessed=2**20, transcendentals=0),
    )(place, pattern.T)


def tiles_of(refs, scratch, d):
    tiles, held = [], 0
    for ref in refs:
        rows = ref.shape[0]
        if rows % (2 * BLOCK) == 0:
            tiles += [(ref, k, 2 * BLOCK) for k in range(0, rows, 2 * BLOCK)]
        else:
            scratch[held : held + rows, :] = ref[:, :d]
            held += rows
    k = 0
    while k < held:
        rows = next(w for w in (2 * BLOCK, BLOCK, BLOCK // 2) if held - k >= w)
        tiles.append((scratch, k, rows))
        k += rows
    return tiles


def gram_kernel(nt, ns, sub, d, t_first, s_first, flags, *refs):
    t_in, s_in, refs = refs[:nt], refs[nt : nt + ns], refs[nt + ns :]
    kern, acc, t_join, s_join = refs
    t_tiles, s_tiles = tiles_of(t_in, t_join, d), tiles_of(s_in, s_join, d)
    rows, cols = kern.shape
    col = 0
    for s_ref, s_at, width in s_tiles:
        row = 0
        for t_ref, t_at, tall in t_tiles:
            scores = lax.dot_general(
                t_ref[t_at : t_at + tall, :],
                s_ref[s_at : s_at + width, :d],
                (((1,), (1,)), ((), ())),
                preferred_element_type=jnp.float32,
            )
            value = jnp.exp(sharpness * scores).astype(jnp.bfloat16).astype(jnp.float32)
            for a in range(tall // sub):
                at = row + a * sub
                flag = flags[
                    (t_first + at) // sub : (t_first + at) // sub + 1,
                    s_first + col : s_first + col + width,
                ]
                part = jnp.where(flag > 0, value[a * sub : (a + 1) * sub], 0.0)
                kern[at : at + sub, col : col + width] = part.astype(jnp.bfloat16)
                if width % BLOCK:
                    if col == 0:
                        acc[at : at + sub, :] = jnp.zeros((sub, BLOCK), jnp.float32)
                    acc[at : at + sub, :width] += part
                    continue
                total = part[:, :BLOCK]
                for b in range(1, width // BLOCK):
                    total = total + part[:, b * BLOCK : (b + 1) * BLOCK]
                if col > 0:
                    total = total + acc[at : at + sub, :]
                acc[at : at + sub, :] = total
            row += tall
        col += width


def gram_call(flags, t_pieces, s_pieces, sub, t_first, s_first):
    rows, cols = (sum(p.shape[0] for p in pieces) for pieces in (t_pieces, s_pieces))
    d = t_pieces[0].shape[1]
    join = [
        shape((max(16, sum(p.shape[0] for p in pieces if p.shape[0] % (2 * BLOCK))), d))
        for pieces in (t_pieces, s_pieces)
    ]
    outs = [shape((rows, cols)), shape((rows, BLOCK), jnp.float32)]
    return pl.pallas_call(
        functools.partial(
            gram_kernel, len(t_pieces), len(s_pieces), sub, d, t_first, s_first
        ),
        out_shape=outs,
        in_specs=[VMEM] * (1 + len(t_pieces) + len(s_pieces)),
        out_specs=[VMEM] * 2,
        scratch_shapes=[pltpu.VMEM(j.shape, j.dtype) for j in join],
        compiler_params=limits(flags, *t_pieces, *s_pieces, *outs, *join),
        cost_estimate=pl.CostEstimate(
            flops=2 * rows * cols * d,
            bytes_accessed=2 * (rows + cols) * d,
            transcendentals=rows * cols,
        ),
    )(flags, *t_pieces, *s_pieces)


def row_sums(kerns, rects, pcat, row, rows, lo, hi):
    part = None
    for kern, (t0, t1, c0, c1) in zip(kerns, rects):
        first, last = max(c0, lo), min(c1, hi)
        if t0 <= row < t1 and first < last:
            term = jnp.dot(
                kern[row - t0 : row - t0 + rows, first - c0 : last - c0],
                pcat[first - lo : last - lo, :],
                preferred_element_type=jnp.float32,
            )
            part = term if part is None else part + term
    return part


def base_kernel(t_layout, rects, nk, *refs):
    kerns, p_in, (out_ref, pcat) = refs[:nk], refs[nk:-2], refs[-2:]
    at = 0
    for ref in p_in:
        pcat[at : at + ref.shape[0], :] = ref[...]
        at += ref.shape[0]
    row = 0
    for _, _, rows in t_layout:
        out_ref[row : row + rows, :] = row_sums(kerns, rects, pcat, row, rows, 0, at)
        row += rows


def base_call(kerns, p_pieces, t_layout, rects):
    m, c = p_pieces[0].shape
    rows, cols = sum(r for _, _, r in t_layout), m * len(p_pieces)
    out = shape((rows, c), jnp.float32)
    return pl.pallas_call(
        functools.partial(base_kernel, t_layout, rects, len(kerns)),
        out_shape=out,
        in_specs=[VMEM] * (len(kerns) + len(p_pieces)),
        out_specs=VMEM,
        scratch_shapes=[pltpu.VMEM((cols, c), jnp.bfloat16)],
        compiler_params=limits(*kerns, *p_pieces, out, shape((cols, c))),
        cost_estimate=pl.CostEstimate(
            flops=2 * rows * cols * c, bytes_accessed=2 * rows * cols, transcendentals=0
        ),
    )(*kerns, *p_pieces)


def spread_kernel(plan, nk, na, ns, *refs):
    m, t_layout, rects, p_map, lo, chosen = plan
    kerns, refs = refs[:nk], refs[nk:]
    base, refs = (refs[0], refs[1:]) if lo else (None, refs)
    accs, refs = refs[:na], refs[na:]
    p_in, refs = refs[:ns], refs[ns:]
    outs, pcat = refs[:-1], refs[-1]
    owned = (2 if na else 1) if 0 in chosen else 0
    own_ref = outs[0]
    other_refs = dict(zip([p for p in chosen if p], outs[owned:]))
    c = pcat.shape[1]
    at = 0
    for index, start, rows, lane in p_map:
        pcat[at : at + rows, :] = p_in[index][start : start + rows, lane : lane + c]
        at += rows
    row = 0
    for piece, start, rows in t_layout:
        if piece not in chosen:
            row += rows
            continue
        part = row_sums(kerns, rects, pcat, row, rows, lo, lo + pcat.shape[0])
        if lo:
            part = part + base[row : row + rows, :]
        if piece == 0:
            own_ref[start : start + rows, :] = part
        else:
            other_refs[piece][start : start + rows, :] = part.astype(jnp.bfloat16)
        step = math.gcd(rows, BLOCK)
        for lane in range(0, rows if na else 0, step):
            total = None
            for acc, (t0, t1, c0, c1) in zip(accs, rects):
                if t0 <= row < t1:
                    first = row - t0 + lane
                    term = acc[first : first + step, :]
                    total = term if total is None else total + term
            total = jnp.sum(total.T, axis=0, keepdims=True)
            lanes = slice(start + lane, start + lane + step)
            if piece == 0:
                outs[1][:, lanes] = total
            else:
                high = total.astype(jnp.bfloat16).astype(jnp.float32)
                mid = (total - high).astype(jnp.bfloat16).astype(jnp.float32)
                low = total - high - mid
                index = lax.broadcasted_iota(jnp.int32, (16, step), 0)
                terms = jnp.where(index == 0, high, jnp.where(index == 1, mid, low))
                terms = jnp.where(index < 3, terms, 0.0)
                other_refs[piece][m:, lanes] = terms.astype(jnp.bfloat16)
        row += rows


def spread_call(kerns, accs, p_pieces, c, plan, base=()):
    m, t_layout, rects, p_map, lo, chosen = plan
    nt = len(chosen)
    cols = sum(rows for _, _, rows, _ in p_map)
    extra = 16 if accs else 0
    outs = []
    if 0 in chosen:
        outs.append(shape((m, c), jnp.float32))
        if accs:
            outs.append(shape((1, m), jnp.float32))
    outs += [shape((m + extra, c)) for p in chosen if p]
    return pl.pallas_call(
        functools.partial(spread_kernel, plan, len(kerns), len(accs), len(p_pieces)),
        out_shape=outs,
        in_specs=[VMEM] * (len(kerns) + len(base) + len(accs) + len(p_pieces)),
        out_specs=[VMEM] * len(outs),
        scratch_shapes=[pltpu.VMEM((cols, c), jnp.bfloat16)],
        compiler_params=limits(*kerns, *base, *accs, *p_pieces, *outs, shape((cols, c))),
        cost_estimate=pl.CostEstimate(
            flops=2 * nt * m * cols * c,
            bytes_accessed=2 * (nt * m * cols + cols * c),
            transcendentals=0,
        ),
    )(*kerns, *base, *accs, *p_pieces)


def first_update_kernel(seed_ref, own_ref, own_total_ref, *refs):
    got, (panel_ref, total_ref) = refs[:-2], refs[-2:]
    m = seed_ref.shape[0]
    numerators = own_ref[...]
    for ref in got:
        numerators = numerators + ref[:m, :].astype(jnp.float32)
    totals = own_total_ref[...]
    for ref in got:
        terms = ref[m:, :m].astype(jnp.float32)
        totals = totals + jnp.sum(terms, axis=0, keepdims=True)
    step = min(m, BLOCK)
    for k in range(0, m, step):
        total_ref[k : k + step, :] = jnp.broadcast_to(totals[:, k : k + step], (BLOCK, step)).T
    for k in range(0, seed_ref.shape[1], BLOCK):
        labels = mixing * numerators[:, k : k + BLOCK] / total_ref[...] + (
            1.0 - mixing
        ) * seed_ref[:, k : k + BLOCK].astype(jnp.float32)
        panel_ref[:, k : k + BLOCK] = labels.astype(jnp.bfloat16)


def last_update_kernel(seed_ref, own_ref, total_ref, *refs):
    got, out_ref = refs[:-1], refs[-1]
    numerators = own_ref[...]
    for ref in got:
        numerators = numerators + ref[...].astype(jnp.float32)
    for k in range(0, seed_ref.shape[1], BLOCK):
        out_ref[:, k : k + BLOCK] = mixing * numerators[:, k : k + BLOCK] / total_ref[...] + (
            1.0 - mixing
        ) * seed_ref[:, k : k + BLOCK].astype(jnp.float32)


def update(kernel, seeds, own, totals, got, out_shape):
    return pl.pallas_call(
        kernel,
        out_shape=out_shape,
        in_specs=[VMEM] * (3 + len(got)),
        out_specs=jax.tree.map(lambda _: VMEM, out_shape),
        compiler_params=limits(seeds, own, totals, *got, own, own),
    )(seeds, own, totals, *got)


def after(value, *earlier):
    return lax.optimization_barrier((value, *earlier))[0]


def on_device(embeddings, seed_labels, pattern):
    layout = Layout(lax.axis_size("row"), lax.axis_size("col"))
    size = layout.sizes
    m, c = embeddings.shape[0], seed_labels.shape[1]
    sub = min(m, BLOCK)
    other = {k: range(1, size[k]) for k in size}

    def fetch(values, axis, *earlier):
        return [
            layout.fetch(after(v, *earlier), **{axis: k}) for k in other[axis] for v in values
        ]

    t_offsets = [dict(zl=b, x=a) for b in range(size["zl"]) for a in range(size["x"])]
    near_t = [i for i, o in enumerate(t_offsets) if o["x"] == 0 or o["zl"] == 0]
    t_order = near_t + [i for i in range(len(t_offsets)) if i not in near_t]
    t_layout = [(i, 0, m) for i in t_order]
    both = [0] + list(other["core"])
    groups = [
        [(0, a, k) for a in range(size["y"]) for k in both],
        [(b, 0, k) for k in both for b in other["zh"]],
        [(b, a, 0) for a in other["y"] for b in other["zh"]],
        [(b, a, k) for k in other["core"] for a in other["y"] for b in other["zh"]],
    ]
    s_layout = [dict(zh=b, y=a, core=k) for group in groups for b, a, k in group]
    seeds_map = []
    for i, o in enumerate(s_layout):
        if o["zh"] == 0:
            seeds_map.append((i, 0, m, embeddings.shape[1]))
        else:
            stack = len(groups[0]) + o["core"] * (size["zh"] - 1) + o["zh"] - 1
            seeds_map.append((stack, o["y"] * m, m, 0))
    t_parts = [(t_offsets[i], k) for i in t_order for k in range(0, m, sub)]
    s_parts = [(o, k) for o in s_layout for k in range(0, m, sub)]
    place = jnp.stack([lax.axis_index("row"), lax.axis_index("col")]).astype(jnp.int32)
    units = unit_rows(after(embeddings, place))
    packed = pack_rows(units, seed_labels)

    t_pieces, kerns, accs, rects = [], [], [], []
    s_pieces = [None] * len(groups)

    def rectangle(first, last, g0, g1):
        t0, t1 = first * m, last * m
        c0, c1 = (m * sum(len(group) for group in groups[:g]) for g in (g0, g1))
        if t0 == t1 or c0 == c1:
            return []
        kern, acc = gram_call(
            flags,
            t_pieces[first:last],
            [p for g in range(g0, g1) for p in s_pieces[g]],
            sub,
            t0,
            c0,
        )
        kerns.append(kern)
        accs.append(acc)
        rects.append((t0, t1, c0, c1))
        return [acc]

    zh, zl, x = fetch([units], "zh"), fetch([units], "zl"), fetch([units], "x")
    y, own_core = fetch([packed], "y"), fetch([packed], "core")
    flags = flags_call(layout, m, t_parts, s_parts, sub, pattern, place)
    held = stack_seeds(after(seed_labels, flags, *zh), [], 2 * 10**10)
    done = zh + zl + x + y + own_core + [held]
    zh_y, zl_x = fetch(zh, "y", *done), fetch(zl, "x", *done)
    y_core = [fetch([v], "core", *done) for v in y]
    zh_core = fetch(zh, "core", *done)
    seeds_zh = fetch([stack_seeds(held, y)], "zh", *done)
    by_offset = {(0, 0): units}
    by_offset.update({(0, a): v for a, v in zip(other["x"], x)})
    by_offset.update({(b, 0): v for b, v in zip(other["zl"], zl)})
    by_offset.update({(b, a): v for (a, b), v in zip([(a, b) for a in other["x"] for b in other["zl"]], zl_x)})
    t_pieces += [by_offset[t_offsets[i]["zl"], t_offsets[i]["x"]] for i in t_order]
    s_pieces[0] = [packed] + own_core + [p for v, w in zip(y, y_core) for p in [v] + w]
    s_pieces[1] = zh + zh_core
    s_pieces[2] = zh_y
    early, last = len(near_t), len(t_order)
    gram = rectangle(0, early, 0, 1) + rectangle(0, early, 1, 2)
    seeds_zh = [stack_seeds(after(v, *gram), [], 2 * 10**10) for v in seeds_zh]
    done = zh_y + zh_core + gram + seeds_zh
    zh_y_core = fetch(zh_y, "core", *done)
    s_pieces[3] = zh_y_core
    seeds_core = fetch(seeds_zh, "core", *done)
    rectangle(early, last, 0, 3)
    rectangle(0, early, 2, 3)
    rectangle(0, last, 3, 4)
    plan = (m, t_layout, rects)

    def home(values):
        return [
            layout.fetch(v, **{k: -d for k, d in o.items()})
            for v, o in zip(values, t_offsets[1:])
        ]

    def panels(panel):
        far, near = fetch([panel], "zh"), fetch([panel], "y")
        far_y = fetch(far, "y")
        near = [p for v in [panel] + near for p in [v] + fetch([v], "core")]
        return near + far + fetch(far, "core") + far_y + fetch(far_y, "core")

    seeds = s_pieces[0] + seeds_zh + seeds_core
    over_x = tuple(i for i, o in enumerate(t_offsets) if o["x"])
    along = tuple(i for i, o in enumerate(t_offsets) if not o["x"])
    every = tuple(range(len(t_offsets)))
    sent = spread_call(kerns, accs, seeds, c, (*plan, seeds_map, 0, over_x))
    own, totals, *rest = spread_call(kerns, accs, seeds, c, (*plan, seeds_map, 0, along))
    by_piece = dict(zip(over_x + along[1:], list(sent) + rest))
    others = [by_piece[i] for i in every[1:]]
    panel, totals = update(
        first_update_kernel,
        held,
        own,
        totals,
        home(others),
        [
            jax.ShapeDtypeStruct((m, c), jnp.bfloat16),
            jax.ShapeDtypeStruct((m, BLOCK), jnp.float32),
        ],
    )
    pieces = panels(panel)
    first = len(groups[0]) + len(groups[1])
    base = base_call(kerns, pieces[:first], t_layout, rects)
    rest = [(i, 0, m, 0) for i in range(len(pieces) - first)]
    own, *others = spread_call(kerns, [], pieces[first:], c, (*plan, rest, first * m, every), [base])
    return update(
        last_update_kernel,
        held,
        own,
        totals,
        home(others),
        jax.ShapeDtypeStruct((m, c), jnp.float32),
    )


def solution(mesh):
    return jax.shard_map(
        on_device,
        mesh=mesh,
        in_specs=(P(("col", "row"), None), P(("col", "row"), None), P()),
        out_specs=P(("col", "row"), None),
        check_vma=False,
    )
```

```python
import functools
import math

import jax
import jax.numpy as jnp
from jax import lax
from jax.experimental import pallas as pl
from jax.experimental.pallas import tpu as pltpu
from jax.sharding import PartitionSpec as P

BLOCK = 128
AXES = ("row", "col")

sharpness = 30.0
mixing = 0.8
epsilon = 1e-06


def split_two(n):
    low = max(d for d in range(1, math.isqrt(n) + 1) if n % d == 0)
    return n // low, low


class Layout:
    def __init__(self, rows, cols):
        core = 2 if cols % 2 == 0 else 1
        ny, nx = split_two(rows)
        nzh, nzl = split_two(cols // core)
        self.sizes = dict(y=ny, x=nx, zh=nzh, zl=nzl, core=core)
        self.rows, self.cols = rows, cols

    def coords(self, row, col):
        s = self.sizes
        return dict(
            y=row // s["x"],
            x=row % s["x"],
            zh=col // (s["zl"] * s["core"]),
            zl=col // s["core"] % s["zl"],
            core=col % s["core"],
        )

    def moved(self, at, offset):
        return {k: (at[k] + offset.get(k, 0)) % self.sizes[k] for k in at}

    def row_col(self, at):
        s = self.sizes
        return at["y"] * s["x"] + at["x"], (at["zh"] * s["zl"] + at["zl"]) * s["core"] + at["core"]

    def fetch(self, value, **offset):
        if all(v % self.sizes[k] == 0 for k, v in offset.items()):
            return value
        pairs = []
        for row in range(self.rows):
            for col in range(self.cols):
                r, c = self.row_col(self.moved(self.coords(row, col), offset))
                pairs.append((r * self.cols + c, row * self.cols + col))
        return lax.ppermute(value, AXES, pairs)

    def device(self, offset):
        at = self.coords(lax.axis_index("row"), lax.axis_index("col"))
        row, col = self.row_col(self.moved(at, offset))
        return col * self.rows + row


VMEM = pl.BlockSpec(memory_space=pltpu.VMEM)


def limits(*arrays, mib=3):
    total = sum(max(math.prod(a.shape), 8 * BLOCK) * a.dtype.itemsize for a in arrays)
    return pltpu.CompilerParams(vmem_limit_bytes=total * 5 // 4 + mib * 2**20)


def shape(dims, dtype=jnp.bfloat16):
    return jax.ShapeDtypeStruct(dims, dtype)


def unit_of(values):
    values = values.astype(jnp.float32)
    mean_square = jnp.mean(values * values, axis=1, keepdims=True)
    scaled = values * lax.rsqrt(mean_square + epsilon) * values.shape[1] ** (-0.5)
    return scaled.astype(jnp.bfloat16)


def unit_kernel(emb_ref, unit_ref):
    unit_ref[...] = unit_of(emb_ref[...])


def unit_rows(embeddings):
    out = shape(embeddings.shape)
    return pl.pallas_call(
        unit_kernel,
        out_shape=out,
        in_specs=[VMEM],
        out_specs=VMEM,
        compiler_params=limits(*[out] * 4),
    )(embeddings)


def pack_kernel(unit_ref, seed_ref, packed_ref):
    d = unit_ref.shape[1]
    packed_ref[:, :d] = unit_ref[...]
    packed_ref[:, d:] = seed_ref[...]


def pack_rows(units, seeds):
    out = shape((units.shape[0], units.shape[1] + seeds.shape[1]))
    return pl.pallas_call(
        pack_kernel,
        out_shape=out,
        in_specs=[VMEM] * 2,
        out_specs=VMEM,
        compiler_params=limits(out, out),
    )(units, seeds)


def stack_kernel(seed_ref, *refs):
    *packed, out_ref = refs
    m, c = seed_ref.shape
    out_ref[:m, :] = seed_ref[...]
    for k, ref in enumerate(packed):
        out_ref[(k + 1) * m : (k + 2) * m, :] = ref[:, ref.shape[1] - c :]


def stack_seeds(seeds, packed, work=0):
    m, c = seeds.shape
    out = shape(((len(packed) + 1) * m, c))
    return pl.pallas_call(
        stack_kernel,
        out_shape=out,
        in_specs=[VMEM] * (len(packed) + 1),
        out_specs=VMEM,
        compiler_params=limits(seeds, *packed, out),
        cost_estimate=pl.CostEstimate(flops=work, bytes_accessed=2 * m * c, transcendentals=0),
    )(seeds, *packed)


def flags_kernel(layout, m, t_parts, s_parts, unit, place_ref, pattern_ref, out_ref, block_ref):
    at = layout.coords(place_ref[0], place_ref[1])

    def block(offset, start):
        row, col = layout.row_col(layout.moved(at, offset))
        return ((col * layout.rows + row) * m + start) // BLOCK

    for k, (offset, start) in enumerate(s_parts):
        block_ref[:, k * unit : (k + 1) * unit] = jnp.full((1, unit), block(offset, start), jnp.int32)
    blocks = block_ref[...]
    for r, (offset, start) in enumerate(t_parts):
        target = block(offset, start)
        hits = blocks == pattern_ref[0, target]
        for k in range(1, pattern_ref.shape[0]):
            hits = hits | (blocks == pattern_ref[k, target])
        out_ref[r : r + 1, :] = jnp.where(hits, 1, 0)


def flags_call(layout, m, t_parts, s_parts, unit, pattern, place):
    out = shape((len(t_parts), len(s_parts) * unit), jnp.int32)
    smem = pl.BlockSpec(memory_space=pltpu.SMEM)
    return pl.pallas_call(
        functools.partial(flags_kernel, layout, m, t_parts, s_parts, unit),
        out_shape=out,
        in_specs=[smem] * 2,
        out_specs=VMEM,
        scratch_shapes=[pltpu.VMEM((1, out.shape[1]), jnp.int32)],
        compiler_params=limits(out, out),
        cost_estimate=pl.CostEstimate(flops=10**7, bytes_accessed=2**20, transcendentals=0),
    )(place, pattern.T)


def tiles_of(refs, scratch, d):
    tiles, held = [], 0
    for ref in refs:
        rows = ref.shape[0]
        if rows % (2 * BLOCK) == 0:
            tiles += [(ref, k, 2 * BLOCK) for k in range(0, rows, 2 * BLOCK)]
        else:
            scratch[held : held + rows, :] = ref[:, :d]
            held += rows
    k = 0
    while k < held:
        rows = next(w for w in (2 * BLOCK, BLOCK, BLOCK // 2) if held - k >= w)
        tiles.append((scratch, k, rows))
        k += rows
    return tiles


def gram_kernel(nt, ns, sub, d, t_first, s_first, flags, *refs):
    t_in, s_in, refs = refs[:nt], refs[nt : nt + ns], refs[nt + ns :]
    kern, acc, t_join, s_join = refs
    t_tiles, s_tiles = tiles_of(t_in, t_join, d), tiles_of(s_in, s_join, d)
    rows, cols = kern.shape
    col = 0
    for s_ref, s_at, width in s_tiles:
        row = 0
        for t_ref, t_at, tall in t_tiles:
            scores = lax.dot_general(
                t_ref[t_at : t_at + tall, :],
                s_ref[s_at : s_at + width, :d],
                (((1,), (1,)), ((), ())),
                preferred_element_type=jnp.float32,
            )
            value = jnp.exp(sharpness * scores).astype(jnp.bfloat16).astype(jnp.float32)
            for a in range(tall // sub):
                at = row + a * sub
                flag = flags[
                    (t_first + at) // sub : (t_first + at) // sub + 1,
                    s_first + col : s_first + col + width,
                ]
                part = jnp.where(flag > 0, value[a * sub : (a + 1) * sub], 0.0)
                kern[at : at + sub, col : col + width] = part.astype(jnp.bfloat16)
                if width % BLOCK:
                    if col == 0:
                        acc[at : at + sub, :] = jnp.zeros((sub, BLOCK), jnp.float32)
                    acc[at : at + sub, :width] += part
                    continue
                total = part[:, :BLOCK]
                for b in range(1, width // BLOCK):
                    total = total + part[:, b * BLOCK : (b + 1) * BLOCK]
                if col > 0:
                    total = total + acc[at : at + sub, :]
                acc[at : at + sub, :] = total
            row += tall
        col += width


def gram_call(flags, t_pieces, s_pieces, sub, t_first, s_first):
    rows, cols = (sum(p.shape[0] for p in pieces) for pieces in (t_pieces, s_pieces))
    d = t_pieces[0].shape[1]
    join = [
        shape((max(16, sum(p.shape[0] for p in pieces if p.shape[0] % (2 * BLOCK))), d))
        for pieces in (t_pieces, s_pieces)
    ]
    outs = [shape((rows, cols)), shape((rows, BLOCK), jnp.float32)]
    return pl.pallas_call(
        functools.partial(
            gram_kernel, len(t_pieces), len(s_pieces), sub, d, t_first, s_first
        ),
        out_shape=outs,
        in_specs=[VMEM] * (1 + len(t_pieces) + len(s_pieces)),
        out_specs=[VMEM] * 2,
        scratch_shapes=[pltpu.VMEM(j.shape, j.dtype) for j in join],
        compiler_params=limits(flags, *t_pieces, *s_pieces, *outs, *join),
        cost_estimate=pl.CostEstimate(
            flops=2 * rows * cols * d,
            bytes_accessed=2 * (rows + cols) * d,
            transcendentals=rows * cols,
        ),
    )(flags, *t_pieces, *s_pieces)


def row_sums(kerns, rects, pcat, row, rows, lo, hi):
    part = None
    for kern, (t0, t1, c0, c1) in zip(kerns, rects):
        first, last = max(c0, lo), min(c1, hi)
        if t0 <= row < t1 and first < last:
            term = jnp.dot(
                kern[row - t0 : row - t0 + rows, first - c0 : last - c0],
                pcat[first - lo : last - lo, :],
                preferred_element_type=jnp.float32,
            )
            part = term if part is None else part + term
    return part


def base_kernel(t_layout, rects, nk, *refs):
    kerns, p_in, (out_ref, pcat) = refs[:nk], refs[nk:-2], refs[-2:]
    at = 0
    for ref in p_in:
        pcat[at : at + ref.shape[0], :] = ref[...]
        at += ref.shape[0]
    row = 0
    for _, _, rows in t_layout:
        out_ref[row : row + rows, :] = row_sums(kerns, rects, pcat, row, rows, 0, at)
        row += rows


def base_call(kerns, p_pieces, t_layout, rects):
    m, c = p_pieces[0].shape
    rows, cols = sum(r for _, _, r in t_layout), m * len(p_pieces)
    out = shape((rows, c), jnp.float32)
    return pl.pallas_call(
        functools.partial(base_kernel, t_layout, rects, len(kerns)),
        out_shape=out,
        in_specs=[VMEM] * (len(kerns) + len(p_pieces)),
        out_specs=VMEM,
        scratch_shapes=[pltpu.VMEM((cols, c), jnp.bfloat16)],
        compiler_params=limits(*kerns, *p_pieces, out, shape((cols, c))),
        cost_estimate=pl.CostEstimate(
            flops=2 * rows * cols * c, bytes_accessed=2 * rows * cols, transcendentals=0
        ),
    )(*kerns, *p_pieces)


def spread_kernel(plan, nk, na, ns, *refs):
    m, t_layout, rects, p_map, lo, chosen = plan
    kerns, refs = refs[:nk], refs[nk:]
    base, refs = (refs[0], refs[1:]) if lo else (None, refs)
    accs, refs = refs[:na], refs[na:]
    p_in, refs = refs[:ns], refs[ns:]
    outs, pcat = refs[:-1], refs[-1]
    owned = (2 if na else 1) if 0 in chosen else 0
    own_ref = outs[0]
    other_refs = dict(zip([p for p in chosen if p], outs[owned:]))
    c = pcat.shape[1]
    at = 0
    for index, start, rows, lane in p_map:
        pcat[at : at + rows, :] = p_in[index][start : start + rows, lane : lane + c]
        at += rows
    row = 0
    for piece, start, rows in t_layout:
        if piece not in chosen:
            row += rows
            continue
        part = row_sums(kerns, rects, pcat, row, rows, lo, lo + pcat.shape[0])
        if lo:
            part = part + base[row : row + rows, :]
        if piece == 0:
            own_ref[start : start + rows, :] = part
        else:
            other_refs[piece][start : start + rows, :] = part.astype(jnp.bfloat16)
        step = math.gcd(rows, BLOCK)
        for lane in range(0, rows if na else 0, step):
            total = None
            for acc, (t0, t1, c0, c1) in zip(accs, rects):
                if t0 <= row < t1:
                    first = row - t0 + lane
                    term = acc[first : first + step, :]
                    total = term if total is None else total + term
            total = jnp.sum(total.T, axis=0, keepdims=True)
            lanes = slice(start + lane, start + lane + step)
            if piece == 0:
                outs[1][:, lanes] = total
            else:
                high = total.astype(jnp.bfloat16).astype(jnp.float32)
                mid = (total - high).astype(jnp.bfloat16).astype(jnp.float32)
                low = total - high - mid
                index = lax.broadcasted_iota(jnp.int32, (16, step), 0)
                terms = jnp.where(index == 0, high, jnp.where(index == 1, mid, low))
                terms = jnp.where(index < 3, terms, 0.0)
                other_refs[piece][m:, lanes] = terms.astype(jnp.bfloat16)
        row += rows


def spread_call(kerns, accs, p_pieces, c, plan, base=()):
    m, t_layout, rects, p_map, lo, chosen = plan
    nt = len(chosen)
    cols = sum(rows for _, _, rows, _ in p_map)
    extra = 16 if accs else 0
    outs = []
    if 0 in chosen:
        outs.append(shape((m, c), jnp.float32))
        if accs:
            outs.append(shape((1, m), jnp.float32))
    outs += [shape((m + extra, c)) for p in chosen if p]
    return pl.pallas_call(
        functools.partial(spread_kernel, plan, len(kerns), len(accs), len(p_pieces)),
        out_shape=outs,
        in_specs=[VMEM] * (len(kerns) + len(base) + len(accs) + len(p_pieces)),
        out_specs=[VMEM] * len(outs),
        scratch_shapes=[pltpu.VMEM((cols, c), jnp.bfloat16)],
        compiler_params=limits(*kerns, *base, *accs, *p_pieces, *outs, shape((cols, c))),
        cost_estimate=pl.CostEstimate(
            flops=2 * nt * m * cols * c,
            bytes_accessed=2 * (nt * m * cols + cols * c),
            transcendentals=0,
        ),
    )(*kerns, *base, *accs, *p_pieces)


def first_update_kernel(seed_ref, own_ref, own_total_ref, *refs):
    got, (panel_ref, total_ref) = refs[:-2], refs[-2:]
    m = seed_ref.shape[0]
    numerators = own_ref[...]
    for ref in got:
        numerators = numerators + ref[:m, :].astype(jnp.float32)
    totals = own_total_ref[...]
    for ref in got:
        terms = ref[m:, :m].astype(jnp.float32)
        totals = totals + jnp.sum(terms, axis=0, keepdims=True)
    step = min(m, BLOCK)
    for k in range(0, m, step):
        total_ref[k : k + step, :] = jnp.broadcast_to(totals[:, k : k + step], (BLOCK, step)).T
    for k in range(0, seed_ref.shape[1], BLOCK):
        labels = mixing * numerators[:, k : k + BLOCK] / total_ref[...] + (
            1.0 - mixing
        ) * seed_ref[:, k : k + BLOCK].astype(jnp.float32)
        panel_ref[:, k : k + BLOCK] = labels.astype(jnp.bfloat16)


def last_update_kernel(seed_ref, own_ref, total_ref, *refs):
    got, out_ref = refs[:-1], refs[-1]
    numerators = own_ref[...]
    for ref in got:
        numerators = numerators + ref[...].astype(jnp.float32)
    for k in range(0, seed_ref.shape[1], BLOCK):
        out_ref[:, k : k + BLOCK] = mixing * numerators[:, k : k + BLOCK] / total_ref[...] + (
            1.0 - mixing
        ) * seed_ref[:, k : k + BLOCK].astype(jnp.float32)


def update(kernel, seeds, own, totals, got, out_shape):
    return pl.pallas_call(
        kernel,
        out_shape=out_shape,
        in_specs=[VMEM] * (3 + len(got)),
        out_specs=jax.tree.map(lambda _: VMEM, out_shape),
        compiler_params=limits(seeds, own, totals, *got, own, own),
    )(seeds, own, totals, *got)


def after(value, *earlier):
    return lax.optimization_barrier((value, *earlier))[0]


def on_device(embeddings, seed_labels, pattern):
    layout = Layout(lax.axis_size("row"), lax.axis_size("col"))
    size = layout.sizes
    m, c = embeddings.shape[0], seed_labels.shape[1]
    sub = min(m, BLOCK)
    other = {k: range(1, size[k]) for k in size}

    def fetch(values, axis, *earlier):
        return [
            layout.fetch(after(v, *earlier), **{axis: k}) for k in other[axis] for v in values
        ]

    t_offsets = [dict(zl=b, x=a) for b in range(size["zl"]) for a in range(size["x"])]
    near_t = [i for i, o in enumerate(t_offsets) if o["x"] == 0 or o["zl"] == 0]
    t_order = near_t + [i for i in range(len(t_offsets)) if i not in near_t]
    t_layout = [(i, 0, m) for i in t_order]
    both = [0] + list(other["core"])
    groups = [
        [(0, a, k) for a in range(size["y"]) for k in both],
        [(b, 0, k) for k in both for b in other["zh"]],
        [(b, a, 0) for a in other["y"] for b in other["zh"]],
        [(b, a, k) for k in other["core"] for a in other["y"] for b in other["zh"]],
    ]
    s_layout = [dict(zh=b, y=a, core=k) for group in groups for b, a, k in group]
    seeds_map = []
    for i, o in enumerate(s_layout):
        if o["zh"] == 0:
            seeds_map.append((i, 0, m, embeddings.shape[1]))
        else:
            stack = len(groups[0]) + o["core"] * (size["zh"] - 1) + o["zh"] - 1
            seeds_map.append((stack, o["y"] * m, m, 0))
    t_parts = [(t_offsets[i], k) for i in t_order for k in range(0, m, sub)]
    s_parts = [(o, k) for o in s_layout for k in range(0, m, sub)]
    place = jnp.stack([lax.axis_index("row"), lax.axis_index("col")]).astype(jnp.int32)
    units = unit_rows(after(embeddings, place))
    packed = pack_rows(units, seed_labels)

    t_pieces, kerns, accs, rects = [], [], [], []
    s_pieces = [None] * len(groups)

    def rectangle(first, last, g0, g1):
        t0, t1 = first * m, last * m
        c0, c1 = (m * sum(len(group) for group in groups[:g]) for g in (g0, g1))
        if t0 == t1 or c0 == c1:
            return []
        kern, acc = gram_call(
            flags,
            t_pieces[first:last],
            [p for g in range(g0, g1) for p in s_pieces[g]],
            sub,
            t0,
            c0,
        )
        kerns.append(kern)
        accs.append(acc)
        rects.append((t0, t1, c0, c1))
        return [acc]

    zh, zl, x = fetch([units], "zh"), fetch([units], "zl"), fetch([units], "x")
    y, own_core = fetch([packed], "y"), fetch([packed], "core")
    flags = flags_call(layout, m, t_parts, s_parts, sub, pattern, place)
    held = stack_seeds(after(seed_labels, flags, *zh), [], 2 * 10**10)
    done = zh + zl + x + y + own_core + [held]
    zh_y, zl_x = fetch(zh, "y", *done), fetch(zl, "x", *done)
    y_core = [fetch([v], "core", *done) for v in y]
    zh_core = fetch(zh, "core", *done)
    seeds_zh = fetch([stack_seeds(held, y)], "zh", *done)
    by_offset = {(0, 0): units}
    by_offset.update({(0, a): v for a, v in zip(other["x"], x)})
    by_offset.update({(b, 0): v for b, v in zip(other["zl"], zl)})
    by_offset.update({(b, a): v for (a, b), v in zip([(a, b) for a in other["x"] for b in other["zl"]], zl_x)})
    t_pieces += [by_offset[t_offsets[i]["zl"], t_offsets[i]["x"]] for i in t_order]
    s_pieces[0] = [packed] + own_core + [p for v, w in zip(y, y_core) for p in [v] + w]
    s_pieces[1] = zh + zh_core
    early, last = len(near_t), len(t_order)
    gram = rectangle(0, early, 0, 1) + rectangle(0, early, 1, 2)
    done = zh_y + zh_core + gram
    s_pieces[2] = [after(v, *gram) for v in zh_y]
    zh_y_core = fetch(zh_y, "core", *done)
    s_pieces[3] = zh_y_core
    seeds_in = seeds_zh
    gram = rectangle(0, early, 2, 3)
    seeds_zh = [stack_seeds(after(v, *gram), [], 2 * 10**10) for v in seeds_in]
    seeds_core = fetch(seeds_zh, "core")
    rectangle(early, last, 0, 3)
    rectangle(0, last, 3, 4)
    plan = (m, t_layout, rects)

    def home(values):
        return [
            layout.fetch(v, **{k: -d for k, d in o.items()})
            for v, o in zip(values, t_offsets[1:])
        ]

    def panels(panel):
        far, near = fetch([panel], "zh"), fetch([panel], "y")
        far_y = fetch(far, "y")
        near = [p for v in [panel] + near for p in [v] + fetch([v], "core")]
        return near + far + fetch(far, "core") + far_y + fetch(far_y, "core")

    seeds = s_pieces[0] + seeds_zh + seeds_core
    over_x = tuple(i for i, o in enumerate(t_offsets) if o["x"])
    along = tuple(i for i, o in enumerate(t_offsets) if not o["x"])
    every = tuple(range(len(t_offsets)))
    sent = spread_call(kerns, accs, seeds, c, (*plan, seeds_map, 0, over_x))
    own, totals, *rest = spread_call(kerns, accs, seeds, c, (*plan, seeds_map, 0, along))
    by_piece = dict(zip(over_x + along[1:], list(sent) + rest))
    others = [by_piece[i] for i in every[1:]]
    panel, totals = update(
        first_update_kernel,
        held,
        own,
        totals,
        home(others),
        [
            jax.ShapeDtypeStruct((m, c), jnp.bfloat16),
            jax.ShapeDtypeStruct((m, BLOCK), jnp.float32),
        ],
    )
    pieces = panels(panel)
    first = len(groups[0]) + len(groups[1])
    base = base_call(kerns, pieces[:first], t_layout, rects)
    rest = [(i, 0, m, 0) for i in range(len(pieces) - first)]
    own, *others = spread_call(kerns, [], pieces[first:], c, (*plan, rest, first * m, every), [base])
    return update(
        last_update_kernel,
        held,
        own,
        totals,
        home(others),
        jax.ShapeDtypeStruct((m, c), jnp.float32),
    )


def solution(mesh):
    return jax.shard_map(
        on_device,
        mesh=mesh,
        in_specs=(P(("col", "row"), None), P(("col", "row"), None), P()),
        out_specs=P(("col", "row"), None),
        check_vma=False,
    )
```

```python
import functools
import math

import jax
import jax.numpy as jnp
from jax import lax
from jax.experimental import pallas as pl
from jax.experimental.pallas import tpu as pltpu
from jax.sharding import PartitionSpec as P

BLOCK = 128
AXES = ("row", "col")

sharpness = 30.0
mixing = 0.8
epsilon = 1e-06


def split_two(n):
    low = max(d for d in range(1, math.isqrt(n) + 1) if n % d == 0)
    return n // low, low


class Layout:
    def __init__(self, rows, cols):
        core = 2 if cols % 2 == 0 else 1
        ny, nx = split_two(rows)
        nzh, nzl = split_two(cols // core)
        self.sizes = dict(y=ny, x=nx, zh=nzh, zl=nzl, core=core)
        self.rows, self.cols = rows, cols

    def coords(self, row, col):
        s = self.sizes
        return dict(
            y=row // s["x"],
            x=row % s["x"],
            zh=col // (s["zl"] * s["core"]),
            zl=col // s["core"] % s["zl"],
            core=col % s["core"],
        )

    def moved(self, at, offset):
        return {k: (at[k] + offset.get(k, 0)) % self.sizes[k] for k in at}

    def row_col(self, at):
        s = self.sizes
        return at["y"] * s["x"] + at["x"], (at["zh"] * s["zl"] + at["zl"]) * s["core"] + at["core"]

    def fetch(self, value, **offset):
        if all(v % self.sizes[k] == 0 for k, v in offset.items()):
            return value
        pairs = []
        for row in range(self.rows):
            for col in range(self.cols):
                r, c = self.row_col(self.moved(self.coords(row, col), offset))
                pairs.append((r * self.cols + c, row * self.cols + col))
        return lax.ppermute(value, AXES, pairs)

    def device(self, offset):
        at = self.coords(lax.axis_index("row"), lax.axis_index("col"))
        row, col = self.row_col(self.moved(at, offset))
        return col * self.rows + row


VMEM = pl.BlockSpec(memory_space=pltpu.VMEM)


def limits(*arrays, mib=3):
    total = sum(max(math.prod(a.shape), 8 * BLOCK) * a.dtype.itemsize for a in arrays)
    return pltpu.CompilerParams(vmem_limit_bytes=total * 5 // 4 + mib * 2**20)


def shape(dims, dtype=jnp.bfloat16):
    return jax.ShapeDtypeStruct(dims, dtype)


def unit_of(values):
    values = values.astype(jnp.float32)
    mean_square = jnp.mean(values * values, axis=1, keepdims=True)
    scaled = values * lax.rsqrt(mean_square + epsilon) * values.shape[1] ** (-0.5)
    return scaled.astype(jnp.bfloat16)


def unit_kernel(emb_ref, unit_ref):
    unit_ref[...] = unit_of(emb_ref[...])


def unit_rows(embeddings):
    out = shape(embeddings.shape)
    return pl.pallas_call(
        unit_kernel,
        out_shape=out,
        in_specs=[VMEM],
        out_specs=VMEM,
        compiler_params=limits(*[out] * 4),
    )(embeddings)


def pack_kernel(unit_ref, seed_ref, packed_ref):
    d = unit_ref.shape[1]
    packed_ref[:, :d] = unit_ref[...]
    packed_ref[:, d:] = seed_ref[...]


def pack_rows(units, seeds):
    out = shape((units.shape[0], units.shape[1] + seeds.shape[1]))
    return pl.pallas_call(
        pack_kernel,
        out_shape=out,
        in_specs=[VMEM] * 2,
        out_specs=VMEM,
        compiler_params=limits(out, out),
    )(units, seeds)


def stack_kernel(seed_ref, *refs):
    *packed, out_ref = refs
    m, c = seed_ref.shape
    out_ref[:m, :] = seed_ref[...]
    for k, ref in enumerate(packed):
        out_ref[(k + 1) * m : (k + 2) * m, :] = ref[:, ref.shape[1] - c :]


def stack_seeds(seeds, packed, work=0):
    m, c = seeds.shape
    out = shape(((len(packed) + 1) * m, c))
    return pl.pallas_call(
        stack_kernel,
        out_shape=out,
        in_specs=[VMEM] * (len(packed) + 1),
        out_specs=VMEM,
        compiler_params=limits(seeds, *packed, out),
        cost_estimate=pl.CostEstimate(flops=work, bytes_accessed=2 * m * c, transcendentals=0),
    )(seeds, *packed)


def flags_kernel(layout, m, t_parts, s_parts, unit, place_ref, pattern_ref, out_ref, block_ref):
    at = layout.coords(place_ref[0], place_ref[1])

    def block(offset, start):
        row, col = layout.row_col(layout.moved(at, offset))
        return ((col * layout.rows + row) * m + start) // BLOCK

    for k, (offset, start) in enumerate(s_parts):
        block_ref[:, k * unit : (k + 1) * unit] = jnp.full((1, unit), block(offset, start), jnp.int32)
    blocks = block_ref[...]
    for r, (offset, start) in enumerate(t_parts):
        target = block(offset, start)
        hits = blocks == pattern_ref[0, target]
        for k in range(1, pattern_ref.shape[0]):
            hits = hits | (blocks == pattern_ref[k, target])
        out_ref[r : r + 1, :] = jnp.where(hits, 1, 0)


def flags_call(layout, m, t_parts, s_parts, unit, pattern, place):
    out = shape((len(t_parts), len(s_parts) * unit), jnp.int32)
    smem = pl.BlockSpec(memory_space=pltpu.SMEM)
    return pl.pallas_call(
        functools.partial(flags_kernel, layout, m, t_parts, s_parts, unit),
        out_shape=out,
        in_specs=[smem] * 2,
        out_specs=VMEM,
        scratch_shapes=[pltpu.VMEM((1, out.shape[1]), jnp.int32)],
        compiler_params=limits(out, out),
        cost_estimate=pl.CostEstimate(flops=10**7, bytes_accessed=2**20, transcendentals=0),
    )(place, pattern.T)


def tiles_of(refs, scratch, d):
    tiles, held = [], 0
    for ref in refs:
        rows = ref.shape[0]
        if rows % (2 * BLOCK) == 0:
            tiles += [(ref, k, 2 * BLOCK) for k in range(0, rows, 2 * BLOCK)]
        else:
            scratch[held : held + rows, :] = ref[:, :d]
            held += rows
    k = 0
    while k < held:
        rows = next(w for w in (2 * BLOCK, BLOCK, BLOCK // 2) if held - k >= w)
        tiles.append((scratch, k, rows))
        k += rows
    return tiles


def gram_kernel(nt, ns, sub, d, t_first, s_first, flags, *refs):
    t_in, s_in, refs = refs[:nt], refs[nt : nt + ns], refs[nt + ns :]
    kern, acc, t_join, s_join = refs
    t_tiles, s_tiles = tiles_of(t_in, t_join, d), tiles_of(s_in, s_join, d)
    rows, cols = kern.shape
    col = 0
    for s_ref, s_at, width in s_tiles:
        row = 0
        for t_ref, t_at, tall in t_tiles:
            scores = lax.dot_general(
                t_ref[t_at : t_at + tall, :],
                s_ref[s_at : s_at + width, :d],
                (((1,), (1,)), ((), ())),
                preferred_element_type=jnp.float32,
            )
            value = jnp.exp(sharpness * scores).astype(jnp.bfloat16).astype(jnp.float32)
            for a in range(tall // sub):
                at = row + a * sub
                flag = flags[
                    (t_first + at) // sub : (t_first + at) // sub + 1,
                    s_first + col : s_first + col + width,
                ]
                part = jnp.where(flag > 0, value[a * sub : (a + 1) * sub], 0.0)
                kern[at : at + sub, col : col + width] = part.astype(jnp.bfloat16)
                if width % BLOCK:
                    if col == 0:
                        acc[at : at + sub, :] = jnp.zeros((sub, BLOCK), jnp.float32)
                    acc[at : at + sub, :width] += part
                    continue
                total = part[:, :BLOCK]
                for b in range(1, width // BLOCK):
                    total = total + part[:, b * BLOCK : (b + 1) * BLOCK]
                if col > 0:
                    total = total + acc[at : at + sub, :]
                acc[at : at + sub, :] = total
            row += tall
        col += width


def gram_call(flags, t_pieces, s_pieces, sub, t_first, s_first):
    rows, cols = (sum(p.shape[0] for p in pieces) for pieces in (t_pieces, s_pieces))
    d = t_pieces[0].shape[1]
    join = [
        shape((max(16, sum(p.shape[0] for p in pieces if p.shape[0] % (2 * BLOCK))), d))
        for pieces in (t_pieces, s_pieces)
    ]
    outs = [shape((rows, cols)), shape((rows, BLOCK), jnp.float32)]
    return pl.pallas_call(
        functools.partial(
            gram_kernel, len(t_pieces), len(s_pieces), sub, d, t_first, s_first
        ),
        out_shape=outs,
        in_specs=[VMEM] * (1 + len(t_pieces) + len(s_pieces)),
        out_specs=[VMEM] * 2,
        scratch_shapes=[pltpu.VMEM(j.shape, j.dtype) for j in join],
        compiler_params=limits(flags, *t_pieces, *s_pieces, *outs, *join),
        cost_estimate=pl.CostEstimate(
            flops=2 * rows * cols * d,
            bytes_accessed=2 * (rows + cols) * d,
            transcendentals=rows * cols,
        ),
    )(flags, *t_pieces, *s_pieces)


def row_sums(kerns, rects, pcat, row, rows, lo, hi):
    part = None
    for kern, (t0, t1, c0, c1) in zip(kerns, rects):
        first, last = max(c0, lo), min(c1, hi)
        if t0 <= row < t1 and first < last:
            term = jnp.dot(
                kern[row - t0 : row - t0 + rows, first - c0 : last - c0],
                pcat[first - lo : last - lo, :],
                preferred_element_type=jnp.float32,
            )
            part = term if part is None else part + term
    return part


def base_kernel(t_layout, rects, nk, *refs):
    kerns, p_in, (out_ref, pcat) = refs[:nk], refs[nk:-2], refs[-2:]
    at = 0
    for ref in p_in:
        pcat[at : at + ref.shape[0], :] = ref[...]
        at += ref.shape[0]
    row = 0
    for _, _, rows in t_layout:
        out_ref[row : row + rows, :] = row_sums(kerns, rects, pcat, row, rows, 0, at)
        row += rows


def base_call(kerns, p_pieces, t_layout, rects):
    m, c = p_pieces[0].shape
    rows, cols = sum(r for _, _, r in t_layout), m * len(p_pieces)
    out = shape((rows, c), jnp.float32)
    return pl.pallas_call(
        functools.partial(base_kernel, t_layout, rects, len(kerns)),
        out_shape=out,
        in_specs=[VMEM] * (len(kerns) + len(p_pieces)),
        out_specs=VMEM,
        scratch_shapes=[pltpu.VMEM((cols, c), jnp.bfloat16)],
        compiler_params=limits(*kerns, *p_pieces, out, shape((cols, c))),
        cost_estimate=pl.CostEstimate(
            flops=2 * rows * cols * c, bytes_accessed=2 * rows * cols, transcendentals=0
        ),
    )(*kerns, *p_pieces)


def spread_kernel(plan, nk, na, ns, *refs):
    m, t_layout, rects, p_map, lo, chosen = plan
    kerns, refs = refs[:nk], refs[nk:]
    base, refs = (refs[0], refs[1:]) if lo else (None, refs)
    accs, refs = refs[:na], refs[na:]
    p_in, refs = refs[:ns], refs[ns:]
    outs, pcat = refs[:-1], refs[-1]
    owned = (2 if na else 1) if 0 in chosen else 0
    own_ref = outs[0]
    other_refs = dict(zip([p for p in chosen if p], outs[owned:]))
    c = pcat.shape[1]
    at = 0
    for index, start, rows, lane in p_map:
        pcat[at : at + rows, :] = p_in[index][start : start + rows, lane : lane + c]
        at += rows
    row = 0
    for piece, start, rows in t_layout:
        if piece not in chosen:
            row += rows
            continue
        part = row_sums(kerns, rects, pcat, row, rows, lo, lo + pcat.shape[0])
        if lo:
            part = part + base[row : row + rows, :]
        if piece == 0:
            own_ref[start : start + rows, :] = part
        else:
            other_refs[piece][start : start + rows, :] = part.astype(jnp.bfloat16)
        step = math.gcd(rows, BLOCK)
        for lane in range(0, rows if na else 0, step):
            total = None
            for acc, (t0, t1, c0, c1) in zip(accs, rects):
                if t0 <= row < t1:
                    first = row - t0 + lane
                    term = acc[first : first + step, :]
                    total = term if total is None else total + term
            total = jnp.sum(total.T, axis=0, keepdims=True)
            lanes = slice(start + lane, start + lane + step)
            if piece == 0:
                outs[1][:, lanes] = total
            else:
                high = total.astype(jnp.bfloat16).astype(jnp.float32)
                mid = (total - high).astype(jnp.bfloat16).astype(jnp.float32)
                low = total - high - mid
                index = lax.broadcasted_iota(jnp.int32, (16, step), 0)
                terms = jnp.where(index == 0, high, jnp.where(index == 1, mid, low))
                terms = jnp.where(index < 3, terms, 0.0)
                other_refs[piece][m:, lanes] = terms.astype(jnp.bfloat16)
        row += rows


def spread_call(kerns, accs, p_pieces, c, plan, base=()):
    m, t_layout, rects, p_map, lo, chosen = plan
    nt = len(chosen)
    cols = sum(rows for _, _, rows, _ in p_map)
    extra = 16 if accs else 0
    outs = []
    if 0 in chosen:
        outs.append(shape((m, c), jnp.float32))
        if accs:
            outs.append(shape((1, m), jnp.float32))
    outs += [shape((m + extra, c)) for p in chosen if p]
    return pl.pallas_call(
        functools.partial(spread_kernel, plan, len(kerns), len(accs), len(p_pieces)),
        out_shape=outs,
        in_specs=[VMEM] * (len(kerns) + len(base) + len(accs) + len(p_pieces)),
        out_specs=[VMEM] * len(outs),
        scratch_shapes=[pltpu.VMEM((cols, c), jnp.bfloat16)],
        compiler_params=limits(*kerns, *base, *accs, *p_pieces, *outs, shape((cols, c))),
        cost_estimate=pl.CostEstimate(
            flops=2 * nt * m * cols * c,
            bytes_accessed=2 * (nt * m * cols + cols * c),
            transcendentals=0,
        ),
    )(*kerns, *base, *accs, *p_pieces)


def first_update_kernel(seed_ref, own_ref, own_total_ref, *refs):
    got, (panel_ref, total_ref) = refs[:-2], refs[-2:]
    m = seed_ref.shape[0]
    numerators = own_ref[...]
    for ref in got:
        numerators = numerators + ref[:m, :].astype(jnp.float32)
    totals = own_total_ref[...]
    for ref in got:
        terms = ref[m:, :m].astype(jnp.float32)
        totals = totals + jnp.sum(terms, axis=0, keepdims=True)
    step = min(m, BLOCK)
    for k in range(0, m, step):
        total_ref[k : k + step, :] = jnp.broadcast_to(totals[:, k : k + step], (BLOCK, step)).T
    for k in range(0, seed_ref.shape[1], BLOCK):
        labels = mixing * numerators[:, k : k + BLOCK] / total_ref[...] + (
            1.0 - mixing
        ) * seed_ref[:, k : k + BLOCK].astype(jnp.float32)
        panel_ref[:, k : k + BLOCK] = labels.astype(jnp.bfloat16)


def last_update_kernel(seed_ref, own_ref, total_ref, *refs):
    got, out_ref = refs[:-1], refs[-1]
    numerators = own_ref[...]
    for ref in got:
        numerators = numerators + ref[...].astype(jnp.float32)
    for k in range(0, seed_ref.shape[1], BLOCK):
        out_ref[:, k : k + BLOCK] = mixing * numerators[:, k : k + BLOCK] / total_ref[...] + (
            1.0 - mixing
        ) * seed_ref[:, k : k + BLOCK].astype(jnp.float32)


def update(kernel, seeds, own, totals, got, out_shape):
    return pl.pallas_call(
        kernel,
        out_shape=out_shape,
        in_specs=[VMEM] * (3 + len(got)),
        out_specs=jax.tree.map(lambda _: VMEM, out_shape),
        compiler_params=limits(seeds, own, totals, *got, own, own),
    )(seeds, own, totals, *got)


def after(value, *earlier):
    return lax.optimization_barrier((value, *earlier))[0]


def on_device(embeddings, seed_labels, pattern):
    layout = Layout(lax.axis_size("row"), lax.axis_size("col"))
    size = layout.sizes
    m, c = embeddings.shape[0], seed_labels.shape[1]
    sub = min(m, BLOCK)
    other = {k: range(1, size[k]) for k in size}

    def fetch(values, axis, *earlier):
        return [
            layout.fetch(after(v, *earlier), **{axis: k}) for k in other[axis] for v in values
        ]

    t_offsets = [dict(zl=b, x=a) for b in range(size["zl"]) for a in range(size["x"])]
    near_t = [i for i, o in enumerate(t_offsets) if o["x"] == 0 or o["zl"] == 0]
    t_order = near_t + [i for i in range(len(t_offsets)) if i not in near_t]
    t_layout = [(i, 0, m) for i in t_order]
    both = [0] + list(other["core"])
    groups = [
        [(0, a, k) for a in range(size["y"]) for k in both],
        [(b, 0, k) for k in both for b in other["zh"]],
        [(b, a, 0) for a in other["y"] for b in other["zh"]],
        [(b, a, k) for k in other["core"] for a in other["y"] for b in other["zh"]],
    ]
    s_layout = [dict(zh=b, y=a, core=k) for group in groups for b, a, k in group]
    seeds_map = []
    for i, o in enumerate(s_layout):
        if o["zh"] == 0:
            seeds_map.append((i, 0, m, embeddings.shape[1]))
        else:
            stack = len(groups[0]) + o["core"] * (size["zh"] - 1) + o["zh"] - 1
            seeds_map.append((stack, o["y"] * m, m, 0))
    t_parts = [(t_offsets[i], k) for i in t_order for k in range(0, m, sub)]
    s_parts = [(o, k) for o in s_layout for k in range(0, m, sub)]
    place = jnp.stack([lax.axis_index("row"), lax.axis_index("col")]).astype(jnp.int32)
    units = unit_rows(after(embeddings, place))
    packed = pack_rows(units, seed_labels)

    t_pieces, kerns, accs, rects = [], [], [], []
    s_pieces = [None] * len(groups)

    def rectangle(first, last, g0, g1):
        t0, t1 = first * m, last * m
        c0, c1 = (m * sum(len(group) for group in groups[:g]) for g in (g0, g1))
        if t0 == t1 or c0 == c1:
            return []
        kern, acc = gram_call(
            flags,
            t_pieces[first:last],
            [p for g in range(g0, g1) for p in s_pieces[g]],
            sub,
            t0,
            c0,
        )
        kerns.append(kern)
        accs.append(acc)
        rects.append((t0, t1, c0, c1))
        return [acc]

    zh, zl, x = fetch([units], "zh"), fetch([units], "zl"), fetch([units], "x")
    y, own_core = fetch([packed], "y"), fetch([packed], "core")
    flags = flags_call(layout, m, t_parts, s_parts, sub, pattern, place)
    held = stack_seeds(after(seed_labels, flags, *zh), [], 2 * 10**10)
    done = zh + zl + x + y + own_core + [held]
    zh_y, zl_x = fetch(zh, "y", *done), fetch(zl, "x", *done)
    y_core = [fetch([v], "core", *done) for v in y]
    zh_core = fetch(zh, "core", *done)
    seeds_zh = fetch([stack_seeds(held, y)], "zh", *done)
    by_offset = {(0, 0): units}
    by_offset.update({(0, a): v for a, v in zip(other["x"], x)})
    by_offset.update({(b, 0): v for b, v in zip(other["zl"], zl)})
    by_offset.update({(b, a): v for (a, b), v in zip([(a, b) for a in other["x"] for b in other["zl"]], zl_x)})
    t_pieces += [by_offset[t_offsets[i]["zl"], t_offsets[i]["x"]] for i in t_order]
    s_pieces[0] = [packed] + own_core + [p for v, w in zip(y, y_core) for p in [v] + w]
    s_pieces[1] = zh + zh_core
    early, last = len(near_t), len(t_order)
    gram = rectangle(0, early, 0, 1) + rectangle(0, early, 1, 2)
    done = zh_y + zh_core + gram
    s_pieces[2] = [after(v, *gram) for v in zh_y]
    zh_y_core = fetch(zh_y, "core", *done)
    s_pieces[3] = zh_y_core
    seeds_in = seeds_zh
    gram = rectangle(0, early, 2, 3)
    seeds_zh = [stack_seeds(after(v, *gram), [], 2 * 10**10) for v in seeds_in]
    seeds_core = fetch(seeds_zh, "core")
    rectangle(early, last, 0, 3)
    rectangle(0, last, 3, 4)
    plan = (m, t_layout, rects)

    def home(values):
        return [
            layout.fetch(v, **{k: -d for k, d in o.items()})
            for v, o in zip(values, t_offsets[1:])
        ]

    def panels(panel):
        far, near = fetch([panel], "zh"), fetch([panel], "y")
        far_y = fetch(far, "y")
        near = [p for v in [panel] + near for p in [v] + fetch([v], "core")]
        return near + far + fetch(far, "core") + far_y + fetch(far_y, "core")

    seeds = s_pieces[0] + seeds_zh + seeds_core
    over_x = tuple(i for i, o in enumerate(t_offsets) if o["x"] and not o["zl"])
    along = tuple(i for i in range(len(t_offsets)) if i not in over_x)
    every = tuple(range(len(t_offsets)))
    sent = spread_call(kerns, accs, seeds, c, (*plan, seeds_map, 0, over_x))
    own, totals, *rest = spread_call(kerns, accs, seeds, c, (*plan, seeds_map, 0, along))
    by_piece = dict(zip(over_x + along[1:], list(sent) + rest))
    others = [by_piece[i] for i in every[1:]]
    panel, totals = update(
        first_update_kernel,
        held,
        own,
        totals,
        home(others),
        [
            jax.ShapeDtypeStruct((m, c), jnp.bfloat16),
            jax.ShapeDtypeStruct((m, BLOCK), jnp.float32),
        ],
    )
    pieces = panels(panel)
    first = len(groups[0]) + len(groups[1])
    base = base_call(kerns, pieces[:first], t_layout, rects)
    rest = [(i, 0, m, 0) for i in range(len(pieces) - first)]
    own, *others = spread_call(kerns, [], pieces[first:], c, (*plan, rest, first * m, every), [base])
    return update(
        last_update_kernel,
        held,
        own,
        totals,
        home(others),
        jax.ShapeDtypeStruct((m, c), jnp.float32),
    )


def solution(mesh):
    return jax.shard_map(
        on_device,
        mesh=mesh,
        in_specs=(P(("col", "row"), None), P(("col", "row"), None), P()),
        out_specs=P(("col", "row"), None),
        check_vma=False,
    )
```

```python
import functools
import math

import jax
import jax.numpy as jnp
from jax import lax
from jax.experimental import pallas as pl
from jax.experimental.pallas import tpu as pltpu
from jax.sharding import PartitionSpec as P

BLOCK = 128
AXES = ("row", "col")

sharpness = 30.0
mixing = 0.8
epsilon = 1e-06


def split_two(n):
    low = max(d for d in range(1, math.isqrt(n) + 1) if n % d == 0)
    return n // low, low


class Layout:
    def __init__(self, rows, cols):
        core = 2 if cols % 2 == 0 else 1
        ny, nx = split_two(rows)
        nzh, nzl = split_two(cols // core)
        self.sizes = dict(y=ny, x=nx, zh=nzh, zl=nzl, core=core)
        self.rows, self.cols = rows, cols

    def coords(self, row, col):
        s = self.sizes
        return dict(
            y=row // s["x"],
            x=row % s["x"],
            zh=col // (s["zl"] * s["core"]),
            zl=col // s["core"] % s["zl"],
            core=col % s["core"],
        )

    def moved(self, at, offset):
        return {k: (at[k] + offset.get(k, 0)) % self.sizes[k] for k in at}

    def row_col(self, at):
        s = self.sizes
        return at["y"] * s["x"] + at["x"], (at["zh"] * s["zl"] + at["zl"]) * s["core"] + at["core"]

    def fetch(self, value, **offset):
        if all(v % self.sizes[k] == 0 for k, v in offset.items()):
            return value
        pairs = []
        for row in range(self.rows):
            for col in range(self.cols):
                r, c = self.row_col(self.moved(self.coords(row, col), offset))
                pairs.append((r * self.cols + c, row * self.cols + col))
        return lax.ppermute(value, AXES, pairs)

    def device(self, offset):
        at = self.coords(lax.axis_index("row"), lax.axis_index("col"))
        row, col = self.row_col(self.moved(at, offset))
        return col * self.rows + row


VMEM = pl.BlockSpec(memory_space=pltpu.VMEM)


def limits(*arrays, mib=3):
    total = sum(max(math.prod(a.shape), 8 * BLOCK) * a.dtype.itemsize for a in arrays)
    return pltpu.CompilerParams(vmem_limit_bytes=total * 5 // 4 + mib * 2**20)


def shape(dims, dtype=jnp.bfloat16):
    return jax.ShapeDtypeStruct(dims, dtype)


def unit_of(values):
    values = values.astype(jnp.float32)
    mean_square = jnp.mean(values * values, axis=1, keepdims=True)
    scaled = values * lax.rsqrt(mean_square + epsilon) * values.shape[1] ** (-0.5)
    return scaled.astype(jnp.bfloat16)


def unit_kernel(emb_ref, unit_ref):
    unit_ref[...] = unit_of(emb_ref[...])


def unit_rows(embeddings):
    out = shape(embeddings.shape)
    return pl.pallas_call(
        unit_kernel,
        out_shape=out,
        in_specs=[VMEM],
        out_specs=VMEM,
        compiler_params=limits(*[out] * 4),
    )(embeddings)


def pack_kernel(unit_ref, seed_ref, packed_ref):
    d = unit_ref.shape[1]
    packed_ref[:, :d] = unit_ref[...]
    packed_ref[:, d:] = seed_ref[...]


def pack_rows(units, seeds):
    out = shape((units.shape[0], units.shape[1] + seeds.shape[1]))
    return pl.pallas_call(
        pack_kernel,
        out_shape=out,
        in_specs=[VMEM] * 2,
        out_specs=VMEM,
        compiler_params=limits(out, out),
    )(units, seeds)


def stack_kernel(seed_ref, *refs):
    *packed, out_ref = refs
    m, c = seed_ref.shape
    out_ref[:m, :] = seed_ref[...]
    for k, ref in enumerate(packed):
        out_ref[(k + 1) * m : (k + 2) * m, :] = ref[:, ref.shape[1] - c :]


def stack_seeds(seeds, packed, work=0):
    m, c = seeds.shape
    out = shape(((len(packed) + 1) * m, c))
    return pl.pallas_call(
        stack_kernel,
        out_shape=out,
        in_specs=[VMEM] * (len(packed) + 1),
        out_specs=VMEM,
        compiler_params=limits(seeds, *packed, out),
        cost_estimate=pl.CostEstimate(flops=work, bytes_accessed=2 * m * c, transcendentals=0),
    )(seeds, *packed)


def flags_kernel(layout, m, t_parts, s_parts, unit, place_ref, pattern_ref, out_ref, block_ref):
    at = layout.coords(place_ref[0], place_ref[1])

    def block(offset, start):
        row, col = layout.row_col(layout.moved(at, offset))
        return ((col * layout.rows + row) * m + start) // BLOCK

    for k, (offset, start) in enumerate(s_parts):
        block_ref[:, k * unit : (k + 1) * unit] = jnp.full((1, unit), block(offset, start), jnp.int32)
    blocks = block_ref[...]
    for r, (offset, start) in enumerate(t_parts):
        target = block(offset, start)
        hits = blocks == pattern_ref[0, target]
        for k in range(1, pattern_ref.shape[0]):
            hits = hits | (blocks == pattern_ref[k, target])
        out_ref[r : r + 1, :] = jnp.where(hits, 1, 0)


def flags_call(layout, m, t_parts, s_parts, unit, pattern, place):
    out = shape((len(t_parts), len(s_parts) * unit), jnp.int32)
    smem = pl.BlockSpec(memory_space=pltpu.SMEM)
    return pl.pallas_call(
        functools.partial(flags_kernel, layout, m, t_parts, s_parts, unit),
        out_shape=out,
        in_specs=[smem] * 2,
        out_specs=VMEM,
        scratch_shapes=[pltpu.VMEM((1, out.shape[1]), jnp.int32)],
        compiler_params=limits(out, out),
        cost_estimate=pl.CostEstimate(flops=10**7, bytes_accessed=2**20, transcendentals=0),
    )(place, pattern.T)


def tiles_of(refs, scratch, d):
    tiles, held = [], 0
    for ref in refs:
        rows = ref.shape[0]
        if rows % (2 * BLOCK) == 0:
            tiles += [(ref, k, 2 * BLOCK) for k in range(0, rows, 2 * BLOCK)]
        else:
            scratch[held : held + rows, :] = ref[:, :d]
            held += rows
    k = 0
    while k < held:
        rows = next(w for w in (2 * BLOCK, BLOCK, BLOCK // 2) if held - k >= w)
        tiles.append((scratch, k, rows))
        k += rows
    return tiles


def gram_kernel(nt, ns, sub, d, t_first, s_first, flags, *refs):
    t_in, s_in, refs = refs[:nt], refs[nt : nt + ns], refs[nt + ns :]
    kern, acc, t_join, s_join = refs
    t_tiles, s_tiles = tiles_of(t_in, t_join, d), tiles_of(s_in, s_join, d)
    rows, cols = kern.shape
    col = 0
    for s_ref, s_at, width in s_tiles:
        row = 0
        for t_ref, t_at, tall in t_tiles:
            scores = lax.dot_general(
                t_ref[t_at : t_at + tall, :],
                s_ref[s_at : s_at + width, :d],
                (((1,), (1,)), ((), ())),
                preferred_element_type=jnp.float32,
            )
            value = jnp.exp(sharpness * scores).astype(jnp.bfloat16).astype(jnp.float32)
            for a in range(tall // sub):
                at = row + a * sub
                flag = flags[
                    (t_first + at) // sub : (t_first + at) // sub + 1,
                    s_first + col : s_first + col + width,
                ]
                part = jnp.where(flag > 0, value[a * sub : (a + 1) * sub], 0.0)
                kern[at : at + sub, col : col + width] = part.astype(jnp.bfloat16)
                if width % BLOCK:
                    if col == 0:
                        acc[at : at + sub, :] = jnp.zeros((sub, BLOCK), jnp.float32)
                    acc[at : at + sub, :width] += part
                    continue
                total = part[:, :BLOCK]
                for b in range(1, width // BLOCK):
                    total = total + part[:, b * BLOCK : (b + 1) * BLOCK]
                if col > 0:
                    total = total + acc[at : at + sub, :]
                acc[at : at + sub, :] = total
            row += tall
        col += width


def gram_call(flags, t_pieces, s_pieces, sub, t_first, s_first):
    rows, cols = (sum(p.shape[0] for p in pieces) for pieces in (t_pieces, s_pieces))
    d = t_pieces[0].shape[1]
    join = [
        shape((max(16, sum(p.shape[0] for p in pieces if p.shape[0] % (2 * BLOCK))), d))
        for pieces in (t_pieces, s_pieces)
    ]
    outs = [shape((rows, cols)), shape((rows, BLOCK), jnp.float32)]
    return pl.pallas_call(
        functools.partial(
            gram_kernel, len(t_pieces), len(s_pieces), sub, d, t_first, s_first
        ),
        out_shape=outs,
        in_specs=[VMEM] * (1 + len(t_pieces) + len(s_pieces)),
        out_specs=[VMEM] * 2,
        scratch_shapes=[pltpu.VMEM(j.shape, j.dtype) for j in join],
        compiler_params=limits(flags, *t_pieces, *s_pieces, *outs, *join),
        cost_estimate=pl.CostEstimate(
            flops=2 * rows * cols * d,
            bytes_accessed=2 * (rows + cols) * d,
            transcendentals=rows * cols,
        ),
    )(flags, *t_pieces, *s_pieces)


def row_sums(kerns, rects, pcat, row, rows, lo, hi):
    part = None
    for kern, (t0, t1, c0, c1) in zip(kerns, rects):
        first, last = max(c0, lo), min(c1, hi)
        if t0 <= row < t1 and first < last:
            term = jnp.dot(
                kern[row - t0 : row - t0 + rows, first - c0 : last - c0],
                pcat[first - lo : last - lo, :],
                preferred_element_type=jnp.float32,
            )
            part = term if part is None else part + term
    return part


def base_kernel(t_layout, rects, nk, *refs):
    kerns, p_in, (out_ref, pcat) = refs[:nk], refs[nk:-2], refs[-2:]
    at = 0
    for ref in p_in:
        pcat[at : at + ref.shape[0], :] = ref[...]
        at += ref.shape[0]
    row = 0
    for _, _, rows in t_layout:
        out_ref[row : row + rows, :] = row_sums(kerns, rects, pcat, row, rows, 0, at)
        row += rows


def base_call(kerns, p_pieces, t_layout, rects):
    m, c = p_pieces[0].shape
    rows, cols = sum(r for _, _, r in t_layout), m * len(p_pieces)
    out = shape((rows, c), jnp.float32)
    return pl.pallas_call(
        functools.partial(base_kernel, t_layout, rects, len(kerns)),
        out_shape=out,
        in_specs=[VMEM] * (len(kerns) + len(p_pieces)),
        out_specs=VMEM,
        scratch_shapes=[pltpu.VMEM((cols, c), jnp.bfloat16)],
        compiler_params=limits(*kerns, *p_pieces, out, shape((cols, c))),
        cost_estimate=pl.CostEstimate(
            flops=2 * rows * cols * c, bytes_accessed=2 * rows * cols, transcendentals=0
        ),
    )(*kerns, *p_pieces)


def spread_kernel(plan, nk, na, ns, *refs):
    m, t_layout, rects, p_map, lo, chosen = plan
    kerns, refs = refs[:nk], refs[nk:]
    base, refs = (refs[0], refs[1:]) if lo else (None, refs)
    accs, refs = refs[:na], refs[na:]
    p_in, refs = refs[:ns], refs[ns:]
    outs, pcat = refs[:-1], refs[-1]
    owned = (2 if na else 1) if 0 in chosen else 0
    own_ref = outs[0]
    other_refs = dict(zip([p for p in chosen if p], outs[owned:]))
    c = pcat.shape[1]
    at = 0
    for index, start, rows, lane in p_map:
        pcat[at : at + rows, :] = p_in[index][start : start + rows, lane : lane + c]
        at += rows
    row = 0
    for piece, start, rows in t_layout:
        if piece not in chosen:
            row += rows
            continue
        part = row_sums(kerns, rects, pcat, row, rows, lo, lo + pcat.shape[0])
        if lo:
            part = part + base[row : row + rows, :]
        if piece == 0:
            own_ref[start : start + rows, :] = part
        else:
            other_refs[piece][start : start + rows, :] = part.astype(jnp.bfloat16)
        step = math.gcd(rows, BLOCK)
        for lane in range(0, rows if na else 0, step):
            total = None
            for acc, (t0, t1, c0, c1) in zip(accs, rects):
                if t0 <= row < t1:
                    first = row - t0 + lane
                    term = acc[first : first + step, :]
                    total = term if total is None else total + term
            total = jnp.sum(total.T, axis=0, keepdims=True)
            lanes = slice(start + lane, start + lane + step)
            if piece == 0:
                outs[1][:, lanes] = total
            else:
                high = total.astype(jnp.bfloat16).astype(jnp.float32)
                mid = (total - high).astype(jnp.bfloat16).astype(jnp.float32)
                low = total - high - mid
                index = lax.broadcasted_iota(jnp.int32, (16, step), 0)
                terms = jnp.where(index == 0, high, jnp.where(index == 1, mid, low))
                terms = jnp.where(index < 3, terms, 0.0)
                other_refs[piece][m:, lanes] = terms.astype(jnp.bfloat16)
        row += rows


def spread_call(kerns, accs, p_pieces, c, plan, base=()):
    m, t_layout, rects, p_map, lo, chosen = plan
    nt = len(chosen)
    cols = sum(rows for _, _, rows, _ in p_map)
    extra = 16 if accs else 0
    outs = []
    if 0 in chosen:
        outs.append(shape((m, c), jnp.float32))
        if accs:
            outs.append(shape((1, m), jnp.float32))
    outs += [shape((m + extra, c)) for p in chosen if p]
    return pl.pallas_call(
        functools.partial(spread_kernel, plan, len(kerns), len(accs), len(p_pieces)),
        out_shape=outs,
        in_specs=[VMEM] * (len(kerns) + len(base) + len(accs) + len(p_pieces)),
        out_specs=[VMEM] * len(outs),
        scratch_shapes=[pltpu.VMEM((cols, c), jnp.bfloat16)],
        compiler_params=limits(*kerns, *base, *accs, *p_pieces, *outs, shape((cols, c))),
        cost_estimate=pl.CostEstimate(
            flops=2 * nt * m * cols * c,
            bytes_accessed=2 * (nt * m * cols + cols * c),
            transcendentals=0,
        ),
    )(*kerns, *base, *accs, *p_pieces)


def first_update_kernel(seed_ref, own_ref, own_total_ref, *refs):
    got, (panel_ref, total_ref) = refs[:-2], refs[-2:]
    m = seed_ref.shape[0]
    numerators = own_ref[...]
    for ref in got:
        numerators = numerators + ref[:m, :].astype(jnp.float32)
    totals = own_total_ref[...]
    for ref in got:
        terms = ref[m:, :m].astype(jnp.float32)
        totals = totals + jnp.sum(terms, axis=0, keepdims=True)
    step = min(m, BLOCK)
    for k in range(0, m, step):
        total_ref[k : k + step, :] = jnp.broadcast_to(totals[:, k : k + step], (BLOCK, step)).T
    for k in range(0, seed_ref.shape[1], BLOCK):
        labels = mixing * numerators[:, k : k + BLOCK] / total_ref[...] + (
            1.0 - mixing
        ) * seed_ref[:, k : k + BLOCK].astype(jnp.float32)
        panel_ref[:, k : k + BLOCK] = labels.astype(jnp.bfloat16)


def last_update_kernel(seed_ref, own_ref, total_ref, *refs):
    got, out_ref = refs[:-1], refs[-1]
    numerators = own_ref[...]
    for ref in got:
        numerators = numerators + ref[...].astype(jnp.float32)
    for k in range(0, seed_ref.shape[1], BLOCK):
        out_ref[:, k : k + BLOCK] = mixing * numerators[:, k : k + BLOCK] / total_ref[...] + (
            1.0 - mixing
        ) * seed_ref[:, k : k + BLOCK].astype(jnp.float32)


def update(kernel, seeds, own, totals, got, out_shape):
    return pl.pallas_call(
        kernel,
        out_shape=out_shape,
        in_specs=[VMEM] * (3 + len(got)),
        out_specs=jax.tree.map(lambda _: VMEM, out_shape),
        compiler_params=limits(seeds, own, totals, *got, own, own),
    )(seeds, own, totals, *got)


def after(value, *earlier):
    return lax.optimization_barrier((value, *earlier))[0]


def on_device(embeddings, seed_labels, pattern):
    layout = Layout(lax.axis_size("row"), lax.axis_size("col"))
    size = layout.sizes
    m, c = embeddings.shape[0], seed_labels.shape[1]
    sub = min(m, BLOCK)
    other = {k: range(1, size[k]) for k in size}

    def fetch(values, axis, *earlier):
        return [
            layout.fetch(after(v, *earlier), **{axis: k}) for k in other[axis] for v in values
        ]

    t_offsets = [dict(zl=b, x=a) for b in range(size["zl"]) for a in range(size["x"])]
    near_t = [i for i, o in enumerate(t_offsets) if o["x"] == 0 or o["zl"] == 0]
    t_order = near_t + [i for i in range(len(t_offsets)) if i not in near_t]
    t_layout = [(i, 0, m) for i in t_order]
    both = [0] + list(other["core"])
    groups = [
        [(0, a, k) for a in range(size["y"]) for k in both],
        [(b, 0, k) for k in both for b in other["zh"]],
        [(b, a, 0) for a in other["y"] for b in other["zh"]],
        [(b, a, k) for k in other["core"] for a in other["y"] for b in other["zh"]],
    ]
    s_layout = [dict(zh=b, y=a, core=k) for group in groups for b, a, k in group]
    seeds_map = []
    for i, o in enumerate(s_layout):
        if o["zh"] == 0:
            seeds_map.append((i, 0, m, embeddings.shape[1]))
        else:
            stack = len(groups[0]) + o["core"] * (size["zh"] - 1) + o["zh"] - 1
            seeds_map.append((stack, o["y"] * m, m, 0))
    t_parts = [(t_offsets[i], k) for i in t_order for k in range(0, m, sub)]
    s_parts = [(o, k) for o in s_layout for k in range(0, m, sub)]
    place = jnp.stack([lax.axis_index("row"), lax.axis_index("col")]).astype(jnp.int32)
    units = unit_rows(after(embeddings, place))
    packed = pack_rows(units, seed_labels)

    t_pieces, kerns, accs, rects = [], [], [], []
    s_pieces = [None] * len(groups)

    def rectangle(first, last, g0, g1):
        t0, t1 = first * m, last * m
        c0, c1 = (m * sum(len(group) for group in groups[:g]) for g in (g0, g1))
        if t0 == t1 or c0 == c1:
            return []
        kern, acc = gram_call(
            flags,
            t_pieces[first:last],
            [p for g in range(g0, g1) for p in s_pieces[g]],
            sub,
            t0,
            c0,
        )
        kerns.append(kern)
        accs.append(acc)
        rects.append((t0, t1, c0, c1))
        return [acc]

    zh, zl, x = fetch([units], "zh"), fetch([units], "zl"), fetch([units], "x")
    y, own_core = fetch([packed], "y"), fetch([packed], "core")
    flags = flags_call(layout, m, t_parts, s_parts, sub, pattern, place)
    held = stack_seeds(after(seed_labels, flags, *zh), [], 2 * 10**10)
    done = zh + zl + x + y + own_core + [held]
    zh_y, zl_x = fetch(zh, "y", *done), fetch(zl, "x", *done)
    y_core = [fetch([v], "core", *done) for v in y]
    zh_core = fetch(zh, "core", *done)
    seeds_zh = fetch([stack_seeds(held, y)], "zh", *done)
    by_offset = {(0, 0): units}
    by_offset.update({(0, a): v for a, v in zip(other["x"], x)})
    by_offset.update({(b, 0): v for b, v in zip(other["zl"], zl)})
    by_offset.update({(b, a): v for (a, b), v in zip([(a, b) for a in other["x"] for b in other["zl"]], zl_x)})
    t_pieces += [by_offset[t_offsets[i]["zl"], t_offsets[i]["x"]] for i in t_order]
    s_pieces[0] = [packed] + own_core + [p for v, w in zip(y, y_core) for p in [v] + w]
    s_pieces[1] = zh + zh_core
    early, last = len(near_t), len(t_order)
    gram = rectangle(0, early, 0, 1) + rectangle(0, early, 1, 2)
    done = zh_y + zh_core + gram
    s_pieces[2] = [after(v, *gram) for v in zh_y]
    zh_y_core = fetch(zh_y, "core", *done)
    s_pieces[3] = zh_y_core
    seeds_in = seeds_zh
    gram = rectangle(0, early, 2, 3)
    seeds_zh = [stack_seeds(after(v, *gram), [], 2 * 10**10) for v in seeds_in]
    seeds_core = fetch(seeds_zh, "core")
    rectangle(early, last, 0, 3)
    rectangle(0, last, 3, 4)
    plan = (m, t_layout, rects)

    def home(values):
        return [
            layout.fetch(v, **{k: -d for k, d in o.items()})
            for v, o in zip(values, t_offsets[1:])
        ]

    def panels(panel):
        far, near = fetch([panel], "zh"), fetch([panel], "y")
        far_y = fetch(far, "y")
        near = [p for v in [panel] + near for p in [v] + fetch([v], "core")]
        return near + far + fetch(far, "core") + far_y + fetch(far_y, "core")

    seeds = s_pieces[0] + seeds_zh + seeds_core
    over_x = tuple(i for i, o in enumerate(t_offsets) if i)
    along = (0,)
    every = tuple(range(len(t_offsets)))
    sent = spread_call(kerns, accs, seeds, c, (*plan, seeds_map, 0, over_x))
    own, totals, *rest = spread_call(kerns, accs, seeds, c, (*plan, seeds_map, 0, along))
    by_piece = dict(zip(over_x + along[1:], list(sent) + rest))
    others = [by_piece[i] for i in every[1:]]
    panel, totals = update(
        first_update_kernel,
        held,
        own,
        totals,
        home(others),
        [
            jax.ShapeDtypeStruct((m, c), jnp.bfloat16),
            jax.ShapeDtypeStruct((m, BLOCK), jnp.float32),
        ],
    )
    pieces = panels(panel)
    first = len(groups[0]) + len(groups[1])
    base = base_call(kerns, pieces[:first], t_layout, rects)
    rest = [(i, 0, m, 0) for i in range(len(pieces) - first)]
    own, *others = spread_call(kerns, [], pieces[first:], c, (*plan, rest, first * m, every), [base])
    return update(
        last_update_kernel,
        held,
        own,
        totals,
        home(others),
        jax.ShapeDtypeStruct((m, c), jnp.float32),
    )


def solution(mesh):
    return jax.shard_map(
        on_device,
        mesh=mesh,
        in_specs=(P(("col", "row"), None), P(("col", "row"), None), P()),
        out_specs=P(("col", "row"), None),
        check_vma=False,
    )
```
